256 devices in a mesh: section: 2 (over core), group: 32 (over z, y), tp: 4 (over x).
Axes of the slice: x: 4, y: 4, z: 8, core: 2. Of those that a mesh axis runs over, the one named last changes fastest.
Arguments:
- resp_queries: bfloat16 [16384, 5120], P(('section', 'group', 'tp')), may hold values from -8 to 8
- resp_keys: bfloat16 [16384, 1024], P(('section', 'group', 'tp')), may hold values from -6 to 6
- resp_values: bfloat16 [16384, 1024], P(('section', 'group', 'tp')), may hold values from -6 to 6
- resp_dout: bfloat16 [16384, 5120], P(('section', 'group', 'tp')), may hold values from -6 to 6
- prompt_kv: bfloat16 [32, 2, 1024, 1024], P('group', None, None, 'tp'), may hold values from -8 to 8
- lengths: int32 [64], P(('section', 'group')), may hold values from 64 to 256, as said below
- owners: int32 [64], P(('section', 'group')), may hold values from 0 to 3
- visible_tiles: int32 [64, 8], P(('section', 'group')), may hold values from 0 to 1, as said below
Outputs:
- resp_dq: bfloat16 [16384, 5120], P(('section', 'group', 'tp'))
- resp_dk: bfloat16 [16384, 1024], P(('section', 'group', 'tp'))
- resp_dv: bfloat16 [16384, 1024], P(('section', 'group', 'tp'))
- prompt_grads: bfloat16 [32, 2, 1024, 1024], P('group', None, 'section', 'tp')
The draws below stay inside these ranges and needn't reach their ends.
Inputs may be any that keep to these rules, and one draw needn't show every extreme that they name: Response j lies on section index j // 32 and group index g = j mod 32 and belongs to the prompt on group index (g - owners[j]) mod 32. `lengths`: rows of a response at or past its length are padding; some response fills all 256 slots. `visible_tiles`: tile 0 of a prompt is visible to every response.
All inputs are finite; a program needn't handle non-finite values.
Results may differ from the reference program's by a relative error of at most 0.04.
Values may be sent and summed in bfloat16 or wider, within the bound.
No kernel may reach another device: no remote copies, remote signals or barrier semaphores. Data moves between devices by JAX's collectives and lax.ppermute only.
A program may use at most 128 MiB of HBM per device.

```python
import jax
import jax.numpy as jnp
from jax import lax

HEADS = 40
KV_HEADS = 8
HEAD_DIM = 128
PROMPT = 1024
RLEN = 256
SEQS = 1
PTILE = 128
WIN = 4
SEQUENCES = 64
RESP_ROWS = 16384
PBLOCKS = 8
N_GROUP = 32


def draw_prompt_kv(key, part):
    key = jax.random.fold_in(key, 11)
    full_shape = (N_GROUP, 2, PROMPT, KV_HEADS * HEAD_DIM)
    sample = jnp.clip(jax.random.normal(key, full_shape, jnp.float32), -6.0, 6.0)
    return sample.astype(jnp.bfloat16)


def draw_resp_queries(key, part):
    key = jax.random.fold_in(key, 12)
    full_shape = (RESP_ROWS, HEADS * HEAD_DIM)
    sample = jnp.clip(jax.random.normal(key, full_shape, jnp.float32), -6.0, 6.0)
    return sample.astype(jnp.bfloat16)


def draw_lengths(key, part):
    key = jax.random.fold_in(key, 21)
    sample = jax.random.randint(key, (SEQUENCES,), RLEN // 4, RLEN + 1)
    chosen_seq = jax.random.randint(jax.random.fold_in(key, 1), (), 0, SEQUENCES)
    return jnp.where(jnp.arange(SEQUENCES) == chosen_seq, RLEN, sample).astype(jnp.int32)


def draw_visible_tiles(key, part):
    key = jax.random.fold_in(key, 31)
    sample = (jax.random.randint(key, (SEQUENCES, PBLOCKS), 0, 5) < 3).astype(jnp.int32)
    column = jnp.arange(PBLOCKS)[None, :]
    return jnp.where(column == 0, 1, sample).astype(jnp.int32)


def with_ends(result, key, low, high):
    place = [jax.random.randint(jax.random.fold_in(key, axis), (), 0, length) for axis, length in enumerate(result.shape)]
    widest = result.shape.index(max(result.shape))
    beside = place[:widest] + [(place[widest] + 1) % result.shape[widest]] + place[widest + 1:]
    return result.at[tuple(place)].set(low).at[tuple(beside)].set(high)


def block_scale(stream_key, dims, shards, low, top_value):
    level, own = 1.0, jax.random.fold_in(stream_key, 6)
    for axis_at, parts in shards:
        draws = jnp.exp(jax.random.uniform(jax.random.fold_in(own, axis_at), (parts,), jnp.float32, low / len(shards), top_value / len(shards)))
        level = level * jnp.repeat(draws, dims[axis_at] // parts).reshape([-1 if axis == axis_at else 1 for axis in range(len(dims))])
    return level


def scatter_about(key, dims, spread, bound, split=(), kind=jnp.bfloat16):
    drawn = jax.random.normal(key, dims, jnp.float32) * spread
    if len(split) > 0:
        drawn = block_scale(key, dims, split, -0.22, 0.18) * drawn
    return jnp.clip(drawn, min=-bound, max=bound).astype(kind)


def setup_inputs(seed: int = 0) -> dict:
    arg_keys = jax.random.split(jax.random.key(seed), 9)
    return {
        "resp_queries": draw_resp_queries(jax.random.fold_in(arg_keys[8], 71), 0),
        "resp_keys": scatter_about(arg_keys[1], (RESP_ROWS, KV_HEADS * HEAD_DIM), 1.0, 6.0, ((0, 256),)),
        "resp_values": scatter_about(arg_keys[2], (RESP_ROWS, KV_HEADS * HEAD_DIM), 1.0, 6.0, ((0, 256),)),
        "resp_dout": scatter_about(arg_keys[3], (RESP_ROWS, HEADS * HEAD_DIM), 1.0, 6.0, ((0, 256),)),
        "prompt_kv": draw_prompt_kv(jax.random.fold_in(arg_keys[8], 71), 0),
        "lengths": draw_lengths(jax.random.fold_in(arg_keys[8], 71), 0),
        "owners": with_ends(jax.random.randint(arg_keys[6], (SEQUENCES,), 0, WIN), jax.random.fold_in(arg_keys[6], 1), 0, WIN - 1).astype(jnp.int32),
        "visible_tiles": draw_visible_tiles(jax.random.fold_in(arg_keys[8], 71), 0),
    }


MASKED = -1.0e30


def sequence_grads(query_rows, key_rows, value_rows, dout_rows, prompt_tiles, length, visible):
    row_count = query_rows.shape[0]
    prompt_len = prompt_tiles.shape[1]
    kv_count = key_rows.shape[1] // HEAD_DIM
    per_kv = HEADS // KV_HEADS
    scaling = HEAD_DIM ** -0.5
    keys_all = jnp.concatenate([prompt_tiles[0], key_rows], 0).astype(jnp.float32).reshape(prompt_len + row_count, kv_count, HEAD_DIM)
    values_all = jnp.concatenate([prompt_tiles[1], value_rows], 0).astype(jnp.float32).reshape(prompt_len + row_count, kv_count, HEAD_DIM)
    queries = query_rows.astype(jnp.float32).reshape(row_count, kv_count, per_kv, HEAD_DIM)
    grad_out = dout_rows.astype(jnp.float32).reshape(row_count, kv_count, per_kv, HEAD_DIM)
    scores = jnp.einsum("qkgd,tkd->kgqt", queries, keys_all) * scaling
    position = jnp.arange(row_count, dtype=jnp.int32)
    open_prompt = jnp.repeat(visible, PTILE, total_repeat_length=prompt_len) == 1
    causal = position[None, :] <= position[:, None]
    allowed = jnp.concatenate([jnp.broadcast_to(open_prompt[None, :], (row_count, prompt_len)), causal], 1)
    scores = jnp.where(allowed, scores, MASKED)
    largest = jnp.max(scores, axis=-1, keepdims=True)
    exponent = jnp.exp(scores - largest)
    probabilities = exponent / jnp.sum(exponent, axis=-1, keepdims=True)
    live_rows = (position < length).astype(jnp.float32)
    probabilities = probabilities * live_rows[:, None]
    weights = lax.optimization_barrier(probabilities.astype(jnp.bfloat16)).astype(jnp.float32)
    attended = jnp.einsum("kgqt,tkd->qkgd", weights, values_all)
    attended = lax.optimization_barrier(attended.astype(jnp.bfloat16)).astype(jnp.float32)
    row_delta = jnp.sum(grad_out * attended, axis=-1)
    grad_prob = jnp.einsum("qkgd,tkd->kgqt", grad_out, values_all)
    grad_scores = probabilities * (grad_prob - jnp.transpose(row_delta, (1, 2, 0))[..., None])
    grad_scores = lax.optimization_barrier(grad_scores.astype(jnp.bfloat16)).astype(jnp.float32)
    grad_query = (jnp.einsum("kgqt,tkd->qkgd", grad_scores, keys_all) * scaling).astype(jnp.bfloat16).reshape(row_count, -1)
    grad_key = jnp.einsum("kgqt,qkgd->tkd", grad_scores, queries) * scaling
    grad_value = jnp.einsum("kgqt,qkgd->tkd", weights, grad_out)
    return grad_query, grad_key, grad_value


def reference(resp_queries, resp_keys, resp_values, resp_dout, prompt_kv, lengths, owners, visible_tiles):
    seq_count = lengths.shape[0]
    pair_index = jnp.arange(seq_count, dtype=jnp.int32) // SEQS
    prompt_ids = ((pair_index % N_GROUP) - owners) % N_GROUP

    def split_rows(array):
        return array.reshape(seq_count, RLEN, array.shape[1])

    prompt_len = prompt_kv.shape[2]

    def per_sequence(totals, pieces):
        query_rows, key_rows, value_rows, dout_rows, prompt_id, length, visible = pieces
        prompt_tiles = lax.dynamic_index_in_dim(prompt_kv, prompt_id, 0, keepdims=False)
        grad_query, grad_key, grad_value = sequence_grads(query_rows, key_rows, value_rows, dout_rows, prompt_tiles, length, visible)
        columns = key_rows.shape[1]
        collected = jnp.stack([grad_key[:prompt_len], grad_value[:prompt_len]]).reshape(2, prompt_len, columns)
        totals = totals.at[prompt_id].add(collected)
        resp_key = grad_key[prompt_len:].reshape(RLEN, columns).astype(jnp.bfloat16)
        resp_value = grad_value[prompt_len:].reshape(RLEN, columns).astype(jnp.bfloat16)
        return totals, (grad_query, resp_key, resp_value)

    start = jnp.zeros(prompt_kv.shape, jnp.float32)
    totals, (all_query, all_key, all_value) = lax.scan(
        per_sequence, start,
        (split_rows(resp_queries), split_rows(resp_keys), split_rows(resp_values), split_rows(resp_dout), prompt_ids, lengths, visible_tiles))
    return (all_query.reshape(resp_queries.shape), all_key.reshape(resp_keys.shape),
            all_value.reshape(resp_values.shape), totals.astype(jnp.bfloat16))
```

```python
import functools

import jax
import jax.numpy as jnp
from jax import lax
from jax.experimental import pallas as pl
from jax.experimental.pallas import tpu as pltpu
from jax.sharding import PartitionSpec as P

HEADS = 40
KV_HEADS = 8
HEAD_DIM = 128
PTILE = 128
WIN = 4
PER_KV = HEADS // KV_HEADS
CHUNKS = 1

MASKED = -1e30
SCALING = HEAD_DIM ** (-0.5)
LOG2E = 1.4426950408889634
VMEM_LIMIT = 48 * 1024 * 1024

TP, SECTION, LENGTH, VISIBLE = 0, 1, 2, 3


def shifted(block, axis, distance):
    devices = range(lax.axis_size(axis))
    route = [((i - distance) % len(devices), i) for i in devices]
    return lax.ppermute(block, axis, route)


def whole():
    return pl.BlockSpec(memory_space=pltpu.VMEM)


def scalars():
    return pl.BlockSpec(memory_space=pltpu.SMEM)


def pack_kernel(tp_count, meta, queries, grad_out, keys, values, *packs):
    q_cols = queries.shape[1] // tp_count
    k_cols = keys.shape[1] // tp_count
    q_part, k_part = q_cols // CHUNKS, k_cols // CHUNKS
    for chunk in range(CHUNKS):
        for d in range(tp_count):
            owner = lax.rem(meta[TP] + d, tp_count)
            pack = packs[chunk * tp_count + d]
            q_at = pl.ds(pl.multiple_of(owner * q_cols + chunk * q_part, 128), q_part)
            k_at = pl.ds(pl.multiple_of(owner * k_cols + chunk * k_part, 128), k_part)
            pack[:, :q_part] = queries[:, q_at]
            pack[:, q_part : 2 * q_part] = grad_out[:, q_at]
            pack[:, 2 * q_part : 2 * q_part + k_part] = keys[:, k_at]
            pack[:, 2 * q_part + k_part :] = values[:, k_at]


def unpack_kernel(tp_count, meta, *refs):
    packs, (grad_q, grad_k, grad_v) = refs[:-3], refs[-3:]
    q_cols = grad_q.shape[1] // tp_count
    k_cols = grad_k.shape[1] // tp_count
    q_part, k_part = q_cols // CHUNKS, k_cols // CHUNKS
    for chunk in range(CHUNKS):
        for d in range(tp_count):
            owner = lax.rem(meta[TP] + d, tp_count)
            pack = packs[chunk * tp_count + d]
            q_at = pl.ds(pl.multiple_of(owner * q_cols + chunk * q_part, 128), q_part)
            k_at = pl.ds(pl.multiple_of(owner * k_cols + chunk * k_part, 128), k_part)
            grad_q[:, q_at] = pack[:, :q_part]
            grad_k[:, k_at] = pack[:, q_part : q_part + k_part]
            grad_v[:, k_at] = pack[:, q_part + k_part :]


def place(index, tp, tp_count, rows):
    block = index // rows
    return lax.rem(tp - block + tp_count, tp_count) * rows + lax.rem(index, rows)


def attend_kernel(tp_count, kv_heads, meta, *refs):
    packs = refs[:tp_count]
    own, other = refs[tp_count : tp_count + 2]
    backs = refs[tp_count + 2 : 2 * tp_count + 2]
    own_grad, other_grad = refs[2 * tp_count + 2 : 2 * tp_count + 4]
    q_all, do_all, keys, values, keys_t, bias, scores, grad_prob, weights, grad_scores, dk, dv = refs[
        2 * tp_count + 4 :
    ]
    rows = packs[0].shape[0]
    resp = rows * tp_count
    half = own.shape[1]
    prompt_len = 2 * half
    total = prompt_len + resp
    per_half = half // PTILE
    q_cols = kv_heads * PER_KV * HEAD_DIM
    k_cols = kv_heads * HEAD_DIM
    tp, section, length = meta[TP], meta[SECTION], meta[LENGTH]

    key_at = place(lax.broadcasted_iota(jnp.int32, (resp, resp), 0), tp, tp_count, rows)
    row_at = place(lax.broadcasted_iota(jnp.int32, (resp, resp), 1), tp, tp_count, rows)
    bias[...] = jnp.where(key_at <= row_at, 0.0, MASKED)
    live = (
        place(lax.broadcasted_iota(jnp.int32, (1, resp), 1), tp, tp_count, rows) < length
    ).astype(jnp.float32)
    tile_bias = []
    for tile in range(2 * per_half):
        side = section if tile < per_half else 1 - section
        visible = meta[VISIBLE + side * per_half + tile % per_half]
        tile_bias.append(jnp.where(visible == 1, 0.0, MASKED))

    nt = (((1,), (1,)), ((), ()))
    for kv in range(kv_heads):
        at = slice(kv * HEAD_DIM, (kv + 1) * HEAD_DIM)
        keys[:half] = own[0, :, at]
        keys[half:prompt_len] = other[0, :, at]
        values[:half] = own[1, :, at]
        values[half:prompt_len] = other[1, :, at]
        for d in range(tp_count):
            pack = packs[d]
            k_from = 2 * q_cols + kv * HEAD_DIM
            keys[prompt_len + d * rows : prompt_len + (d + 1) * rows] = pack[
                :, k_from : k_from + HEAD_DIM
            ]
            v_from = k_from + k_cols
            values[prompt_len + d * rows : prompt_len + (d + 1) * rows] = pack[
                :, v_from : v_from + HEAD_DIM
            ]
            for head in range(PER_KV):
                q_from = (kv * PER_KV + head) * HEAD_DIM
                q_all[head, d * rows : (d + 1) * rows] = pack[:, q_from : q_from + HEAD_DIM]
                do_all[head, d * rows : (d + 1) * rows] = pack[
                    :, q_cols + q_from : q_cols + q_from + HEAD_DIM
                ]
        keys_t[...] = keys[...].T
        dk[...] = jnp.zeros_like(dk)
        dv[...] = jnp.zeros_like(dv)

        for head in range(PER_KV):
            query = q_all[head]
            cotangent = do_all[head]
            tops = []
            for tile in range(total // PTILE):
                span = slice(tile * PTILE, (tile + 1) * PTILE)
                part = lax.dot_general(
                    keys[span], query, nt, preferred_element_type=jnp.float32
                )
                if tile >= 2 * per_half:
                    low = (tile - 2 * per_half) * PTILE
                    part = part + bias[low : low + PTILE]
                scores[span] = part
                top = jnp.max(part.reshape(PTILE // 8, 8, resp), axis=0)
                if tile < 2 * per_half:
                    top = top + tile_bias[tile]
                tops.append(top)
                grad_prob[span] = lax.dot_general(
                    values[span], cotangent, nt, preferred_element_type=jnp.float32
                )
            largest = jnp.max(functools.reduce(jnp.maximum, tops), axis=0, keepdims=True)
            factor = SCALING * LOG2E
            sums = jnp.zeros((8, resp), jnp.float32)
            dots = jnp.zeros((8, resp), jnp.float32)
            for tile in range(total // PTILE):
                span = slice(tile * PTILE, (tile + 1) * PTILE)
                shift = largest
                if tile < 2 * per_half:
                    shift = shift - tile_bias[tile]
                exponent = jnp.exp2((scores[span] - shift) * factor)
                scores[span] = exponent
                sums += jnp.sum(exponent.reshape(PTILE // 8, 8, resp), axis=0)
                dots += jnp.sum((exponent * grad_prob[span]).reshape(PTILE // 8, 8, resp), axis=0)
            inverse = 1.0 / jnp.sum(sums, axis=0, keepdims=True)
            row_delta = jnp.sum(dots, axis=0, keepdims=True) * inverse
            inverse = inverse * live
            for tile in range(total // PTILE):
                span = slice(tile * PTILE, (tile + 1) * PTILE)
                probabilities = scores[span] * inverse
                weights[span] = probabilities.astype(jnp.bfloat16)
                grad_scores[span] = (probabilities * (grad_prob[span] - row_delta)).astype(
                    jnp.bfloat16
                )
            dv[...] += jnp.dot(weights[...], cotangent, preferred_element_type=jnp.float32)
            dk[...] += jnp.dot(grad_scores[...], query, preferred_element_type=jnp.float32)
            grad_query_t = jnp.dot(
                keys_t[...], grad_scores[...], preferred_element_type=jnp.float32
            )
            grad_query = (grad_query_t.T * SCALING).astype(jnp.bfloat16)
            q_from = (kv * PER_KV + head) * HEAD_DIM
            for d in range(tp_count):
                backs[d][:, q_from : q_from + HEAD_DIM] = grad_query[d * rows : (d + 1) * rows]

        own_grad[0, :, at] = (dk[:half] * SCALING).astype(jnp.bfloat16)
        other_grad[0, :, at] = (dk[half:prompt_len] * SCALING).astype(jnp.bfloat16)
        own_grad[1, :, at] = dv[:half].astype(jnp.bfloat16)
        other_grad[1, :, at] = dv[half:prompt_len].astype(jnp.bfloat16)
        for d in range(tp_count):
            k_from = q_cols + kv * HEAD_DIM
            span = slice(prompt_len + d * rows, prompt_len + (d + 1) * rows)
            backs[d][:, k_from : k_from + HEAD_DIM] = (dk[span] * SCALING).astype(jnp.bfloat16)
            backs[d][:, k_from + k_cols : k_from + k_cols + HEAD_DIM] = dv[span].astype(
                jnp.bfloat16
            )


def attend(meta, packs, own, other):
    tp_count = len(packs)
    rows = packs[0].shape[0]
    resp = rows * tp_count
    half, k_cols = own.shape[1:]
    kv_heads = k_cols // HEAD_DIM
    q_cols = kv_heads * PER_KV * HEAD_DIM
    total = 2 * half + resp
    f32, bf16 = jnp.float32, jnp.bfloat16
    flops = 10 * resp * total * kv_heads * PER_KV * HEAD_DIM
    results = pl.pallas_call(
        functools.partial(attend_kernel, tp_count, kv_heads),
        out_shape=[jax.ShapeDtypeStruct((rows, q_cols + 2 * k_cols), bf16)] * tp_count
        + [jax.ShapeDtypeStruct(own.shape, bf16)] * 2,
        in_specs=[scalars()] + [whole()] * (tp_count + 2),
        out_specs=[whole()] * (tp_count + 2),
        scratch_shapes=[
            pltpu.VMEM((PER_KV, resp, HEAD_DIM), bf16),
            pltpu.VMEM((PER_KV, resp, HEAD_DIM), bf16),
            pltpu.VMEM((total, HEAD_DIM), bf16),
            pltpu.VMEM((total, HEAD_DIM), bf16),
            pltpu.VMEM((HEAD_DIM, total), bf16),
            pltpu.VMEM((resp, resp), f32),
            pltpu.VMEM((total, resp), f32),
            pltpu.VMEM((total, resp), f32),
            pltpu.VMEM((total, resp), bf16),
            pltpu.VMEM((total, resp), bf16),
            pltpu.VMEM((total, HEAD_DIM), f32),
            pltpu.VMEM((total, HEAD_DIM), f32),
        ],
        compiler_params=pltpu.CompilerParams(vmem_limit_bytes=VMEM_LIMIT),
        cost_estimate=pl.CostEstimate(
            flops=flops, bytes_accessed=6 * 1024 * 1024, transcendentals=flops // 1280
        ),
        name="attend",
    )(meta, *packs, own, other)
    return results[:tp_count], results[tp_count], results[tp_count + 1]


def pick(which, choices):
    chosen = choices[0]
    for offset in range(1, len(choices)):
        chosen = jnp.where(which == offset, choices[offset], chosen)
    return chosen


def shards(
    resp_queries, resp_keys, resp_values, resp_dout, prompt_kv, lengths, owners, visible_tiles
):
    tp_count = lax.axis_size("tp")
    section = lax.axis_index("section").astype(jnp.int32)
    rows = resp_queries.shape[0]
    half = prompt_kv.shape[2] // 2
    k_cols = prompt_kv.shape[3]
    k_part = k_cols // CHUNKS
    q_part = k_part * PER_KV
    bf16 = jnp.bfloat16

    owner = owners[0]
    sibling_owner = shifted(owners, "section", 1)[0]
    meta = jnp.concatenate(
        [lax.axis_index("tp").astype(jnp.int32)[None], section[None], lengths, visible_tiles[0]]
    )
    own_half = lax.dynamic_slice_in_dim(prompt_kv[0], section * half, half, 1)
    halves = [own_half[:, :, c * k_part : (c + 1) * k_part] for c in range(CHUNKS)]
    offers = [
        [part] + [shifted(part, "group", offset) for offset in range(1, WIN)] for part in halves
    ]

    packs = pl.pallas_call(
        functools.partial(pack_kernel, tp_count),
        out_shape=[jax.ShapeDtypeStruct((rows, 2 * q_part + 2 * k_part), bf16)]
        * (CHUNKS * tp_count),
        in_specs=[scalars()] + [whole()] * 4,
        out_specs=[whole()] * (CHUNKS * tp_count),
        compiler_params=pltpu.CompilerParams(vmem_limit_bytes=VMEM_LIMIT),
        name="pack",
    )(meta, resp_queries, resp_dout, resp_keys, resp_values)

    returned, kept_grads, shares = [], [], []
    for c in range(CHUNKS):
        mine = packs[c * tp_count : (c + 1) * tp_count]
        inputs = [mine[0]] + [shifted(mine[d], "tp", d) for d in range(1, tp_count)]
        other = shifted(pick(sibling_owner, offers[c]), "section", 1)
        own = pick(owner, offers[c])
        backs, own_grad, other_grad = attend(meta, inputs, own, other)
        sibling_grad = shifted(other_grad, "section", 1)
        terms = []
        for offset in range(WIN):
            term = jnp.where(owner == offset, own_grad.astype(jnp.float32), 0.0) + jnp.where(
                sibling_owner == offset, sibling_grad.astype(jnp.float32), 0.0
            )
            terms.append(term)
        arrived = [terms[0]] + [
            shifted(terms[offset].astype(bf16), "group", -offset).astype(jnp.float32)
            for offset in range(1, WIN)
        ]
        shares.append(functools.reduce(jnp.add, arrived).astype(bf16))
        returned += [backs[0]] + [shifted(backs[d], "tp", -d) for d in range(1, tp_count)]

    grads = pl.pallas_call(
        functools.partial(unpack_kernel, tp_count),
        out_shape=[
            jax.ShapeDtypeStruct(resp_queries.shape, bf16),
            jax.ShapeDtypeStruct(resp_keys.shape, bf16),
            jax.ShapeDtypeStruct(resp_values.shape, bf16),
        ],
        in_specs=[scalars()] + [whole()] * (CHUNKS * tp_count),
        out_specs=[whole()] * 3,
        compiler_params=pltpu.CompilerParams(vmem_limit_bytes=VMEM_LIMIT),
        name="unpack",
    )(meta, *returned)
    return (grads[0], grads[1], grads[2], jnp.concatenate(shares, -1)[None])


def solution(mesh):
    placed = (
        P(("section", "group", "tp"), None),
        P(("section", "group", "tp"), None),
        P(("section", "group", "tp"), None),
        P(("section", "group", "tp"), None),
        P("group", None, None, "tp"),
        P(("section", "group")),
        P(("section", "group")),
        P(("section", "group"), None),
    )
    return jax.shard_map(
        shards,
        mesh=mesh,
        in_specs=placed,
        out_specs=(
            P(("section", "group", "tp"), None),
            P(("section", "group", "tp"), None),
            P(("section", "group", "tp"), None),
            P("group", None, "section", "tp"),
        ),
        check_vma=False,
    )
```

```python
import functools

import jax
import jax.numpy as jnp
from jax import lax
from jax.experimental import pallas as pl
from jax.experimental.pallas import tpu as pltpu
from jax.sharding import PartitionSpec as P

HEADS = 40
KV_HEADS = 8
HEAD_DIM = 128
PTILE = 128
WIN = 4
PER_KV = HEADS // KV_HEADS
CHUNKS = 2
ROW = 4

MASKED = -1e30
SCALING = HEAD_DIM ** (-0.5)
LOG2E = 1.4426950408889634
VMEM_LIMIT = 48 * 1024 * 1024

TP, SECTION, LENGTH, VISIBLE = 0, 1, 2, 3


def shifted(block, axis, distance):
    devices = range(lax.axis_size(axis))
    route = [((i - distance) % len(devices), i) for i in devices]
    return lax.ppermute(block, axis, route)


def whole():
    return pl.BlockSpec(memory_space=pltpu.VMEM)


def scalars():
    return pl.BlockSpec(memory_space=pltpu.SMEM)


def pack_kernel(tp_count, meta, queries, grad_out, keys, values, *packs):
    q_cols = queries.shape[1] // tp_count
    k_cols = keys.shape[1] // tp_count
    q_part, k_part = q_cols // CHUNKS, k_cols // CHUNKS
    for d in range(tp_count):
        owner = lax.rem(meta[TP] + d, tp_count)
        pack, at = packs[d], 0
        for chunk in range(CHUNKS):
            q_at = pl.ds(pl.multiple_of(owner * q_cols + chunk * q_part, 128), q_part)
            k_at = pl.ds(pl.multiple_of(owner * k_cols + chunk * k_part, 128), k_part)
            pack[:, at : at + q_part] = queries[:, q_at]
            pack[:, at + q_part : at + 2 * q_part] = grad_out[:, q_at]
            at += 2 * q_part
            pack[:, at : at + k_part] = keys[:, k_at]
            pack[:, at + k_part : at + 2 * k_part] = values[:, k_at]
            at += 2 * k_part


def unpack_kernel(tp_count, meta, *refs):
    packs, (grad_q, grad_k, grad_v) = refs[:-3], refs[-3:]
    q_cols = grad_q.shape[1] // tp_count
    k_cols = grad_k.shape[1] // tp_count
    q_part, k_part = q_cols // CHUNKS, k_cols // CHUNKS
    for d in range(tp_count):
        owner = lax.rem(meta[TP] + d, tp_count)
        pack, at = packs[d], 0
        for chunk in range(CHUNKS):
            q_at = pl.ds(pl.multiple_of(owner * q_cols + chunk * q_part, 128), q_part)
            k_at = pl.ds(pl.multiple_of(owner * k_cols + chunk * k_part, 128), k_part)
            grad_q[:, q_at] = pack[:, at : at + q_part]
            grad_k[:, k_at] = pack[:, at + q_part : at + q_part + k_part]
            at += q_part + k_part
            grad_v[:, k_at] = pack[:, at : at + k_part]
            at += k_part


def place(index, tp, tp_count, rows):
    block = index // rows
    return lax.rem(tp - block + tp_count, tp_count) * rows + lax.rem(index, rows)


def attend_kernel(tp_count, kv_heads, chunk, meta, *refs):
    packs, refs = refs[:tp_count], refs[tp_count:]
    earlier, refs = refs[: tp_count if chunk else 0], refs[tp_count if chunk else 0 :]
    (own, other), refs = refs[:2], refs[2:]
    backs, refs = refs[:tp_count], refs[tp_count:]
    own_grad, other_grad = refs[:2]
    q_all, do_all, keys, values, keys_t, bias, scores, grad_prob, weights, grad_scores, dk, dv = refs[
        2:
    ]
    rows = packs[0].shape[0]
    resp = rows * tp_count
    half = own.shape[1]
    prompt_len = 2 * half
    total = prompt_len + resp
    per_half = half // PTILE
    q_cols = kv_heads * PER_KV * HEAD_DIM
    k_cols = kv_heads * HEAD_DIM
    tp, section, length = meta[TP], meta[SECTION], meta[LENGTH]
    taken = chunk * 2 * (q_cols + k_cols)
    given = chunk * (q_cols + 2 * k_cols)
    if chunk:
        for d in range(tp_count):
            backs[d][:, :given] = earlier[d][...]

    key_at = place(lax.broadcasted_iota(jnp.int32, (resp, resp), 0), tp, tp_count, rows)
    row_at = place(lax.broadcasted_iota(jnp.int32, (resp, resp), 1), tp, tp_count, rows)
    bias[...] = jnp.where(key_at <= row_at, 0.0, MASKED)
    live = (
        place(lax.broadcasted_iota(jnp.int32, (1, resp), 1), tp, tp_count, rows) < length
    ).astype(jnp.float32)
    tile_bias = []
    for tile in range(2 * per_half):
        side = section if tile < per_half else 1 - section
        visible = meta[VISIBLE + side * per_half + tile % per_half]
        tile_bias.append(jnp.where(visible == 1, 0.0, MASKED))

    nt = (((1,), (1,)), ((), ()))
    for kv in range(kv_heads):
        at = slice(kv * HEAD_DIM, (kv + 1) * HEAD_DIM)
        keys[:half] = own[0, :, at]
        keys[half:prompt_len] = other[0, :, at]
        values[:half] = own[1, :, at]
        values[half:prompt_len] = other[1, :, at]
        for d in range(tp_count):
            pack = packs[d]
            k_from = taken + 2 * q_cols + kv * HEAD_DIM
            keys[prompt_len + d * rows : prompt_len + (d + 1) * rows] = pack[
                :, k_from : k_from + HEAD_DIM
            ]
            v_from = k_from + k_cols
            values[prompt_len + d * rows : prompt_len + (d + 1) * rows] = pack[
                :, v_from : v_from + HEAD_DIM
            ]
            for head in range(PER_KV):
                q_from = taken + (kv * PER_KV + head) * HEAD_DIM
                q_all[head, d * rows : (d + 1) * rows] = pack[:, q_from : q_from + HEAD_DIM]
                do_all[head, d * rows : (d + 1) * rows] = pack[
                    :, q_cols + q_from : q_cols + q_from + HEAD_DIM
                ]
        keys_t[...] = keys[...].T
        dk[...] = jnp.zeros_like(dk)
        dv[...] = jnp.zeros_like(dv)

        for head in range(PER_KV):
            query = q_all[head]
            cotangent = do_all[head]
            tops = []
            for tile in range(total // PTILE):
                span = slice(tile * PTILE, (tile + 1) * PTILE)
                part = lax.dot_general(
                    keys[span], query, nt, preferred_element_type=jnp.float32
                )
                if tile >= 2 * per_half:
                    low = (tile - 2 * per_half) * PTILE
                    part = part + bias[low : low + PTILE]
                scores[span] = part
                top = jnp.max(part.reshape(PTILE // 8, 8, resp), axis=0)
                if tile < 2 * per_half:
                    top = top + tile_bias[tile]
                tops.append(top)
                grad_prob[span] = lax.dot_general(
                    values[span], cotangent, nt, preferred_element_type=jnp.float32
                )
            largest = jnp.max(functools.reduce(jnp.maximum, tops), axis=0, keepdims=True)
            factor = SCALING * LOG2E
            sums = jnp.zeros((8, resp), jnp.float32)
            dots = jnp.zeros((8, resp), jnp.float32)
            for tile in range(total // PTILE):
                span = slice(tile * PTILE, (tile + 1) * PTILE)
                shift = largest
                if tile < 2 * per_half:
                    shift = shift - tile_bias[tile]
                exponent = jnp.exp2((scores[span] - shift) * factor)
                scores[span] = exponent
                sums += jnp.sum(exponent.reshape(PTILE // 8, 8, resp), axis=0)
                dots += jnp.sum((exponent * grad_prob[span]).reshape(PTILE // 8, 8, resp), axis=0)
            inverse = 1.0 / jnp.sum(sums, axis=0, keepdims=True)
            row_delta = jnp.sum(dots, axis=0, keepdims=True) * inverse
            inverse = inverse * live
            for tile in range(total // PTILE):
                span = slice(tile * PTILE, (tile + 1) * PTILE)
                probabilities = scores[span] * inverse
                weights[span] = probabilities.astype(jnp.bfloat16)
                grad_scores[span] = (probabilities * (grad_prob[span] - row_delta)).astype(
                    jnp.bfloat16
                )
            dv[...] += jnp.dot(weights[...], cotangent, preferred_element_type=jnp.float32)
            dk[...] += jnp.dot(grad_scores[...], query, preferred_element_type=jnp.float32)
            grad_query_t = jnp.dot(
                keys_t[...], grad_scores[...], preferred_element_type=jnp.float32
            )
            grad_query = (grad_query_t.T * SCALING).astype(jnp.bfloat16)
            q_from = given + (kv * PER_KV + head) * HEAD_DIM
            for d in range(tp_count):
                backs[d][:, q_from : q_from + HEAD_DIM] = grad_query[d * rows : (d + 1) * rows]

        own_grad[0, :, at] = (dk[:half] * SCALING).astype(jnp.bfloat16)
        other_grad[0, :, at] = (dk[half:prompt_len] * SCALING).astype(jnp.bfloat16)
        own_grad[1, :, at] = dv[:half].astype(jnp.bfloat16)
        other_grad[1, :, at] = dv[half:prompt_len].astype(jnp.bfloat16)
        for d in range(tp_count):
            k_from = given + q_cols + kv * HEAD_DIM
            span = slice(prompt_len + d * rows, prompt_len + (d + 1) * rows)
            backs[d][:, k_from : k_from + HEAD_DIM] = (dk[span] * SCALING).astype(jnp.bfloat16)
            backs[d][:, k_from + k_cols : k_from + k_cols + HEAD_DIM] = dv[span].astype(
                jnp.bfloat16
            )


def attend(chunk, meta, packs, earlier, own, other):
    tp_count = len(packs)
    rows = packs[0].shape[0]
    resp = rows * tp_count
    half, k_cols = own.shape[1:]
    kv_heads = k_cols // HEAD_DIM
    q_cols = kv_heads * PER_KV * HEAD_DIM
    total = 2 * half + resp
    f32, bf16 = jnp.float32, jnp.bfloat16
    flops = 10 * resp * total * kv_heads * PER_KV * HEAD_DIM
    results = pl.pallas_call(
        functools.partial(attend_kernel, tp_count, kv_heads, chunk),
        out_shape=[jax.ShapeDtypeStruct((rows, (chunk + 1) * (q_cols + 2 * k_cols)), bf16)]
        * tp_count
        + [jax.ShapeDtypeStruct(own.shape, bf16)] * 2,
        in_specs=[scalars()] + [whole()] * (tp_count + len(earlier) + 2),
        out_specs=[whole()] * (tp_count + 2),
        scratch_shapes=[
            pltpu.VMEM((PER_KV, resp, HEAD_DIM), bf16),
            pltpu.VMEM((PER_KV, resp, HEAD_DIM), bf16),
            pltpu.VMEM((total, HEAD_DIM), bf16),
            pltpu.VMEM((total, HEAD_DIM), bf16),
            pltpu.VMEM((HEAD_DIM, total), bf16),
            pltpu.VMEM((resp, resp), f32),
            pltpu.VMEM((total, resp), f32),
            pltpu.VMEM((total, resp), f32),
            pltpu.VMEM((total, resp), bf16),
            pltpu.VMEM((total, resp), bf16),
            pltpu.VMEM((total, HEAD_DIM), f32),
            pltpu.VMEM((total, HEAD_DIM), f32),
        ],
        compiler_params=pltpu.CompilerParams(vmem_limit_bytes=VMEM_LIMIT),
        cost_estimate=pl.CostEstimate(
            flops=flops, bytes_accessed=6 * 1024 * 1024, transcendentals=flops // 1280
        ),
        name="attend",
    )(meta, *packs, *earlier, own, other)
    return results[:tp_count], results[tp_count], results[tp_count + 1]


def pick(which, choices):
    chosen = choices[0]
    for offset in range(1, len(choices)):
        chosen = jnp.where(which == offset, choices[offset], chosen)
    return chosen


def after(block, earlier):
    return lax.optimization_barrier((block, earlier))[0]


def along_row(block, distance):
    count = lax.axis_size("group")
    route = [(i - i % ROW + (i - distance) % ROW, i) for i in range(count)]
    return lax.ppermute(block, "group", route)


def to_row(block, distance):
    return shifted(block, "group", distance * ROW)


def shards(
    resp_queries, resp_keys, resp_values, resp_dout, prompt_kv, lengths, owners, visible_tiles
):
    tp_count = lax.axis_size("tp")
    section = lax.axis_index("section").astype(jnp.int32)
    at_row = lax.rem(lax.axis_index("group").astype(jnp.int32), ROW)
    rows = resp_queries.shape[0]
    half = prompt_kv.shape[2] // 2
    k_cols = prompt_kv.shape[3]
    k_part = k_cols // CHUNKS
    q_part = k_part * PER_KV
    bf16, f32 = jnp.bfloat16, jnp.float32

    owner = owners[0]
    sibling_owner = shifted(owners, "section", 1)[0]
    meta = jnp.concatenate(
        [lax.axis_index("tp").astype(jnp.int32)[None], section[None], lengths, visible_tiles[0]]
    )
    packs = pl.pallas_call(
        functools.partial(pack_kernel, tp_count),
        out_shape=[jax.ShapeDtypeStruct((rows, CHUNKS * 2 * (q_part + k_part)), bf16)] * tp_count,
        in_specs=[scalars()] + [whole()] * 4,
        out_specs=[whole()] * tp_count,
        compiler_params=pltpu.CompilerParams(vmem_limit_bytes=VMEM_LIMIT),
        name="pack",
    )(meta, resp_queries, resp_dout, resp_keys, resp_values)
    own_half = lax.dynamic_slice_in_dim(prompt_kv[0], section * half, half, 1)
    halves = [own_half[:, :, c * k_part : (c + 1) * k_part] for c in range(CHUNKS)]
    packs, halves = lax.optimization_barrier((packs, halves))

    before = [to_row(part, 1) for part in halves]
    arrived = [packs[0]] + [shifted(packs[d], "tp", d) for d in range(1, tp_count)]
    offers = []
    for c in range(CHUNKS):
        offer = [halves[c]]
        for offset in range(1, WIN):
            sent = jnp.where(at_row + offset >= ROW, before[c], halves[c])
            sent = after(sent, offers[c - 1][offset] if c else arrived[1::2])
            offer.append(along_row(sent, offset))
        offers.append(offer)

    backs, shares, passing, held = [], [], [], None
    for c in range(CHUNKS):
        other = shifted(pick(sibling_owner, offers[c]), "section", 1)
        own = pick(owner, offers[c])
        if c:
            own = after(own, held)
        backs, own_grad, other_grad = attend(c, meta, arrived, backs, own, other)
        sibling_grad = shifted(other_grad, "section", 1)
        terms = []
        for offset in range(WIN):
            term = jnp.where(owner == offset, own_grad.astype(f32), 0.0) + jnp.where(
                sibling_owner == offset, sibling_grad.astype(f32), 0.0
            )
            terms.append(term if offset == 0 else term.astype(bf16))
        terms = held = lax.optimization_barrier(terms)
        kept, passed = terms[0], jnp.zeros(terms[0].shape, f32)
        for offset in range(1, WIN):
            term = along_row(terms[offset], -offset).astype(f32)
            crossing = at_row + offset >= ROW
            kept = kept + jnp.where(crossing, 0.0, term)
            passed = passed + jnp.where(crossing, term, 0.0)
        passed = passed.astype(bf16)
        passing.append(passed)
        shares.append((kept + to_row(passed, -1).astype(f32)).astype(bf16))
    backs = after(backs, passing[0])
    returned = [backs[0]] + [shifted(backs[d], "tp", -d) for d in range(1, tp_count)]

    grads = pl.pallas_call(
        functools.partial(unpack_kernel, tp_count),
        out_shape=[
            jax.ShapeDtypeStruct(resp_queries.shape, bf16),
            jax.ShapeDtypeStruct(resp_keys.shape, bf16),
            jax.ShapeDtypeStruct(resp_values.shape, bf16),
        ],
        in_specs=[scalars()] + [whole()] * tp_count,
        out_specs=[whole()] * 3,
        compiler_params=pltpu.CompilerParams(vmem_limit_bytes=VMEM_LIMIT),
        name="unpack",
    )(meta, *returned)
    return (grads[0], grads[1], grads[2], jnp.concatenate(shares, -1)[None])


def solution(mesh):
    placed = (
        P(("section", "group", "tp"), None),
        P(("section", "group", "tp"), None),
        P(("section", "group", "tp"), None),
        P(("section", "group", "tp"), None),
        P("group", None, None, "tp"),
        P(("section", "group")),
        P(("section", "group")),
        P(("section", "group"), None),
    )
    return jax.shard_map(
        shards,
        mesh=mesh,
        in_specs=placed,
        out_specs=(
            P(("section", "group", "tp"), None),
            P(("section", "group", "tp"), None),
            P(("section", "group", "tp"), None),
            P("group", None, "section", "tp"),
        ),
        check_vma=False,
    )
```

```python
import functools

import jax
import jax.numpy as jnp
from jax import lax
from jax.experimental import pallas as pl
from jax.experimental.pallas import tpu as pltpu
from jax.sharding import PartitionSpec as P

HEADS = 40
KV_HEADS = 8
HEAD_DIM = 128
PTILE = 128
WIN = 4
PER_KV = HEADS // KV_HEADS
CHUNKS = 2
ROW = 4

MASKED = -1e30
SCALING = HEAD_DIM ** (-0.5)
LOG2E = 1.4426950408889634
VMEM_LIMIT = 48 * 1024 * 1024
VMEM_MOST = 60 * 1024 * 1024

TP, SECTION, LENGTH, OWNER, VISIBLE = 0, 1, 2, 3, 4


def shifted(block, axis, distance):
    devices = range(lax.axis_size(axis))
    route = [((i - distance) % len(devices), i) for i in devices]
    return lax.ppermute(block, axis, route)


def after(block, earlier):
    return lax.optimization_barrier((block, earlier))[0]


def along_row(block, distance):
    count = lax.axis_size("group")
    route = [(i - i % ROW + (i - distance) % ROW, i) for i in range(count)]
    return lax.ppermute(block, "group", route)


def to_row(block, distance):
    return shifted(block, "group", distance * ROW)


def whole():
    return pl.BlockSpec(memory_space=pltpu.VMEM)


def scalars():
    return pl.BlockSpec(memory_space=pltpu.SMEM)


def small_call(
    kernel, name, out_shape, in_specs, scratch_shapes=(), vmem=VMEM_LIMIT, out_space=pltpu.VMEM
):
    return pl.pallas_call(
        kernel,
        out_shape=out_shape,
        in_specs=in_specs,
        out_specs=jax.tree.map(lambda _: pl.BlockSpec(memory_space=out_space), out_shape),
        scratch_shapes=scratch_shapes,
        compiler_params=pltpu.CompilerParams(vmem_limit_bytes=vmem),
        name=name,
    )


def halves_kernel(section, prompt, *refs):
    parts, sems = refs[:-1], refs[-1]
    half, cols = parts[0].shape[1:]
    copies = []
    for chunk, part in enumerate(parts):
        rows = pl.ds(pl.multiple_of(section[0] * half, half), half)
        source = prompt.at[0, :, rows, chunk * cols : (chunk + 1) * cols]
        copies.append(pltpu.make_async_copy(source, part, sems.at[chunk]))
    for copy in copies:
        copy.start()
    for copy in copies:
        copy.wait()


def sends_kernel(place, own, before, *sends):
    for offset, send in enumerate(sends, 1):

        @pl.when(place[0] + offset >= ROW)
        def _(send=send):
            send[...] = before[...]

        @pl.when(place[0] + offset < ROW)
        def _(send=send):
            send[...] = own[...]


def pick_kernel(which, *refs):
    choices, chosen = refs[:-1], refs[-1]
    for offset, choice in enumerate(choices):

        @pl.when(which[0] == offset)
        def _(choice=choice):
            chosen[...] = choice[...]


def pack_kernel(tp, queries, grad_out, keys, values, *refs):
    packs, sems = refs[:-1], refs[-1]
    tp_count = len(packs)
    copies = []
    for d, pack in enumerate(packs):
        device, at = lax.rem(tp[0] + d, tp_count), 0
        for chunk in range(CHUNKS):
            for source in (queries, grad_out, keys, values):
                cols = source.shape[1] // tp_count
                part = cols // CHUNKS
                start = pl.multiple_of(device * cols + chunk * part, 128)
                copies.append(
                    pltpu.make_async_copy(
                        source.at[:, pl.ds(start, part)],
                        pack.at[:, at : at + part],
                        sems.at[len(copies)],
                    )
                )
                at += part
    for copy in copies:
        copy.start()
    for copy in copies:
        copy.wait()


def unpack_kernel(tp, *refs):
    packs, (grad_q, grad_k, grad_v) = refs[:-3], refs[-3:]
    tp_count = len(packs)
    q_cols = grad_q.shape[1] // tp_count
    k_cols = grad_k.shape[1] // tp_count
    q_part, k_part = q_cols // CHUNKS, k_cols // CHUNKS
    for d, pack in enumerate(packs):
        device, at = lax.rem(tp[0] + d, tp_count), 0
        for chunk in range(CHUNKS):
            q_at = pl.ds(pl.multiple_of(device * q_cols + chunk * q_part, 128), q_part)
            k_at = pl.ds(pl.multiple_of(device * k_cols + chunk * k_part, 128), k_part)
            grad_q[:, q_at] = pack[:, at : at + q_part]
            at += q_part
            grad_k[:, k_at] = pack[:, at : at + k_part]
            at += k_part
            grad_v[:, k_at] = pack[:, at : at + k_part]
            at += k_part


def place(index, tp, tp_count, rows):
    block = index // rows
    return lax.rem(tp - block + tp_count, tp_count) * rows + lax.rem(index, rows)


def attend_kernel(chunk, tp_count, meta, *refs):
    packs, refs = refs[:tp_count], refs[tp_count:]
    earlier, refs = refs[: tp_count if chunk else 0], refs[tp_count if chunk else 0 :]
    offers, other, refs = refs[:WIN], refs[WIN], refs[WIN + 1 :]
    backs, refs = refs[:tp_count], refs[tp_count:]
    own_grad, other_grad = refs[:2]
    q_all, do_all, keys, values, keys_t, bias, scores, grad_prob, weights, grad_scores, dk, dv = refs[
        2:
    ]
    rows = packs[0].shape[0]
    resp = rows * tp_count
    half, k_cols = other.shape[1:]
    kv_heads = k_cols // HEAD_DIM
    prompt_len = 2 * half
    total = prompt_len + resp
    per_half = half // PTILE
    q_cols = kv_heads * PER_KV * HEAD_DIM
    tp, section, length, owner = meta[TP], meta[SECTION], meta[LENGTH], meta[OWNER]
    taken = chunk * 2 * (q_cols + k_cols)
    given = chunk * (q_cols + 2 * k_cols)
    for back, block in zip(backs, earlier):
        back[:, :given] = block[...]

    key_at = place(lax.broadcasted_iota(jnp.int32, (resp, resp), 0), tp, tp_count, rows)
    row_at = place(lax.broadcasted_iota(jnp.int32, (resp, resp), 1), tp, tp_count, rows)
    bias[...] = jnp.where(key_at <= row_at, 0.0, MASKED)
    live = (
        place(lax.broadcasted_iota(jnp.int32, (1, resp), 1), tp, tp_count, rows) < length
    ).astype(jnp.float32)
    tile_bias = []
    for tile in range(2 * per_half):
        side = section if tile < per_half else 1 - section
        visible = meta[VISIBLE + side * per_half + tile % per_half]
        tile_bias.append(jnp.where(visible == 1, 0.0, MASKED))

    nt = (((1,), (1,)), ((), ()))
    for kv in range(kv_heads):
        at = slice(kv * HEAD_DIM, (kv + 1) * HEAD_DIM)
        for offset, offer in enumerate(offers):

            @pl.when(owner == offset)
            def _(offer=offer):
                keys[:half] = offer[0, :, at]
                values[:half] = offer[1, :, at]

        keys[half:prompt_len] = other[0, :, at]
        values[half:prompt_len] = other[1, :, at]
        for i in range(tp_count):
            here = slice(i * rows, (i + 1) * rows)
            there = slice(prompt_len + i * rows, prompt_len + (i + 1) * rows)
            k_from = taken + 2 * q_cols + kv * HEAD_DIM
            keys[there] = packs[i][:, k_from : k_from + HEAD_DIM]
            values[there] = packs[i][:, k_from + k_cols : k_from + k_cols + HEAD_DIM]
            for head in range(PER_KV):
                q_from = taken + (kv * PER_KV + head) * HEAD_DIM
                q_all[head, here] = packs[i][:, q_from : q_from + HEAD_DIM]
                do_all[head, here] = packs[i][:, q_cols + q_from : q_cols + q_from + HEAD_DIM]
        keys_t[...] = keys[...].T
        dk[...] = jnp.zeros_like(dk)
        dv[...] = jnp.zeros_like(dv)

        for head in range(PER_KV):
            query = q_all[head]
            cotangent = do_all[head]
            tops = []
            for tile in range(total // PTILE):
                span = slice(tile * PTILE, (tile + 1) * PTILE)
                part = lax.dot_general(
                    keys[span], query, nt, preferred_element_type=jnp.float32
                )
                if tile >= 2 * per_half:
                    low = (tile - 2 * per_half) * PTILE
                    part = part + bias[low : low + PTILE]
                scores[span] = part
                top = jnp.max(part.reshape(PTILE // 8, 8, resp), axis=0)
                if tile < 2 * per_half:
                    top = top + tile_bias[tile]
                tops.append(top)
                grad_prob[span] = lax.dot_general(
                    values[span], cotangent, nt, preferred_element_type=jnp.float32
                )
            largest = jnp.max(functools.reduce(jnp.maximum, tops), axis=0, keepdims=True)
            factor = SCALING * LOG2E
            sums = jnp.zeros((8, resp), jnp.float32)
            dots = jnp.zeros((8, resp), jnp.float32)
            for tile in range(total // PTILE):
                span = slice(tile * PTILE, (tile + 1) * PTILE)
                shift = largest
                if tile < 2 * per_half:
                    shift = shift - tile_bias[tile]
                exponent = jnp.exp2((scores[span] - shift) * factor)
                scores[span] = exponent
                sums += jnp.sum(exponent.reshape(PTILE // 8, 8, resp), axis=0)
                dots += jnp.sum((exponent * grad_prob[span]).reshape(PTILE // 8, 8, resp), axis=0)
            inverse = 1.0 / jnp.sum(sums, axis=0, keepdims=True)
            row_delta = jnp.sum(dots, axis=0, keepdims=True) * inverse
            inverse = inverse * live
            for tile in range(total // PTILE):
                span = slice(tile * PTILE, (tile + 1) * PTILE)
                probabilities = scores[span] * inverse
                weights[span] = probabilities.astype(jnp.bfloat16)
                grad_scores[span] = (probabilities * (grad_prob[span] - row_delta)).astype(
                    jnp.bfloat16
                )
            dv[...] += jnp.dot(weights[...], cotangent, preferred_element_type=jnp.float32)
            dk[...] += jnp.dot(grad_scores[...], query, preferred_element_type=jnp.float32)
            grad_query_t = jnp.dot(
                keys_t[...], grad_scores[...], preferred_element_type=jnp.float32
            )
            grad_query = (grad_query_t.T * SCALING).astype(jnp.bfloat16)
            q_from = given + (kv * PER_KV + head) * HEAD_DIM
            for i in range(tp_count):
                backs[i][:, q_from : q_from + HEAD_DIM] = grad_query[i * rows : (i + 1) * rows]

        own_grad[0, :, at] = (dk[:half] * SCALING).astype(jnp.bfloat16)
        other_grad[0, :, at] = (dk[half:prompt_len] * SCALING).astype(jnp.bfloat16)
        own_grad[1, :, at] = dv[:half].astype(jnp.bfloat16)
        other_grad[1, :, at] = dv[half:prompt_len].astype(jnp.bfloat16)
        for i in range(tp_count):
            k_from = given + q_cols + kv * HEAD_DIM
            v_from = k_from + k_cols
            span = slice(prompt_len + i * rows, prompt_len + (i + 1) * rows)
            backs[i][:, k_from : k_from + HEAD_DIM] = (dk[span] * SCALING).astype(jnp.bfloat16)
            backs[i][:, v_from : v_from + HEAD_DIM] = dv[span].astype(jnp.bfloat16)


def attend(chunk, meta, packs, earlier, offers, other):
    tp_count, rows = len(packs), packs[0].shape[0]
    resp = rows * tp_count
    half, k_cols = other.shape[1:]
    kv_heads = k_cols // HEAD_DIM
    q_cols = kv_heads * PER_KV * HEAD_DIM
    total = 2 * half + resp
    f32, bf16 = jnp.float32, jnp.bfloat16
    flops = 10 * resp * total * kv_heads * PER_KV * HEAD_DIM
    results = pl.pallas_call(
        functools.partial(attend_kernel, chunk, tp_count),
        out_shape=[
            jax.ShapeDtypeStruct((rows, (chunk + 1) * (q_cols + 2 * k_cols)), bf16)
        ]
        * tp_count
        + [jax.ShapeDtypeStruct(other.shape, bf16)] * 2,
        in_specs=[scalars()] + [whole()] * (tp_count + len(earlier) + len(offers) + 1),
        out_specs=[whole()] * (tp_count + 2),
        scratch_shapes=[
            pltpu.VMEM((PER_KV, resp, HEAD_DIM), bf16),
            pltpu.VMEM((PER_KV, resp, HEAD_DIM), bf16),
            pltpu.VMEM((total, HEAD_DIM), bf16),
            pltpu.VMEM((total, HEAD_DIM), bf16),
            pltpu.VMEM((HEAD_DIM, total), bf16),
            pltpu.VMEM((resp, resp), f32),
            pltpu.VMEM((total, resp), f32),
            pltpu.VMEM((total, resp), f32),
            pltpu.VMEM((total, resp), bf16),
            pltpu.VMEM((total, resp), bf16),
            pltpu.VMEM((total, HEAD_DIM), f32),
            pltpu.VMEM((total, HEAD_DIM), f32),
        ],
        compiler_params=pltpu.CompilerParams(vmem_limit_bytes=VMEM_LIMIT),
        cost_estimate=pl.CostEstimate(
            flops=flops, bytes_accessed=6 * 1024 * 1024, transcendentals=flops // 1280
        ),
        name="attend",
    )(meta, *packs, *earlier, *offers, other)
    return results[:tp_count], results[tp_count], results[tp_count + 1]


def shards(
    resp_queries, resp_keys, resp_values, resp_dout, prompt_kv, lengths, owners, visible_tiles
):
    tp_count = lax.axis_size("tp")
    tp = lax.axis_index("tp").astype(jnp.int32)[None]
    section = lax.axis_index("section").astype(jnp.int32)[None]
    at_row = lax.rem(lax.axis_index("group").astype(jnp.int32), ROW)
    rows = resp_queries.shape[0]
    half = prompt_kv.shape[2] // 2
    k_part = prompt_kv.shape[3] // CHUNKS
    pack_cols = 2 * (resp_queries.shape[1] + resp_keys.shape[1]) // tp_count
    bf16, f32 = jnp.bfloat16, jnp.float32
    part = jax.ShapeDtypeStruct((2, half, k_part), bf16)

    meta = jnp.concatenate([tp, section, lengths, owners, visible_tiles[0]])
    halves = small_call(
        halves_kernel,
        "halves",
        [part] * CHUNKS,
        [scalars(), pl.BlockSpec(memory_space=pl.ANY)],
        [pltpu.SemaphoreType.DMA((CHUNKS,))],
        VMEM_MOST,
        pl.ANY,
    )(section, prompt_kv)
    sibling_owner = shifted(after(owners, halves), "section", 1)
    packs = small_call(
        pack_kernel,
        "pack",
        [jax.ShapeDtypeStruct((rows, pack_cols), bf16)] * tp_count,
        [scalars()] + [pl.BlockSpec(memory_space=pl.ANY)] * 4,
        [pltpu.SemaphoreType.DMA((4 * CHUNKS * tp_count,))],
        VMEM_MOST,
        pl.ANY,
    )(after(tp, sibling_owner), resp_queries, resp_dout, resp_keys, resp_values)
    arrived = {d: shifted(packs[d], "tp", d) for d in range(1, tp_count, 2)}
    for d in range(2, tp_count, 2):
        arrived[d] = shifted(after(packs[d], arrived), "tp", d)
    arrived = [packs[0]] + [arrived[d] for d in range(1, tp_count)]

    before = [to_row(block, 1) for block in halves]
    sends = [
        list(
            small_call(sends_kernel, "sends", [part] * (WIN - 1), [scalars()] + [whole()] * 2)(
                after(at_row[None], packs), halves[c], before[c]
            )
        )
        for c in range(CHUNKS)
    ]
    sends[0][1] = after(sends[0][1], sends[1])
    offers = []
    for c in range(CHUNKS):
        offer = {0: halves[c]}
        for offset in (1, 3, 2):
            send = sends[c][offset - 1]
            if c:
                send = after(send, offers[c - 1][offset])
            offer[offset] = along_row(send, offset)
        offers.append([offer[offset] for offset in range(WIN)])

    backs, shares, passing, ringed, terms = [], [], [], {}, []
    for c in range(CHUNKS):
        wanted = small_call(pick_kernel, "pick", part, [scalars()] + [whole()] * WIN)(
            sibling_owner, *offers[c]
        )
        other = shifted(wanted, "section", 1)
        other = after(other, terms)
        backs, own_grad, other_grad = attend(c, meta, arrived, backs, offers[c], other)
        sibling_grad = shifted(other_grad, "section", 1)
        terms = []
        for offset in range(WIN):
            term = jnp.where(owners[0] == offset, own_grad.astype(f32), 0.0) + jnp.where(
                sibling_owner[0] == offset, sibling_grad.astype(f32), 0.0
            )
            terms.append(term if offset == 0 else term.astype(bf16))
        terms = lax.optimization_barrier(terms)
        for offset in (1, 3, 2):
            term = after(terms[offset], ringed[offset]) if c else terms[offset]
            ringed[offset] = along_row(term, -offset)
        kept, passed = terms[0], jnp.zeros(part.shape, f32)
        for offset in range(1, WIN):
            term = ringed[offset].astype(f32)
            crossing = at_row + offset >= ROW
            kept = kept + jnp.where(crossing, 0.0, term)
            passed = passed + jnp.where(crossing, term, 0.0)
        passed = passed.astype(bf16)
        passing.append(passed)
        shares.append((kept + to_row(passed, -1).astype(f32)).astype(bf16))
    backs = after(backs, passing[0])
    returned = [backs[0]] + [shifted(backs[d], "tp", -d) for d in range(1, tp_count)]

    grads = small_call(
        unpack_kernel,
        "unpack",
        [
            jax.ShapeDtypeStruct(resp_queries.shape, bf16),
            jax.ShapeDtypeStruct(resp_keys.shape, bf16),
            jax.ShapeDtypeStruct(resp_values.shape, bf16),
        ],
        [scalars()] + [whole()] * tp_count,
    )(tp, *returned)
    return (grads[0], grads[1], grads[2], jnp.concatenate(shares, -1)[None])


def solution(mesh):
    placed = (
        P(("section", "group", "tp"), None),
        P(("section", "group", "tp"), None),
        P(("section", "group", "tp"), None),
        P(("section", "group", "tp"), None),
        P("group", None, None, "tp"),
        P(("section", "group")),
        P(("section", "group")),
        P(("section", "group"), None),
    )
    return jax.shard_map(
        shards,
        mesh=mesh,
        in_specs=placed,
        out_specs=(
            P(("section", "group", "tp"), None),
            P(("section", "group", "tp"), None),
            P(("section", "group", "tp"), None),
            P("group", None, "section", "tp"),
        ),
        check_vma=False,
    )
```

```python
import functools

import jax
import jax.numpy as jnp
from jax import lax
from jax.experimental import pallas as pl
from jax.experimental.pallas import tpu as pltpu
from jax.sharding import PartitionSpec as P

HEADS = 40
KV_HEADS = 8
HEAD_DIM = 128
PTILE = 128
WIN = 4
PER_KV = HEADS // KV_HEADS
CHUNKS = 2
ROW = 4

MASKED = -1e30
SCALING = HEAD_DIM ** (-0.5)
LOG2E = 1.4426950408889634
VMEM_LIMIT = 48 * 1024 * 1024

TP, SECTION, LENGTH, OWNER, VISIBLE = 0, 1, 2, 3, 4


def shifted(block, axis, distance):
    devices = range(lax.axis_size(axis))
    route = [((i - distance) % len(devices), i) for i in devices]
    return lax.ppermute(block, axis, route)


def after(block, earlier):
    return lax.optimization_barrier((block, earlier))[0]


def along_row(block, distance):
    count = lax.axis_size("group")
    route = [(i - i % ROW + (i - distance) % ROW, i) for i in range(count)]
    return lax.ppermute(block, "group", route)


def to_row(block, distance):
    return shifted(block, "group", distance * ROW)


def whole():
    return pl.BlockSpec(memory_space=pltpu.VMEM)


def scalars():
    return pl.BlockSpec(memory_space=pltpu.SMEM)


def small_call(kernel, name, out_shape, in_specs):
    return pl.pallas_call(
        kernel,
        out_shape=out_shape,
        in_specs=in_specs,
        out_specs=jax.tree.map(lambda _: whole(), out_shape),
        compiler_params=pltpu.CompilerParams(vmem_limit_bytes=VMEM_LIMIT),
        name=name,
    )


def halves_kernel(section, prompt, *parts):
    half, cols = parts[0].shape[1:]
    rows = pl.ds(pl.multiple_of(section[0] * half, half), half)
    for chunk, part in enumerate(parts):
        part[...] = prompt[0, :, rows, chunk * cols : (chunk + 1) * cols]


def sends_kernel(place, own, before, *sends):
    for offset, send in enumerate(sends, 1):

        @pl.when(place[0] + offset >= ROW)
        def _(send=send):
            send[...] = before[...]

        @pl.when(place[0] + offset < ROW)
        def _(send=send):
            send[...] = own[...]


def pick_kernel(which, *refs):
    choices, chosen = refs[:-1], refs[-1]
    for offset, choice in enumerate(choices):

        @pl.when(which[0] == offset)
        def _(choice=choice):
            chosen[...] = choice[...]


def pack_kernel(tp, queries, grad_out, keys, values, *packs):
    tp_count = len(packs)
    for d, pack in enumerate(packs):
        device, at = lax.rem(tp[0] + d, tp_count), 0
        for chunk in range(CHUNKS):
            for source in (queries, grad_out, keys, values):
                cols = source.shape[1] // tp_count
                part = cols // CHUNKS
                start = pl.multiple_of(device * cols + chunk * part, 128)
                pack[:, at : at + part] = source[:, pl.ds(start, part)]
                at += part


def unpack_kernel(tp, *refs):
    packs, (grad_q, grad_k, grad_v) = refs[:-3], refs[-3:]
    tp_count = len(packs)
    q_cols = grad_q.shape[1] // tp_count
    k_cols = grad_k.shape[1] // tp_count
    q_part, k_part = q_cols // CHUNKS, k_cols // CHUNKS
    for d, pack in enumerate(packs):
        device, at = lax.rem(tp[0] + d, tp_count), 0
        for chunk in range(CHUNKS):
            q_at = pl.ds(pl.multiple_of(device * q_cols + chunk * q_part, 128), q_part)
            k_at = pl.ds(pl.multiple_of(device * k_cols + chunk * k_part, 128), k_part)
            grad_q[:, q_at] = pack[:, at : at + q_part]
            at += q_part
            grad_k[:, k_at] = pack[:, at : at + k_part]
            at += k_part
            grad_v[:, k_at] = pack[:, at : at + k_part]
            at += k_part


def place(index, tp, tp_count, rows):
    block = index // rows
    return lax.rem(tp - block + tp_count, tp_count) * rows + lax.rem(index, rows)


def attend_kernel(chunk, tp_count, meta, *refs):
    packs, refs = refs[:tp_count], refs[tp_count:]
    earlier, refs = refs[: tp_count if chunk else 0], refs[tp_count if chunk else 0 :]
    offers, other, refs = refs[:WIN], refs[WIN], refs[WIN + 1 :]
    backs, refs = refs[:tp_count], refs[tp_count:]
    own_grad, other_grad = refs[:2]
    q_all, do_all, keys, values, keys_t, bias, scores, grad_prob, weights, grad_scores, dk, dv = refs[
        2:
    ]
    rows = packs[0].shape[0]
    resp = rows * tp_count
    half, k_cols = other.shape[1:]
    kv_heads = k_cols // HEAD_DIM
    prompt_len = 2 * half
    total = prompt_len + resp
    per_half = half // PTILE
    q_cols = kv_heads * PER_KV * HEAD_DIM
    tp, section, length, owner = meta[TP], meta[SECTION], meta[LENGTH], meta[OWNER]
    taken = chunk * 2 * (q_cols + k_cols)
    given = chunk * (q_cols + 2 * k_cols)
    for back, block in zip(backs, earlier):
        back[:, :given] = block[...]

    key_at = place(lax.broadcasted_iota(jnp.int32, (resp, resp), 0), tp, tp_count, rows)
    row_at = place(lax.broadcasted_iota(jnp.int32, (resp, resp), 1), tp, tp_count, rows)
    bias[...] = jnp.where(key_at <= row_at, 0.0, MASKED)
    live = (
        place(lax.broadcasted_iota(jnp.int32, (1, resp), 1), tp, tp_count, rows) < length
    ).astype(jnp.float32)
    tile_bias = []
    for tile in range(2 * per_half):
        side = section if tile < per_half else 1 - section
        visible = meta[VISIBLE + side * per_half + tile % per_half]
        tile_bias.append(jnp.where(visible == 1, 0.0, MASKED))

    nt = (((1,), (1,)), ((), ()))
    for kv in range(kv_heads):
        at = slice(kv * HEAD_DIM, (kv + 1) * HEAD_DIM)
        for offset, offer in enumerate(offers):

            @pl.when(owner == offset)
            def _(offer=offer):
                keys[:half] = offer[0, :, at]
                values[:half] = offer[1, :, at]

        keys[half:prompt_len] = other[0, :, at]
        values[half:prompt_len] = other[1, :, at]
        for i in range(tp_count):
            here = slice(i * rows, (i + 1) * rows)
            there = slice(prompt_len + i * rows, prompt_len + (i + 1) * rows)
            k_from = taken + 2 * q_cols + kv * HEAD_DIM
            keys[there] = packs[i][:, k_from : k_from + HEAD_DIM]
            values[there] = packs[i][:, k_from + k_cols : k_from + k_cols + HEAD_DIM]
            for head in range(PER_KV):
                q_from = taken + (kv * PER_KV + head) * HEAD_DIM
                q_all[head, here] = packs[i][:, q_from : q_from + HEAD_DIM]
                do_all[head, here] = packs[i][:, q_cols + q_from : q_cols + q_from + HEAD_DIM]
        keys_t[...] = keys[...].T
        dk[...] = jnp.zeros_like(dk)
        dv[...] = jnp.zeros_like(dv)

        for head in range(PER_KV):
            query = q_all[head]
            cotangent = do_all[head]
            tops = []
            for tile in range(total // PTILE):
                span = slice(tile * PTILE, (tile + 1) * PTILE)
                part = lax.dot_general(
                    keys[span], query, nt, preferred_element_type=jnp.float32
                )
                if tile >= 2 * per_half:
                    low = (tile - 2 * per_half) * PTILE
                    part = part + bias[low : low + PTILE]
                scores[span] = part
                top = jnp.max(part.reshape(PTILE // 8, 8, resp), axis=0)
                if tile < 2 * per_half:
                    top = top + tile_bias[tile]
                tops.append(top)
                grad_prob[span] = lax.dot_general(
                    values[span], cotangent, nt, preferred_element_type=jnp.float32
                )
            largest = jnp.max(functools.reduce(jnp.maximum, tops), axis=0, keepdims=True)
            factor = SCALING * LOG2E
            sums = jnp.zeros((8, resp), jnp.float32)
            dots = jnp.zeros((8, resp), jnp.float32)
            for tile in range(total // PTILE):
                span = slice(tile * PTILE, (tile + 1) * PTILE)
                shift = largest
                if tile < 2 * per_half:
                    shift = shift - tile_bias[tile]
                exponent = jnp.exp2((scores[span] - shift) * factor)
                scores[span] = exponent
                sums += jnp.sum(exponent.reshape(PTILE // 8, 8, resp), axis=0)
                dots += jnp.sum((exponent * grad_prob[span]).reshape(PTILE // 8, 8, resp), axis=0)
            inverse = 1.0 / jnp.sum(sums, axis=0, keepdims=True)
            row_delta = jnp.sum(dots, axis=0, keepdims=True) * inverse
            inverse = inverse * live
            for tile in range(total // PTILE):
                span = slice(tile * PTILE, (tile + 1) * PTILE)
                probabilities = scores[span] * inverse
                weights[span] = probabilities.astype(jnp.bfloat16)
                grad_scores[span] = (probabilities * (grad_prob[span] - row_delta)).astype(
                    jnp.bfloat16
                )
            dv[...] += jnp.dot(weights[...], cotangent, preferred_element_type=jnp.float32)
            dk[...] += jnp.dot(grad_scores[...], query, preferred_element_type=jnp.float32)
            grad_query_t = jnp.dot(
                keys_t[...], grad_scores[...], preferred_element_type=jnp.float32
            )
            grad_query = (grad_query_t.T * SCALING).astype(jnp.bfloat16)
            q_from = given + (kv * PER_KV + head) * HEAD_DIM
            for i in range(tp_count):
                backs[i][:, q_from : q_from + HEAD_DIM] = grad_query[i * rows : (i + 1) * rows]

        own_grad[0, :, at] = (dk[:half] * SCALING).astype(jnp.bfloat16)
        other_grad[0, :, at] = (dk[half:prompt_len] * SCALING).astype(jnp.bfloat16)
        own_grad[1, :, at] = dv[:half].astype(jnp.bfloat16)
        other_grad[1, :, at] = dv[half:prompt_len].astype(jnp.bfloat16)
        for i in range(tp_count):
            k_from = given + q_cols + kv * HEAD_DIM
            v_from = k_from + k_cols
            span = slice(prompt_len + i * rows, prompt_len + (i + 1) * rows)
            backs[i][:, k_from : k_from + HEAD_DIM] = (dk[span] * SCALING).astype(jnp.bfloat16)
            backs[i][:, v_from : v_from + HEAD_DIM] = dv[span].astype(jnp.bfloat16)


def attend(chunk, meta, packs, earlier, offers, other):
    tp_count, rows = len(packs), packs[0].shape[0]
    resp = rows * tp_count
    half, k_cols = other.shape[1:]
    kv_heads = k_cols // HEAD_DIM
    q_cols = kv_heads * PER_KV * HEAD_DIM
    total = 2 * half + resp
    f32, bf16 = jnp.float32, jnp.bfloat16
    flops = 10 * resp * total * kv_heads * PER_KV * HEAD_DIM
    results = pl.pallas_call(
        functools.partial(attend_kernel, chunk, tp_count),
        out_shape=[
            jax.ShapeDtypeStruct((rows, (chunk + 1) * (q_cols + 2 * k_cols)), bf16)
        ]
        * tp_count
        + [jax.ShapeDtypeStruct(other.shape, bf16)] * 2,
        in_specs=[scalars()] + [whole()] * (tp_count + len(earlier) + len(offers) + 1),
        out_specs=[whole()] * (tp_count + 2),
        scratch_shapes=[
            pltpu.VMEM((PER_KV, resp, HEAD_DIM), bf16),
            pltpu.VMEM((PER_KV, resp, HEAD_DIM), bf16),
            pltpu.VMEM((total, HEAD_DIM), bf16),
            pltpu.VMEM((total, HEAD_DIM), bf16),
            pltpu.VMEM((HEAD_DIM, total), bf16),
            pltpu.VMEM((resp, resp), f32),
            pltpu.VMEM((total, resp), f32),
            pltpu.VMEM((total, resp), f32),
            pltpu.VMEM((total, resp), bf16),
            pltpu.VMEM((total, resp), bf16),
            pltpu.VMEM((total, HEAD_DIM), f32),
            pltpu.VMEM((total, HEAD_DIM), f32),
        ],
        compiler_params=pltpu.CompilerParams(vmem_limit_bytes=VMEM_LIMIT),
        cost_estimate=pl.CostEstimate(
            flops=flops, bytes_accessed=6 * 1024 * 1024, transcendentals=flops // 1280
        ),
        name="attend",
    )(meta, *packs, *earlier, *offers, other)
    return results[:tp_count], results[tp_count], results[tp_count + 1]


def shards(
    resp_queries, resp_keys, resp_values, resp_dout, prompt_kv, lengths, owners, visible_tiles
):
    tp_count = lax.axis_size("tp")
    tp = lax.axis_index("tp").astype(jnp.int32)[None]
    section = lax.axis_index("section").astype(jnp.int32)[None]
    at_row = lax.rem(lax.axis_index("group").astype(jnp.int32), ROW)
    rows = resp_queries.shape[0]
    half = prompt_kv.shape[2] // 2
    k_part = prompt_kv.shape[3] // CHUNKS
    pack_cols = 2 * (resp_queries.shape[1] + resp_keys.shape[1]) // tp_count
    bf16, f32 = jnp.bfloat16, jnp.float32
    part = jax.ShapeDtypeStruct((2, half, k_part), bf16)

    meta = jnp.concatenate([tp, section, lengths, owners, visible_tiles[0]])
    halves = small_call(
        halves_kernel,
        "halves",
        [part] * CHUNKS,
        [scalars(), whole()],
    )(section, prompt_kv)
    sibling_owner = shifted(after(owners, halves), "section", 1)
    packs = small_call(
        pack_kernel,
        "pack",
        [jax.ShapeDtypeStruct((rows, pack_cols), bf16)] * tp_count,
        [scalars()] + [whole()] * 4,
    )(after(tp, sibling_owner), resp_queries, resp_dout, resp_keys, resp_values)
    arrived = {d: shifted(packs[d], "tp", d) for d in range(1, tp_count, 2)}
    for d in range(2, tp_count, 2):
        arrived[d] = shifted(after(packs[d], arrived), "tp", d)
    arrived = [packs[0]] + [arrived[d] for d in range(1, tp_count)]

    before = [to_row(block, 1) for block in halves]
    sends = [
        list(
            small_call(sends_kernel, "sends", [part] * (WIN - 1), [scalars()] + [whole()] * 2)(
                after(at_row[None], packs), halves[c], before[c]
            )
        )
        for c in range(CHUNKS)
    ]
    sends[0][1] = after(sends[0][1], sends[1])
    offers = []
    for c in range(CHUNKS):
        offer = {0: halves[c]}
        for offset in (1, 3, 2):
            send = sends[c][offset - 1]
            if c:
                send = after(send, offers[c - 1][offset])
            offer[offset] = along_row(send, offset)
        offers.append([offer[offset] for offset in range(WIN)])

    backs, shares, passing, ringed, terms = [], [], [], {}, []
    for c in range(CHUNKS):
        wanted = small_call(pick_kernel, "pick", part, [scalars()] + [whole()] * WIN)(
            sibling_owner, *offers[c]
        )
        other = shifted(wanted, "section", 1)
        other = after(other, terms)
        backs, own_grad, other_grad = attend(c, meta, arrived, backs, offers[c], other)
        sibling_grad = shifted(other_grad, "section", 1)
        terms = []
        for offset in range(WIN):
            term = jnp.where(owners[0] == offset, own_grad.astype(f32), 0.0) + jnp.where(
                sibling_owner[0] == offset, sibling_grad.astype(f32), 0.0
            )
            terms.append(term if offset == 0 else term.astype(bf16))
        terms = lax.optimization_barrier(terms)
        for offset in (1, 3, 2):
            term = after(terms[offset], ringed[offset]) if c else terms[offset]
            ringed[offset] = along_row(term, -offset)
        kept, passed = terms[0], jnp.zeros(part.shape, f32)
        for offset in range(1, WIN):
            term = ringed[offset].astype(f32)
            crossing = at_row + offset >= ROW
            kept = kept + jnp.where(crossing, 0.0, term)
            passed = passed + jnp.where(crossing, term, 0.0)
        passed = passed.astype(bf16)
        passing.append(passed)
        shares.append((kept + to_row(passed, -1).astype(f32)).astype(bf16))
    backs = after(backs, passing[0])
    returned = [backs[0]] + [shifted(backs[d], "tp", -d) for d in range(1, tp_count)]

    grads = small_call(
        unpack_kernel,
        "unpack",
        [
            jax.ShapeDtypeStruct(resp_queries.shape, bf16),
            jax.ShapeDtypeStruct(resp_keys.shape, bf16),
            jax.ShapeDtypeStruct(resp_values.shape, bf16),
        ],
        [scalars()] + [whole()] * tp_count,
    )(tp, *returned)
    return (grads[0], grads[1], grads[2], jnp.concatenate(shares, -1)[None])


def solution(mesh):
    placed = (
        P(("section", "group", "tp"), None),
        P(("section", "group", "tp"), None),
        P(("section", "group", "tp"), None),
        P(("section", "group", "tp"), None),
        P("group", None, None, "tp"),
        P(("section", "group")),
        P(("section", "group")),
        P(("section", "group"), None),
    )
    return jax.shard_map(
        shards,
        mesh=mesh,
        in_specs=placed,
        out_specs=(
            P(("section", "group", "tp"), None),
            P(("section", "group", "tp"), None),
            P(("section", "group", "tp"), None),
            P("group", None, "section", "tp"),
        ),
        check_vma=False,
    )
```

```python
import functools

import jax
import jax.numpy as jnp
from jax import lax
from jax.experimental import pallas as pl
from jax.experimental.pallas import tpu as pltpu
from jax.sharding import PartitionSpec as P

HEADS = 40
KV_HEADS = 8
HEAD_DIM = 128
PTILE = 128
WIN = 4
PER_KV = HEADS // KV_HEADS
CHUNKS = 2
ROW = 4

MASKED = -1e30
SCALING = HEAD_DIM ** (-0.5)
LOG2E = 1.4426950408889634
ATTEND_VMEM = 24 * 1024 * 1024
SMALL_VMEM = 8 * 1024 * 1024

TP, SECTION, LENGTH, OWNER, VISIBLE = 0, 1, 2, 3, 4


def shifted(block, axis, distance):
    devices = range(lax.axis_size(axis))
    route = [((i - distance) % len(devices), i) for i in devices]
    return lax.ppermute(block, axis, route)


def after(block, earlier):
    return lax.optimization_barrier((block, earlier))[0]


def along_row(block, distance):
    count = lax.axis_size("group")
    route = [(i - i % ROW + (i - distance) % ROW, i) for i in range(count)]
    return lax.ppermute(block, "group", route)


def to_row(block, distance):
    return shifted(block, "group", distance * ROW)


def whole():
    return pl.BlockSpec(memory_space=pltpu.VMEM)


def scalars():
    return pl.BlockSpec(memory_space=pltpu.SMEM)


def small_call(kernel, name, out_shape, in_specs):
    return pl.pallas_call(
        kernel,
        out_shape=out_shape,
        in_specs=in_specs,
        out_specs=jax.tree.map(lambda _: whole(), out_shape),
        compiler_params=pltpu.CompilerParams(vmem_limit_bytes=SMALL_VMEM),
        name=name,
    )


def halves_kernel(section, prompt, *parts):
    half, cols = parts[0].shape[1:]
    rows = pl.ds(pl.multiple_of(section[0] * half, half), half)
    for chunk, part in enumerate(parts):
        part[...] = prompt[0, :, rows, chunk * cols : (chunk + 1) * cols]


def sends_kernel(place, own, before, *sends):
    for offset, send in enumerate(sends, 1):

        @pl.when(place[0] + offset >= ROW)
        def _(send=send):
            send[...] = before[...]

        @pl.when(place[0] + offset < ROW)
        def _(send=send):
            send[...] = own[...]


def pick_kernel(which, *refs):
    choices, chosen = refs[:-1], refs[-1]
    for offset, choice in enumerate(choices):

        @pl.when(which[0] == offset)
        def _(choice=choice):
            chosen[...] = choice[...]


def pack_kernel(meta, queries, grad_out, keys, values, *packs):
    tp_count = len(packs)
    for d, pack in enumerate(packs):
        device, at = lax.rem(meta[TP] + d, tp_count), 0
        for chunk in range(CHUNKS):
            for source in (queries, grad_out, keys, values):
                cols = source.shape[1] // tp_count
                part = cols // CHUNKS
                start = pl.multiple_of(device * cols + chunk * part, 128)
                pack[:, at : at + part] = source[:, pl.ds(start, part)]
                at += part


def unpack_kernel(tp, *refs):
    packs, (grad_q, grad_k, grad_v) = refs[:-3], refs[-3:]
    tp_count = len(packs)
    q_cols = grad_q.shape[1] // tp_count
    k_cols = grad_k.shape[1] // tp_count
    q_part, k_part = q_cols // CHUNKS, k_cols // CHUNKS
    for d, pack in enumerate(packs):
        device, at = lax.rem(tp[0] + d, tp_count), 0
        for chunk in range(CHUNKS):
            q_at = pl.ds(pl.multiple_of(device * q_cols + chunk * q_part, 128), q_part)
            k_at = pl.ds(pl.multiple_of(device * k_cols + chunk * k_part, 128), k_part)
            grad_q[:, q_at] = pack[:, at : at + q_part]
            at += q_part
            grad_k[:, k_at] = pack[:, at : at + k_part]
            at += k_part
            grad_v[:, k_at] = pack[:, at : at + k_part]
            at += k_part


def finish_kernel(*refs):
    shares, total = refs[:-1], refs[-1]
    cols = shares[0].shape[2]
    for chunk in range(CHUNKS):
        kept, came = shares[2 * chunk : 2 * chunk + 2]
        whole_sum = kept[...] + came[...].astype(jnp.float32)
        total[0, :, :, chunk * cols : (chunk + 1) * cols] = whole_sum.astype(jnp.bfloat16)


def place(index, tp, tp_count, rows):
    block = index // rows
    return lax.rem(tp - block + tp_count, tp_count) * rows + lax.rem(index, rows)


def attend_kernel(chunk, tp_count, meta, *refs):
    packs, refs = refs[:tp_count], refs[tp_count:]
    earlier, refs = refs[: tp_count if chunk else 0], refs[tp_count if chunk else 0 :]
    offers, other, refs = refs[:WIN], refs[WIN], refs[WIN + 1 :]
    backs, refs = refs[:tp_count], refs[tp_count:]
    own_grad, other_grad = refs[:2]
    q_all, do_all, keys, values, keys_t, bias, scores, grad_prob, weights, grad_scores, dk, dv = refs[
        2:
    ]
    rows = packs[0].shape[0]
    resp = rows * tp_count
    half, k_cols = other.shape[1:]
    kv_heads = k_cols // HEAD_DIM
    prompt_len = 2 * half
    total = prompt_len + resp
    per_half = half // PTILE
    q_cols = kv_heads * PER_KV * HEAD_DIM
    tp, section, length, owner = meta[TP], meta[SECTION], meta[LENGTH], meta[OWNER]
    taken = chunk * 2 * (q_cols + k_cols)
    given = chunk * (q_cols + 2 * k_cols)
    for back, block in zip(backs, earlier):
        back[:, :given] = block[...]

    key_at = place(lax.broadcasted_iota(jnp.int32, (resp, resp), 0), tp, tp_count, rows)
    row_at = place(lax.broadcasted_iota(jnp.int32, (resp, resp), 1), tp, tp_count, rows)
    bias[...] = jnp.where(key_at <= row_at, 0.0, MASKED)
    live = (
        place(lax.broadcasted_iota(jnp.int32, (1, resp), 1), tp, tp_count, rows) < length
    ).astype(jnp.float32)
    tile_bias = []
    for tile in range(2 * per_half):
        side = section if tile < per_half else 1 - section
        visible = meta[VISIBLE + side * per_half + tile % per_half]
        tile_bias.append(jnp.where(visible == 1, 0.0, MASKED))

    nt = (((1,), (1,)), ((), ()))
    for kv in range(kv_heads):
        at = slice(kv * HEAD_DIM, (kv + 1) * HEAD_DIM)
        for offset, offer in enumerate(offers):

            @pl.when(owner == offset)
            def _(offer=offer):
                keys[:half] = offer[0, :, at]
                values[:half] = offer[1, :, at]

        keys[half:prompt_len] = other[0, :, at]
        values[half:prompt_len] = other[1, :, at]
        for i in range(tp_count):
            here = slice(i * rows, (i + 1) * rows)
            there = slice(prompt_len + i * rows, prompt_len + (i + 1) * rows)
            k_from = taken + 2 * q_cols + kv * HEAD_DIM
            keys[there] = packs[i][:, k_from : k_from + HEAD_DIM]
            values[there] = packs[i][:, k_from + k_cols : k_from + k_cols + HEAD_DIM]
            for head in range(PER_KV):
                q_from = taken + (kv * PER_KV + head) * HEAD_DIM
                q_all[head, here] = packs[i][:, q_from : q_from + HEAD_DIM]
                do_all[head, here] = packs[i][:, q_cols + q_from : q_cols + q_from + HEAD_DIM]
        keys_t[...] = keys[...].T
        dk[...] = jnp.zeros_like(dk)
        dv[...] = jnp.zeros_like(dv)

        for head in range(PER_KV):
            query = q_all[head]
            cotangent = do_all[head]
            tops = []
            for tile in range(total // PTILE):
                span = slice(tile * PTILE, (tile + 1) * PTILE)
                part = lax.dot_general(
                    keys[span], query, nt, preferred_element_type=jnp.float32
                )
                if tile >= 2 * per_half:
                    low = (tile - 2 * per_half) * PTILE
                    part = part + bias[low : low + PTILE]
                scores[span] = part
                top = jnp.max(part.reshape(PTILE // 8, 8, resp), axis=0)
                if tile < 2 * per_half:
                    top = top + tile_bias[tile]
                tops.append(top)
                grad_prob[span] = lax.dot_general(
                    values[span], cotangent, nt, preferred_element_type=jnp.float32
                )
            largest = jnp.max(functools.reduce(jnp.maximum, tops), axis=0, keepdims=True)
            factor = SCALING * LOG2E
            sums = jnp.zeros((8, resp), jnp.float32)
            dots = jnp.zeros((8, resp), jnp.float32)
            for tile in range(total // PTILE):
                span = slice(tile * PTILE, (tile + 1) * PTILE)
                shift = largest
                if tile < 2 * per_half:
                    shift = shift - tile_bias[tile]
                exponent = jnp.exp2((scores[span] - shift) * factor)
                scores[span] = exponent
                sums += jnp.sum(exponent.reshape(PTILE // 8, 8, resp), axis=0)
                dots += jnp.sum((exponent * grad_prob[span]).reshape(PTILE // 8, 8, resp), axis=0)
            inverse = 1.0 / jnp.sum(sums, axis=0, keepdims=True)
            row_delta = jnp.sum(dots, axis=0, keepdims=True) * inverse
            inverse = inverse * live
            for tile in range(total // PTILE):
                span = slice(tile * PTILE, (tile + 1) * PTILE)
                probabilities = scores[span] * inverse
                weights[span] = probabilities.astype(jnp.bfloat16)
                grad_scores[span] = (probabilities * (grad_prob[span] - row_delta)).astype(
                    jnp.bfloat16
                )
            dv[...] += jnp.dot(weights[...], cotangent, preferred_element_type=jnp.float32)
            dk[...] += jnp.dot(grad_scores[...], query, preferred_element_type=jnp.float32)
            grad_query_t = jnp.dot(
                keys_t[...], grad_scores[...], preferred_element_type=jnp.float32
            )
            grad_query = (grad_query_t.T * SCALING).astype(jnp.bfloat16)
            q_from = given + (kv * PER_KV + head) * HEAD_DIM
            for i in range(tp_count):
                backs[i][:, q_from : q_from + HEAD_DIM] = grad_query[i * rows : (i + 1) * rows]

        own_grad[0, :, at] = (dk[:half] * SCALING).astype(jnp.bfloat16)
        other_grad[0, :, at] = (dk[half:prompt_len] * SCALING).astype(jnp.bfloat16)
        own_grad[1, :, at] = dv[:half].astype(jnp.bfloat16)
        other_grad[1, :, at] = dv[half:prompt_len].astype(jnp.bfloat16)
        for i in range(tp_count):
            k_from = given + q_cols + kv * HEAD_DIM
            v_from = k_from + k_cols
            span = slice(prompt_len + i * rows, prompt_len + (i + 1) * rows)
            backs[i][:, k_from : k_from + HEAD_DIM] = (dk[span] * SCALING).astype(jnp.bfloat16)
            backs[i][:, v_from : v_from + HEAD_DIM] = dv[span].astype(jnp.bfloat16)


def attend(chunk, meta, packs, earlier, offers, other):
    tp_count, rows = len(packs), packs[0].shape[0]
    resp = rows * tp_count
    half, k_cols = other.shape[1:]
    kv_heads = k_cols // HEAD_DIM
    q_cols = kv_heads * PER_KV * HEAD_DIM
    total = 2 * half + resp
    f32, bf16 = jnp.float32, jnp.bfloat16
    flops = 10 * resp * total * kv_heads * PER_KV * HEAD_DIM
    results = pl.pallas_call(
        functools.partial(attend_kernel, chunk, tp_count),
        out_shape=[
            jax.ShapeDtypeStruct((rows, (chunk + 1) * (q_cols + 2 * k_cols)), bf16)
        ]
        * tp_count
        + [jax.ShapeDtypeStruct(other.shape, bf16)] * 2,
        in_specs=[scalars()] + [whole()] * (tp_count + len(earlier) + len(offers) + 1),
        out_specs=[whole()] * (tp_count + 2),
        scratch_shapes=[
            pltpu.VMEM((PER_KV, resp, HEAD_DIM), bf16),
            pltpu.VMEM((PER_KV, resp, HEAD_DIM), bf16),
            pltpu.VMEM((total, HEAD_DIM), bf16),
            pltpu.VMEM((total, HEAD_DIM), bf16),
            pltpu.VMEM((HEAD_DIM, total), bf16),
            pltpu.VMEM((resp, resp), f32),
            pltpu.VMEM((total, resp), f32),
            pltpu.VMEM((total, resp), f32),
            pltpu.VMEM((total, resp), bf16),
            pltpu.VMEM((total, resp), bf16),
            pltpu.VMEM((total, HEAD_DIM), f32),
            pltpu.VMEM((total, HEAD_DIM), f32),
        ],
        compiler_params=pltpu.CompilerParams(vmem_limit_bytes=ATTEND_VMEM),
        cost_estimate=pl.CostEstimate(
            flops=8 * flops, bytes_accessed=6 * 1024 * 1024, transcendentals=flops // 1280
        ),
        name="attend",
    )(meta, *packs, *earlier, *offers, other)
    return results[:tp_count], results[tp_count], results[tp_count + 1]


def shards(
    resp_queries, resp_keys, resp_values, resp_dout, prompt_kv, lengths, owners, visible_tiles
):
    tp_count = lax.axis_size("tp")
    tp = lax.axis_index("tp").astype(jnp.int32)[None]
    section = lax.axis_index("section").astype(jnp.int32)[None]
    at_row = lax.rem(lax.axis_index("group").astype(jnp.int32), ROW)
    rows = resp_queries.shape[0]
    half = prompt_kv.shape[2] // 2
    k_part = prompt_kv.shape[3] // CHUNKS
    pack_cols = 2 * (resp_queries.shape[1] + resp_keys.shape[1]) // tp_count
    bf16, f32 = jnp.bfloat16, jnp.float32
    part = jax.ShapeDtypeStruct((2, half, k_part), bf16)

    halves = small_call(
        halves_kernel,
        "halves",
        [part] * CHUNKS,
        [scalars(), whole()],
    )(section, prompt_kv)
    sibling_owner = shifted(after(owners, halves), "section", 1)
    meta = jnp.concatenate([tp, section, lengths, owners, visible_tiles[0]])
    meta = after(meta, sibling_owner)
    packs = small_call(
        pack_kernel,
        "pack",
        [jax.ShapeDtypeStruct((rows, pack_cols), bf16)] * tp_count,
        [scalars()] + [whole()] * 4,
    )(meta, resp_queries, resp_dout, resp_keys, resp_values)
    arrived = {d: shifted(packs[d], "tp", d) for d in range(1, tp_count, 2)}
    for d in range(2, tp_count, 2):
        arrived[d] = shifted(after(packs[d], arrived), "tp", d)
    arrived = [packs[0]] + [arrived[d] for d in range(1, tp_count)]

    before = [to_row(block, 1) for block in halves]
    sends = [
        list(
            small_call(sends_kernel, "sends", [part] * (WIN - 1), [scalars()] + [whole()] * 2)(
                after(at_row[None], packs), halves[c], before[c]
            )
        )
        for c in range(CHUNKS)
    ]

    offers = []
    for c in range(CHUNKS):
        offer = {0: halves[c]}
        for offset in (1, 3, 2):
            send = sends[c][offset - 1]
            if c:
                send = after(send, offers[c - 1][offset])
            offer[offset] = along_row(send, offset)
        offers.append([offer[offset] for offset in range(WIN)])

    backs, shares, passing, ringed, terms = [], [], [], {}, []
    for c in range(CHUNKS):
        wanted = small_call(pick_kernel, "pick", part, [scalars()] + [whole()] * WIN)(
            sibling_owner, *offers[c]
        )
        other = shifted(wanted, "section", 1)
        other = after(other, terms)
        backs, own_grad, other_grad = attend(c, meta, arrived, backs, offers[c], other)
        if c == CHUNKS - 1:
            returned = {d: shifted(backs[d], "tp", -d) for d in range(1, tp_count, 2)}
            for d in range(2, tp_count, 2):
                returned[d] = shifted(after(backs[d], returned), "tp", -d)
        sibling_grad = after(shifted(other_grad, "section", 1), passing)
        terms = []
        for offset in range(WIN):
            term = jnp.where(owners[0] == offset, own_grad.astype(f32), 0.0) + jnp.where(
                sibling_owner[0] == offset, sibling_grad.astype(f32), 0.0
            )
            terms.append(term if offset == 0 else term.astype(bf16))
        terms = lax.optimization_barrier(terms)
        for offset in (1, 3, 2):
            term = after(terms[offset], ringed[offset]) if c else terms[offset]
            ringed[offset] = along_row(term, -offset)
        kept, passed = terms[0], jnp.zeros(part.shape, f32)
        for offset in range(1, WIN):
            term = ringed[offset].astype(f32)
            crossing = at_row + offset >= ROW
            kept = kept + jnp.where(crossing, 0.0, term)
            passed = passed + jnp.where(crossing, term, 0.0)
        passed = passed.astype(bf16)
        if c == CHUNKS - 1:
            passed = after(passed, (returned[1], returned[tp_count - 1]))
        passing.append(passed)
        shares += [kept, passed]

    grads = small_call(
        unpack_kernel,
        "unpack",
        [
            jax.ShapeDtypeStruct(resp_queries.shape, bf16),
            jax.ShapeDtypeStruct(resp_keys.shape, bf16),
            jax.ShapeDtypeStruct(resp_values.shape, bf16),
        ],
        [scalars()] + [whole()] * tp_count,
    )(tp, backs[0], *[returned[d] for d in range(1, tp_count)])
    shares[1] = to_row(after(shares[1], returned[1]), -1)
    shares[3] = to_row(shares[3], -1)
    prompt_grads = small_call(
        finish_kernel,
        "finish",
        jax.ShapeDtypeStruct((1, 2, half, prompt_kv.shape[3]), bf16),
        [whole()] * len(shares),
    )(*shares)
    return (grads[0], grads[1], grads[2], prompt_grads)


def solution(mesh):
    placed = (
        P(("section", "group", "tp"), None),
        P(("section", "group", "tp"), None),
        P(("section", "group", "tp"), None),
        P(("section", "group", "tp"), None),
        P("group", None, None, "tp"),
        P(("section", "group")),
        P(("section", "group")),
        P(("section", "group"), None),
    )
    return jax.shard_map(
        shards,
        mesh=mesh,
        in_specs=placed,
        out_specs=(
            P(("section", "group", "tp"), None),
            P(("section", "group", "tp"), None),
            P(("section", "group", "tp"), None),
            P("group", None, "section", "tp"),
        ),
        check_vma=False,
    )
```

```python
import functools

import jax
import jax.numpy as jnp
from jax import lax
from jax.experimental import pallas as pl
from jax.experimental.pallas import tpu as pltpu
from jax.sharding import PartitionSpec as P

HEADS = 40
KV_HEADS = 8
HEAD_DIM = 128
PTILE = 128
WIN = 4
PER_KV = HEADS // KV_HEADS
CHUNKS = 2
ROW = 4

MASKED = -1e30
SCALING = HEAD_DIM ** (-0.5)
LOG2E = 1.4426950408889634
ATTEND_VMEM = 24 * 1024 * 1024
SMALL_VMEM = 8 * 1024 * 1024

TP, SECTION, LENGTH, VISIBLE = 0, 1, 2, 3


def shifted(block, axis, distance):
    devices = range(lax.axis_size(axis))
    route = [((i - distance) % len(devices), i) for i in devices]
    return lax.ppermute(block, axis, route)


def after(block, earlier):
    return lax.optimization_barrier((block, earlier))[0]


def along_row(block, distance):
    count = lax.axis_size("group")
    route = [(i - i % ROW + (i - distance) % ROW, i) for i in range(count)]
    return lax.ppermute(block, "group", route)


def to_row(block, distance):
    return shifted(block, "group", distance * ROW)


def whole():
    return pl.BlockSpec(memory_space=pltpu.VMEM)


def scalars():
    return pl.BlockSpec(memory_space=pltpu.SMEM)


def small_call(kernel, name, out_shape, in_specs):
    return pl.pallas_call(
        kernel,
        out_shape=out_shape,
        in_specs=in_specs,
        out_specs=jax.tree.map(lambda _: whole(), out_shape),
        compiler_params=pltpu.CompilerParams(vmem_limit_bytes=SMALL_VMEM),
        name=name,
    )


def halves_kernel(section, prompt, *parts):
    half, cols = parts[0].shape[1:]
    rows = pl.ds(pl.multiple_of(section[0] * half, half), half)
    for chunk, part in enumerate(parts):
        part[...] = prompt[0, :, rows, chunk * cols : (chunk + 1) * cols]


def sends_kernel(place, own, before, *sends):
    for offset, send in enumerate(sends, 1):

        @pl.when(place[0] + offset >= ROW)
        def _(send=send):
            send[...] = before[...]

        @pl.when(place[0] + offset < ROW)
        def _(send=send):
            send[...] = own[...]


def pick_kernel(first, second, *refs):
    choices, chosen = refs[:WIN], refs[WIN:]
    for which, target in zip((first, second), chosen):
        for offset, choice in enumerate(choices):

            @pl.when(which[0] == offset)
            def _(choice=choice, target=target):
                target[...] = choice[...]


def pack_kernel(meta, queries, grad_out, keys, values, *packs):
    tp_count = len(packs)
    for d, pack in enumerate(packs):
        device, at = lax.rem(meta[TP] + d, tp_count), 0
        for chunk in range(CHUNKS):
            for source in (queries, grad_out, keys, values):
                cols = source.shape[1] // tp_count
                part = cols // CHUNKS
                start = pl.multiple_of(device * cols + chunk * part, 128)
                pack[:, at : at + part] = source[:, pl.ds(start, part)]
                at += part


def unpack_kernel(tp, *refs):
    packs, (grad_q, grad_k, grad_v) = refs[:-3], refs[-3:]
    tp_count = len(packs)
    q_cols = grad_q.shape[1] // tp_count
    k_cols = grad_k.shape[1] // tp_count
    q_part, k_part = q_cols // CHUNKS, k_cols // CHUNKS
    for d, pack in enumerate(packs):
        device, at = lax.rem(tp[0] + d, tp_count), 0
        for chunk in range(CHUNKS):
            q_at = pl.ds(pl.multiple_of(device * q_cols + chunk * q_part, 128), q_part)
            k_at = pl.ds(pl.multiple_of(device * k_cols + chunk * k_part, 128), k_part)
            grad_q[:, q_at] = pack[:, at : at + q_part]
            at += q_part
            grad_k[:, k_at] = pack[:, at : at + k_part]
            at += k_part
            grad_v[:, k_at] = pack[:, at : at + k_part]
            at += k_part


def finish_kernel(*refs):
    shares, total = refs[:-1], refs[-1]
    cols = shares[0].shape[2]
    for chunk in range(CHUNKS):
        kept, came = shares[2 * chunk : 2 * chunk + 2]
        whole_sum = kept[...] + came[...].astype(jnp.float32)
        total[0, :, :, chunk * cols : (chunk + 1) * cols] = whole_sum.astype(jnp.bfloat16)


def place(index, tp, tp_count, rows):
    block = index // rows
    return lax.rem(tp - block + tp_count, tp_count) * rows + lax.rem(index, rows)


def attend_kernel(chunk, tp_count, meta, *refs):
    packs, refs = refs[:tp_count], refs[tp_count:]
    earlier, refs = refs[: tp_count if chunk else 0], refs[tp_count if chunk else 0 :]
    (own, other), refs = refs[:2], refs[2:]
    backs, refs = refs[:tp_count], refs[tp_count:]
    own_grad, other_grad = refs[:2]
    q_all, do_all, keys, values, keys_t, bias, scores, grad_prob, weights, grad_scores, dk, dv = refs[
        2:
    ]
    rows = packs[0].shape[0]
    resp = rows * tp_count
    half, k_cols = other.shape[1:]
    kv_heads = k_cols // HEAD_DIM
    prompt_len = 2 * half
    total = prompt_len + resp
    per_half = half // PTILE
    q_cols = kv_heads * PER_KV * HEAD_DIM
    tp, section, length = meta[TP], meta[SECTION], meta[LENGTH]
    taken = chunk * 2 * (q_cols + k_cols)
    given = chunk * (q_cols + 2 * k_cols)
    for back, block in zip(backs, earlier):
        back[:, :given] = block[...]

    key_at = place(lax.broadcasted_iota(jnp.int32, (resp, resp), 0), tp, tp_count, rows)
    row_at = place(lax.broadcasted_iota(jnp.int32, (resp, resp), 1), tp, tp_count, rows)
    bias[...] = jnp.where(key_at <= row_at, 0.0, MASKED)
    live = (
        place(lax.broadcasted_iota(jnp.int32, (1, resp), 1), tp, tp_count, rows) < length
    ).astype(jnp.float32)
    tile_bias = []
    for tile in range(2 * per_half):
        side = section if tile < per_half else 1 - section
        visible = meta[VISIBLE + side * per_half + tile % per_half]
        tile_bias.append(jnp.where(visible == 1, 0.0, MASKED))

    nt = (((1,), (1,)), ((), ()))
    for kv in range(kv_heads):
        at = slice(kv * HEAD_DIM, (kv + 1) * HEAD_DIM)
        keys[:half] = own[0, :, at]
        values[:half] = own[1, :, at]
        keys[half:prompt_len] = other[0, :, at]
        values[half:prompt_len] = other[1, :, at]
        for i in range(tp_count):
            here = slice(i * rows, (i + 1) * rows)
            there = slice(prompt_len + i * rows, prompt_len + (i + 1) * rows)
            k_from = taken + 2 * q_cols + kv * HEAD_DIM
            keys[there] = packs[i][:, k_from : k_from + HEAD_DIM]
            values[there] = packs[i][:, k_from + k_cols : k_from + k_cols + HEAD_DIM]
            for head in range(PER_KV):
                q_from = taken + (kv * PER_KV + head) * HEAD_DIM
                q_all[head, here] = packs[i][:, q_from : q_from + HEAD_DIM]
                do_all[head, here] = packs[i][:, q_cols + q_from : q_cols + q_from + HEAD_DIM]
        keys_t[...] = keys[...].T

        def products(head, tile):
            span = slice(tile * PTILE, (tile + 1) * PTILE)
            part = lax.dot_general(
                keys[span], q_all[head], nt, preferred_element_type=jnp.float32
            )
            if tile >= 2 * per_half:
                low = tile * PTILE - prompt_len
                part = part + bias[low : low + PTILE]
            scores[head % 2, span] = part
            grad_prob[head % 2, span] = lax.dot_general(
                values[span], do_all[head], nt, preferred_element_type=jnp.float32
            )
            top = jnp.max(part.reshape(PTILE // 8, 8, resp), axis=0)
            return top + tile_bias[tile] if tile < 2 * per_half else top

        tiles = total // PTILE
        tops = [products(0, tile) for tile in range(tiles)]
        for head in range(PER_KV):
            buf = head % 2
            largest = jnp.max(functools.reduce(jnp.maximum, tops), axis=0, keepdims=True)
            sums, dots, tops = [], [], []
            for tile in range(tiles):
                span = slice(tile * PTILE, (tile + 1) * PTILE)
                shift = largest - tile_bias[tile] if tile < 2 * per_half else largest
                exponent = jnp.exp2((scores[buf, span] - shift) * (SCALING * LOG2E))
                scores[buf, span] = exponent
                sums.append(jnp.sum(exponent.reshape(PTILE // 8, 8, resp), axis=0))
                weighed = exponent * grad_prob[buf, span]
                dots.append(jnp.sum(weighed.reshape(PTILE // 8, 8, resp), axis=0))
                if head + 1 < PER_KV:
                    tops.append(products(head + 1, tile))
            inverse = 1.0 / jnp.sum(functools.reduce(jnp.add, sums), axis=0, keepdims=True)
            row_delta = (
                jnp.sum(functools.reduce(jnp.add, dots), axis=0, keepdims=True) * inverse
            )
            inverse = inverse * live
            for tile in range(tiles):
                span = slice(tile * PTILE, (tile + 1) * PTILE)
                probabilities = scores[buf, span] * inverse
                weights[buf, span] = probabilities.astype(jnp.bfloat16)
                grad_scores[buf, span] = (
                    probabilities * (grad_prob[buf, span] - row_delta)
                ).astype(jnp.bfloat16)
            for target, left, right in (
                (dv, weights, do_all),
                (dk, grad_scores, q_all),
            ):
                product = jnp.dot(left[buf], right[head], preferred_element_type=jnp.float32)
                target[...] = product if head == 0 else target[...] + product
            grad_query_t = jnp.dot(
                keys_t[...], grad_scores[buf], preferred_element_type=jnp.float32
            )
            grad_query = (grad_query_t.T * SCALING).astype(jnp.bfloat16)
            q_from = given + (kv * PER_KV + head) * HEAD_DIM
            for i in range(tp_count):
                backs[i][:, q_from : q_from + HEAD_DIM] = grad_query[i * rows : (i + 1) * rows]

        own_grad[0, :, at] = (dk[:half] * SCALING).astype(jnp.bfloat16)
        other_grad[0, :, at] = (dk[half:prompt_len] * SCALING).astype(jnp.bfloat16)
        own_grad[1, :, at] = dv[:half].astype(jnp.bfloat16)
        other_grad[1, :, at] = dv[half:prompt_len].astype(jnp.bfloat16)
        for i in range(tp_count):
            k_from = given + q_cols + kv * HEAD_DIM
            v_from = k_from + k_cols
            span = slice(prompt_len + i * rows, prompt_len + (i + 1) * rows)
            backs[i][:, k_from : k_from + HEAD_DIM] = (dk[span] * SCALING).astype(jnp.bfloat16)
            backs[i][:, v_from : v_from + HEAD_DIM] = dv[span].astype(jnp.bfloat16)


def attend(chunk, meta, packs, earlier, own, other):
    tp_count, rows = len(packs), packs[0].shape[0]
    resp = rows * tp_count
    half, k_cols = other.shape[1:]
    kv_heads = k_cols // HEAD_DIM
    q_cols = kv_heads * PER_KV * HEAD_DIM
    total = 2 * half + resp
    f32, bf16 = jnp.float32, jnp.bfloat16
    flops = 10 * resp * total * kv_heads * PER_KV * HEAD_DIM
    results = pl.pallas_call(
        functools.partial(attend_kernel, chunk, tp_count),
        out_shape=[
            jax.ShapeDtypeStruct((rows, (chunk + 1) * (q_cols + 2 * k_cols)), bf16)
        ]
        * tp_count
        + [jax.ShapeDtypeStruct(other.shape, bf16)] * 2,
        in_specs=[scalars()] + [whole()] * (tp_count + len(earlier) + 2),
        out_specs=[whole()] * (tp_count + 2),
        scratch_shapes=[
            pltpu.VMEM((PER_KV, resp, HEAD_DIM), bf16),
            pltpu.VMEM((PER_KV, resp, HEAD_DIM), bf16),
            pltpu.VMEM((total, HEAD_DIM), bf16),
            pltpu.VMEM((total, HEAD_DIM), bf16),
            pltpu.VMEM((HEAD_DIM, total), bf16),
            pltpu.VMEM((resp, resp), f32),
            pltpu.VMEM((2, total, resp), f32),
            pltpu.VMEM((2, total, resp), f32),
            pltpu.VMEM((2, total, resp), bf16),
            pltpu.VMEM((2, total, resp), bf16),
            pltpu.VMEM((total, HEAD_DIM), f32),
            pltpu.VMEM((total, HEAD_DIM), f32),
        ],
        compiler_params=pltpu.CompilerParams(vmem_limit_bytes=ATTEND_VMEM),
        cost_estimate=pl.CostEstimate(
            flops=8 * flops, bytes_accessed=6 * 1024 * 1024, transcendentals=flops // 1280
        ),
        name="attend",
    )(meta, *packs, *earlier, own, other)
    return results[:tp_count], results[tp_count], results[tp_count + 1]


def shards(
    resp_queries, resp_keys, resp_values, resp_dout, prompt_kv, lengths, owners, visible_tiles
):
    tp_count = lax.axis_size("tp")
    tp = lax.axis_index("tp").astype(jnp.int32)[None]
    section = lax.axis_index("section").astype(jnp.int32)[None]
    at_row = lax.rem(lax.axis_index("group").astype(jnp.int32), ROW)
    rows = resp_queries.shape[0]
    half = prompt_kv.shape[2] // 2
    k_part = prompt_kv.shape[3] // CHUNKS
    pack_cols = 2 * (resp_queries.shape[1] + resp_keys.shape[1]) // tp_count
    bf16, f32 = jnp.bfloat16, jnp.float32
    part = jax.ShapeDtypeStruct((2, half, k_part), bf16)

    halves = small_call(
        halves_kernel,
        "halves",
        [part] * CHUNKS,
        [scalars(), whole()],
    )(section, prompt_kv)
    sibling_owner = shifted(after(owners, halves), "section", 1)
    meta = jnp.concatenate([tp, section, lengths, visible_tiles[0]])
    meta = after(meta, sibling_owner)
    packs = small_call(
        pack_kernel,
        "pack",
        [jax.ShapeDtypeStruct((rows, pack_cols), bf16)] * tp_count,
        [scalars()] + [whole()] * 4,
    )(meta, resp_queries, resp_dout, resp_keys, resp_values)
    arrived = {d: shifted(packs[d], "tp", d) for d in range(1, tp_count, 2)}
    for d in range(2, tp_count, 2):
        arrived[d] = shifted(after(packs[d], arrived), "tp", d)
    arrived = [packs[0]] + [arrived[d] for d in range(1, tp_count)]

    before = [to_row(block, 1) for block in halves]
    sends = [
        list(
            small_call(sends_kernel, "sends", [part] * (WIN - 1), [scalars()] + [whole()] * 2)(
                after(at_row[None], packs), halves[c], before[c]
            )
        )
        for c in range(CHUNKS)
    ]

    offers = []
    for c in range(CHUNKS):
        offer = {0: halves[c]}
        for offset in (1, 3, 2):
            send = sends[c][offset - 1]
            if c:
                send = after(send, offers[c - 1][offset])
            offer[offset] = along_row(send, offset)
        offers.append([offer[offset] for offset in range(WIN)])

    backs, shares, passing, ringed, terms = [], [], [], {}, []
    for c in range(CHUNKS):
        wanted, own = small_call(
            pick_kernel, "pick", [part] * 2, [scalars()] * 2 + [whole()] * WIN
        )(sibling_owner, owners, *offers[c])
        other = after(shifted(wanted, "section", 1), terms)
        backs, own_grad, other_grad = attend(c, meta, arrived, backs, own, other)
        if c == CHUNKS - 1:
            returned = {d: shifted(backs[d], "tp", -d) for d in range(1, tp_count, 2)}
            for d in range(2, tp_count, 2):
                returned[d] = shifted(after(backs[d], returned), "tp", -d)
        sibling_grad = after(shifted(other_grad, "section", 1), passing)
        terms = []
        for offset in range(WIN):
            term = jnp.where(owners[0] == offset, own_grad.astype(f32), 0.0) + jnp.where(
                sibling_owner[0] == offset, sibling_grad.astype(f32), 0.0
            )
            terms.append(term if offset == 0 else term.astype(bf16))
        terms = lax.optimization_barrier(terms)
        for offset in (1, 3, 2):
            term = after(terms[offset], ringed[offset]) if c else terms[offset]
            ringed[offset] = along_row(term, -offset)
        kept, passed = terms[0], jnp.zeros(part.shape, f32)
        for offset in range(1, WIN):
            term = ringed[offset].astype(f32)
            crossing = at_row + offset >= ROW
            kept = kept + jnp.where(crossing, 0.0, term)
            passed = passed + jnp.where(crossing, term, 0.0)
        passed = passed.astype(bf16)
        if c == CHUNKS - 1:
            passed = after(passed, (returned[1], returned[tp_count - 1]))
        passing.append(passed)
        shares += [kept, passed]

    shares[1] = to_row(after(shares[1], returned[1]), -1)
    shares[3] = to_row(shares[3], -1)
    prompt_grads = small_call(
        finish_kernel,
        "finish",
        jax.ShapeDtypeStruct((1, 2, half, prompt_kv.shape[3]), bf16),
        [whole()] * len(shares),
    )(*shares)
    grads = small_call(
        unpack_kernel,
        "unpack",
        [
            jax.ShapeDtypeStruct(resp_queries.shape, bf16),
            jax.ShapeDtypeStruct(resp_keys.shape, bf16),
            jax.ShapeDtypeStruct(resp_values.shape, bf16),
        ],
        [scalars()] + [whole()] * tp_count,
    )(after(tp, prompt_grads), backs[0], *[returned[d] for d in range(1, tp_count)])
    return (grads[0], grads[1], grads[2], prompt_grads)


def solution(mesh):
    placed = (
        P(("section", "group", "tp"), None),
        P(("section", "group", "tp"), None),
        P(("section", "group", "tp"), None),
        P(("section", "group", "tp"), None),
        P("group", None, None, "tp"),
        P(("section", "group")),
        P(("section", "group")),
        P(("section", "group"), None),
    )
    return jax.shard_map(
        shards,
        mesh=mesh,
        in_specs=placed,
        out_specs=(
            P(("section", "group", "tp"), None),
            P(("section", "group", "tp"), None),
            P(("section", "group", "tp"), None),
            P("group", None, "section", "tp"),
        ),
        check_vma=False,
    )
```

```python
import functools

import jax
import jax.numpy as jnp
from jax import lax
from jax.experimental import pallas as pl
from jax.experimental.pallas import tpu as pltpu
from jax.sharding import PartitionSpec as P

HEADS = 40
KV_HEADS = 8
HEAD_DIM = 128
PTILE = 128
WIN = 4
PER_KV = HEADS // KV_HEADS
CHUNKS = 2
ROW = 4

MASKED = -1e30
SCALING = HEAD_DIM ** (-0.5)
LOG2E = 1.4426950408889634
ATTEND_VMEM = 24 * 1024 * 1024
SMALL_VMEM = 8 * 1024 * 1024

TP, SECTION, LENGTH, VISIBLE = 0, 1, 2, 3


def shifted(block, axis, distance):
    devices = range(lax.axis_size(axis))
    route = [((i - distance) % len(devices), i) for i in devices]
    return lax.ppermute(block, axis, route)


def after(block, earlier):
    return lax.optimization_barrier((block, earlier))[0]


def along_row(block, distance):
    count = lax.axis_size("group")
    route = [(i - i % ROW + (i - distance) % ROW, i) for i in range(count)]
    return lax.ppermute(block, "group", route)


def to_row(block, distance):
    return shifted(block, "group", distance * ROW)


def whole():
    return pl.BlockSpec(memory_space=pltpu.VMEM)


def scalars():
    return pl.BlockSpec(memory_space=pltpu.SMEM)


def small_call(kernel, name, out_shape, in_specs):
    return pl.pallas_call(
        kernel,
        out_shape=out_shape,
        in_specs=in_specs,
        out_specs=jax.tree.map(lambda _: whole(), out_shape),
        compiler_params=pltpu.CompilerParams(vmem_limit_bytes=SMALL_VMEM),
        name=name,
    )


def halves_kernel(section, prompt, *parts):
    half, cols = parts[0].shape[1:]
    rows = pl.ds(pl.multiple_of(section[0] * half, half), half)
    for chunk, part in enumerate(parts):
        part[...] = prompt[0, :, rows, chunk * cols : (chunk + 1) * cols]


def sends_kernel(place, own, before, *sends):
    for offset, send in enumerate(sends, 1):

        @pl.when(place[0] + offset >= ROW)
        def _(send=send):
            send[...] = before[...]

        @pl.when(place[0] + offset < ROW)
        def _(send=send):
            send[...] = own[...]


def pick_kernel(first, second, *refs):
    choices, chosen = refs[:WIN], refs[WIN:]
    for which, target in zip((first, second), chosen):
        for offset, choice in enumerate(choices):

            @pl.when(which[0] == offset)
            def _(choice=choice, target=target):
                target[...] = choice[...]


def pack_kernel(meta, queries, grad_out, keys, values, *packs):
    tp_count = len(packs)
    for d, pack in enumerate(packs):
        device, at = lax.rem(meta[TP] + d, tp_count), 0
        for chunk in range(CHUNKS):
            for source in (queries, grad_out, keys, values):
                cols = source.shape[1] // tp_count
                part = cols // CHUNKS
                start = pl.multiple_of(device * cols + chunk * part, 128)
                pack[:, at : at + part] = source[:, pl.ds(start, part)]
                at += part


def unpack_kernel(tp, *refs):
    packs, (grad_q, grad_k, grad_v) = refs[:-3], refs[-3:]
    tp_count = len(packs)
    q_cols = grad_q.shape[1] // tp_count
    k_cols = grad_k.shape[1] // tp_count
    q_part, k_part = q_cols // CHUNKS, k_cols // CHUNKS
    for d, pack in enumerate(packs):
        device, at = lax.rem(tp[0] + d, tp_count), 0
        for chunk in range(CHUNKS):
            q_at = pl.ds(pl.multiple_of(device * q_cols + chunk * q_part, 128), q_part)
            k_at = pl.ds(pl.multiple_of(device * k_cols + chunk * k_part, 128), k_part)
            grad_q[:, q_at] = pack[:, at : at + q_part]
            at += q_part
            grad_k[:, k_at] = pack[:, at : at + k_part]
            at += k_part
            grad_v[:, k_at] = pack[:, at : at + k_part]
            at += k_part


def finish_kernel(*refs):
    shares, total = refs[:-1], refs[-1]
    cols = shares[0].shape[2]
    for chunk in range(CHUNKS):
        kept, came = shares[2 * chunk : 2 * chunk + 2]
        whole_sum = kept[...] + came[...].astype(jnp.float32)
        total[0, :, :, chunk * cols : (chunk + 1) * cols] = whole_sum.astype(jnp.bfloat16)


def place(index, tp, tp_count, rows):
    block = index // rows
    return lax.rem(tp - block + tp_count, tp_count) * rows + lax.rem(index, rows)


def attend_kernel(chunk, tp_count, meta, *refs):
    packs, refs = refs[:tp_count], refs[tp_count:]
    earlier, refs = refs[: tp_count if chunk else 0], refs[tp_count if chunk else 0 :]
    (own, other), refs = refs[:2], refs[2:]
    backs, refs = refs[:tp_count], refs[tp_count:]
    own_grad, other_grad = refs[:2]
    q_all, do_all, keys, values, keys_t, bias, scores, grad_prob, weights, grad_scores, dk, dv = refs[
        2:
    ]
    rows = packs[0].shape[0]
    resp = rows * tp_count
    half, k_cols = other.shape[1:]
    kv_heads = k_cols // HEAD_DIM
    prompt_len = 2 * half
    total = prompt_len + resp
    per_half = half // PTILE
    q_cols = kv_heads * PER_KV * HEAD_DIM
    tp, section, length = meta[TP], meta[SECTION], meta[LENGTH]
    taken = chunk * 2 * (q_cols + k_cols)
    given = chunk * (q_cols + 2 * k_cols)
    for back, block in zip(backs, earlier):
        back[:, :given] = block[...]

    key_at = place(lax.broadcasted_iota(jnp.int32, (resp, resp), 0), tp, tp_count, rows)
    row_at = place(lax.broadcasted_iota(jnp.int32, (resp, resp), 1), tp, tp_count, rows)
    bias[...] = jnp.where(key_at <= row_at, 0.0, MASKED)
    live = (
        place(lax.broadcasted_iota(jnp.int32, (1, resp), 1), tp, tp_count, rows) < length
    ).astype(jnp.float32)
    tile_bias = []
    for tile in range(2 * per_half):
        side = section if tile < per_half else 1 - section
        visible = meta[VISIBLE + side * per_half + tile % per_half]
        tile_bias.append(jnp.where(visible == 1, 0.0, MASKED))

    nt = (((1,), (1,)), ((), ()))
    for kv in range(kv_heads):
        at = slice(kv * HEAD_DIM, (kv + 1) * HEAD_DIM)
        keys[:half] = own[0, :, at]
        values[:half] = own[1, :, at]
        keys[half:prompt_len] = other[0, :, at]
        values[half:prompt_len] = other[1, :, at]
        for i in range(tp_count):
            here = slice(i * rows, (i + 1) * rows)
            there = slice(prompt_len + i * rows, prompt_len + (i + 1) * rows)
            k_from = taken + 2 * q_cols + kv * HEAD_DIM
            keys[there] = packs[i][:, k_from : k_from + HEAD_DIM]
            values[there] = packs[i][:, k_from + k_cols : k_from + k_cols + HEAD_DIM]
            for head in range(PER_KV):
                q_from = taken + (kv * PER_KV + head) * HEAD_DIM
                q_all[head, here] = packs[i][:, q_from : q_from + HEAD_DIM]
                do_all[head, here] = packs[i][:, q_cols + q_from : q_cols + q_from + HEAD_DIM]
        keys_t[...] = keys[...].T

        def products(head, tile):
            span = slice(tile * PTILE, (tile + 1) * PTILE)
            part = lax.dot_general(
                keys[span], q_all[head], nt, preferred_element_type=jnp.float32
            )
            if tile >= 2 * per_half:
                low = tile * PTILE - prompt_len
                part = part + bias[low : low + PTILE]
            scores[head % 2, span] = part
            grad_prob[head % 2, span] = lax.dot_general(
                values[span], do_all[head], nt, preferred_element_type=jnp.float32
            )
            top = jnp.max(part.reshape(PTILE // 8, 8, resp), axis=0)
            return top + tile_bias[tile] if tile < 2 * per_half else top

        tiles = total // PTILE
        tops = [products(0, tile) for tile in range(tiles)]
        for head in range(PER_KV):
            buf = head % 2
            largest = jnp.max(functools.reduce(jnp.maximum, tops), axis=0, keepdims=True)
            sums, dots, tops = [], [], []
            for tile in range(tiles):
                span = slice(tile * PTILE, (tile + 1) * PTILE)
                shift = largest - tile_bias[tile] if tile < 2 * per_half else largest
                exponent = jnp.exp2((scores[buf, span] - shift) * (SCALING * LOG2E))
                scores[buf, span] = exponent
                sums.append(jnp.sum(exponent.reshape(PTILE // 8, 8, resp), axis=0))
                weighed = exponent * grad_prob[buf, span]
                dots.append(jnp.sum(weighed.reshape(PTILE // 8, 8, resp), axis=0))
                if head + 1 < PER_KV:
                    tops.append(products(head + 1, tile))
            inverse = 1.0 / jnp.sum(functools.reduce(jnp.add, sums), axis=0, keepdims=True)
            row_delta = (
                jnp.sum(functools.reduce(jnp.add, dots), axis=0, keepdims=True) * inverse
            )
            inverse = inverse * live
            for tile in range(tiles):
                span = slice(tile * PTILE, (tile + 1) * PTILE)
                probabilities = scores[buf, span] * inverse
                weights[buf, span] = probabilities.astype(jnp.bfloat16)
                grad_scores[buf, span] = (
                    probabilities * (grad_prob[buf, span] - row_delta)
                ).astype(jnp.bfloat16)
            for target, left, right in (
                (dv, weights, do_all),
                (dk, grad_scores, q_all),
            ):
                product = jnp.dot(left[buf], right[head], preferred_element_type=jnp.float32)
                target[...] = product if head == 0 else target[...] + product
            grad_query_t = jnp.dot(
                keys_t[...], grad_scores[buf], preferred_element_type=jnp.float32
            )
            grad_query = (grad_query_t.T * SCALING).astype(jnp.bfloat16)
            q_from = given + (kv * PER_KV + head) * HEAD_DIM
            for i in range(tp_count):
                backs[i][:, q_from : q_from + HEAD_DIM] = grad_query[i * rows : (i + 1) * rows]

        own_grad[0, :, at] = (dk[:half] * SCALING).astype(jnp.bfloat16)
        other_grad[0, :, at] = (dk[half:prompt_len] * SCALING).astype(jnp.bfloat16)
        own_grad[1, :, at] = dv[:half].astype(jnp.bfloat16)
        other_grad[1, :, at] = dv[half:prompt_len].astype(jnp.bfloat16)
        for i in range(tp_count):
            k_from = given + q_cols + kv * HEAD_DIM
            v_from = k_from + k_cols
            span = slice(prompt_len + i * rows, prompt_len + (i + 1) * rows)
            backs[i][:, k_from : k_from + HEAD_DIM] = (dk[span] * SCALING).astype(jnp.bfloat16)
            backs[i][:, v_from : v_from + HEAD_DIM] = dv[span].astype(jnp.bfloat16)


def attend(chunk, meta, packs, earlier, own, other):
    tp_count, rows = len(packs), packs[0].shape[0]
    resp = rows * tp_count
    half, k_cols = other.shape[1:]
    kv_heads = k_cols // HEAD_DIM
    q_cols = kv_heads * PER_KV * HEAD_DIM
    total = 2 * half + resp
    f32, bf16 = jnp.float32, jnp.bfloat16
    flops = 10 * resp * total * kv_heads * PER_KV * HEAD_DIM
    results = pl.pallas_call(
        functools.partial(attend_kernel, chunk, tp_count),
        out_shape=[
            jax.ShapeDtypeStruct((rows, (chunk + 1) * (q_cols + 2 * k_cols)), bf16)
        ]
        * tp_count
        + [jax.ShapeDtypeStruct(other.shape, bf16)] * 2,
        in_specs=[scalars()] + [whole()] * (tp_count + len(earlier) + 2),
        out_specs=[whole()] * (tp_count + 2),
        scratch_shapes=[
            pltpu.VMEM((PER_KV, resp, HEAD_DIM), bf16),
            pltpu.VMEM((PER_KV, resp, HEAD_DIM), bf16),
            pltpu.VMEM((total, HEAD_DIM), bf16),
            pltpu.VMEM((total, HEAD_DIM), bf16),
            pltpu.VMEM((HEAD_DIM, total), bf16),
            pltpu.VMEM((resp, resp), f32),
            pltpu.VMEM((2, total, resp), f32),
            pltpu.VMEM((2, total, resp), f32),
            pltpu.VMEM((2, total, resp), bf16),
            pltpu.VMEM((2, total, resp), bf16),
            pltpu.VMEM((total, HEAD_DIM), f32),
            pltpu.VMEM((total, HEAD_DIM), f32),
        ],
        compiler_params=pltpu.CompilerParams(vmem_limit_bytes=ATTEND_VMEM),
        cost_estimate=pl.CostEstimate(
            flops=8 * flops, bytes_accessed=6 * 1024 * 1024, transcendentals=flops // 1280
        ),
        name="attend",
    )(meta, *packs, *earlier, own, other)
    return results[:tp_count], results[tp_count], results[tp_count + 1]


def shards(
    resp_queries, resp_keys, resp_values, resp_dout, prompt_kv, lengths, owners, visible_tiles
):
    tp_count = lax.axis_size("tp")
    tp = lax.axis_index("tp").astype(jnp.int32)[None]
    section = lax.axis_index("section").astype(jnp.int32)[None]
    at_row = lax.rem(lax.axis_index("group").astype(jnp.int32), ROW)
    rows = resp_queries.shape[0]
    half = prompt_kv.shape[2] // 2
    k_part = prompt_kv.shape[3] // CHUNKS
    pack_cols = 2 * (resp_queries.shape[1] + resp_keys.shape[1]) // tp_count
    bf16, f32 = jnp.bfloat16, jnp.float32
    part = jax.ShapeDtypeStruct((2, half, k_part), bf16)

    halves = small_call(
        halves_kernel,
        "halves",
        [part] * CHUNKS,
        [scalars(), whole()],
    )(section, prompt_kv)
    sibling_owner = shifted(after(owners, halves), "section", 1)
    meta = jnp.concatenate([tp, section, lengths, visible_tiles[0]])
    meta = after(meta, sibling_owner)
    packs = small_call(
        pack_kernel,
        "pack",
        [jax.ShapeDtypeStruct((rows, pack_cols), bf16)] * tp_count,
        [scalars()] + [whole()] * 4,
    )(meta, resp_queries, resp_dout, resp_keys, resp_values)
    arrived = {1: shifted(packs[1], "tp", 1)}

    before = [to_row(block, 1) for block in halves]
    for d in range(2, tp_count):
        arrived[d] = shifted(after(packs[d], (arrived[1], before[1]) if d > 2 else arrived[1]), "tp", d)
    arrived = [packs[0]] + [arrived[d] for d in range(1, tp_count)]
    sends = [
        list(
            small_call(sends_kernel, "sends", [part] * (WIN - 1), [scalars()] + [whole()] * 2)(
                after(at_row[None], packs), halves[0], before[0]
            )
        )
    ] + [
        [jnp.where(at_row + offset >= ROW, before[c], halves[c]) for offset in range(1, WIN)]
        for c in range(1, CHUNKS)
    ]
    offers = []
    for c in range(CHUNKS):
        offer = {0: halves[c]}
        for offset in (1, 3, 2):
            send = sends[c][offset - 1]
            if c:
                send = after(send, offers[c - 1][offset])
            offer[offset] = along_row(send, offset)
        offers.append([offer[offset] for offset in range(WIN)])

    backs, shares, passing, ringed, terms = [], [], [], {}, []
    for c in range(CHUNKS):
        wanted, own = small_call(
            pick_kernel, "pick", [part] * 2, [scalars()] * 2 + [whole()] * WIN
        )(sibling_owner, owners, *offers[c])
        other = after(shifted(wanted, "section", 1), terms)
        backs, own_grad, other_grad = attend(c, meta, arrived, backs, own, other)
        if c == CHUNKS - 1:
            returned = {1: shifted(backs[1], "tp", -1)}
            for d in range(2, tp_count):
                first = after(backs[d], returned[1] if d > 2 else shares[1])
                returned[d] = shifted(first, "tp", -d)
        sibling_grad = after(shifted(other_grad, "section", 1), passing)
        terms = []
        for offset in range(WIN):
            term = jnp.where(owners[0] == offset, own_grad.astype(f32), 0.0) + jnp.where(
                sibling_owner[0] == offset, sibling_grad.astype(f32), 0.0
            )
            terms.append(term if offset == 0 else term.astype(bf16))
        terms = lax.optimization_barrier(terms)
        for offset in (1, 3, 2):
            term = after(terms[offset], ringed[offset]) if c else terms[offset]
            ringed[offset] = along_row(term, -offset)
        kept, passed = terms[0], jnp.zeros(part.shape, f32)
        for offset in range(1, WIN):
            term = ringed[offset].astype(f32)
            crossing = at_row + offset >= ROW
            kept = kept + jnp.where(crossing, 0.0, term)
            passed = passed + jnp.where(crossing, term, 0.0)
        passed = passed.astype(bf16)
        if c == CHUNKS - 1:
            passed = after(passed, (returned[1], returned[2]))
        passing.append(passed)
        shares += [kept, to_row(passed, -1)]

    prompt_grads = small_call(
        finish_kernel,
        "finish",
        jax.ShapeDtypeStruct((1, 2, half, prompt_kv.shape[3]), bf16),
        [whole()] * len(shares),
    )(*shares)
    grads = small_call(
        unpack_kernel,
        "unpack",
        [
            jax.ShapeDtypeStruct(resp_queries.shape, bf16),
            jax.ShapeDtypeStruct(resp_keys.shape, bf16),
            jax.ShapeDtypeStruct(resp_values.shape, bf16),
        ],
        [scalars()] + [whole()] * tp_count,
    )(tp, backs[0], *[returned[d] for d in range(1, tp_count)])
    return (grads[0], grads[1], grads[2], prompt_grads)


def solution(mesh):
    placed = (
        P(("section", "group", "tp"), None),
        P(("section", "group", "tp"), None),
        P(("section", "group", "tp"), None),
        P(("section", "group", "tp"), None),
        P("group", None, None, "tp"),
        P(("section", "group")),
        P(("section", "group")),
        P(("section", "group"), None),
    )
    return jax.shard_map(
        shards,
        mesh=mesh,
        in_specs=placed,
        out_specs=(
            P(("section", "group", "tp"), None),
            P(("section", "group", "tp"), None),
            P(("section", "group", "tp"), None),
            P("group", None, "section", "tp"),
        ),
        check_vma=False,
    )
```

```python
import functools

import jax
import jax.numpy as jnp
from jax import lax
from jax.experimental import pallas as pl
from jax.experimental.pallas import tpu as pltpu
from jax.sharding import PartitionSpec as P

HEADS = 40
KV_HEADS = 8
HEAD_DIM = 128
PTILE = 128
WIN = 4
PER_KV = HEADS // KV_HEADS
CHUNKS = 2
ROW = 4

MASKED = -1e30
SCALING = HEAD_DIM ** (-0.5)
LOG2E = 1.4426950408889634
ATTEND_VMEM = 24 * 1024 * 1024
SMALL_VMEM = 8 * 1024 * 1024

TP, SECTION, LENGTH, VISIBLE = 0, 1, 2, 3


def shifted(block, axis, distance):
    devices = range(lax.axis_size(axis))
    route = [((i - distance) % len(devices), i) for i in devices]
    return lax.ppermute(block, axis, route)


def after(block, earlier):
    return lax.optimization_barrier((block, earlier))[0]


def along_row(block, distance):
    count = lax.axis_size("group")
    route = [(i - i % ROW + (i - distance) % ROW, i) for i in range(count)]
    return lax.ppermute(block, "group", route)


def to_row(block, distance):
    return shifted(block, "group", distance * ROW)


def whole():
    return pl.BlockSpec(memory_space=pltpu.VMEM)


def scalars():
    return pl.BlockSpec(memory_space=pltpu.SMEM)


def small_call(kernel, name, out_shape, in_specs):
    return pl.pallas_call(
        kernel,
        out_shape=out_shape,
        in_specs=in_specs,
        out_specs=jax.tree.map(lambda _: whole(), out_shape),
        compiler_params=pltpu.CompilerParams(vmem_limit_bytes=SMALL_VMEM),
        name=name,
    )


def halves_kernel(section, prompt, *parts):
    half, cols = parts[0].shape[1:]
    rows = pl.ds(pl.multiple_of(section[0] * half, half), half)
    for chunk, part in enumerate(parts):
        part[...] = prompt[0, :, rows, chunk * cols : (chunk + 1) * cols]


def sends_kernel(place, own, before, *sends):
    for offset, send in enumerate(sends, 1):

        @pl.when(place[0] + offset >= ROW)
        def _(send=send):
            send[...] = before[...]

        @pl.when(place[0] + offset < ROW)
        def _(send=send):
            send[...] = own[...]


def pick_kernel(first, second, *refs):
    choices, chosen = refs[:WIN], refs[WIN:]
    for which, target in zip((first, second), chosen):
        for offset, choice in enumerate(choices):

            @pl.when(which[0] == offset)
            def _(choice=choice, target=target):
                target[...] = choice[...]


def pack_kernel(meta, queries, grad_out, keys, values, *packs):
    tp_count = len(packs)
    for d, pack in enumerate(packs):
        device, at = lax.rem(meta[TP] + d, tp_count), 0
        for chunk in range(CHUNKS):
            for source in (queries, grad_out, keys, values):
                cols = source.shape[1] // tp_count
                part = cols // CHUNKS
                start = pl.multiple_of(device * cols + chunk * part, 128)
                pack[:, at : at + part] = source[:, pl.ds(start, part)]
                at += part


def unpack_kernel(tp, *refs):
    packs, (grad_q, grad_k, grad_v) = refs[:-3], refs[-3:]
    tp_count = len(packs)
    q_cols = grad_q.shape[1] // tp_count
    k_cols = grad_k.shape[1] // tp_count
    q_part, k_part = q_cols // CHUNKS, k_cols // CHUNKS
    for d, pack in enumerate(packs):
        device, at = lax.rem(tp[0] + d, tp_count), 0
        for chunk in range(CHUNKS):
            q_at = pl.ds(pl.multiple_of(device * q_cols + chunk * q_part, 128), q_part)
            k_at = pl.ds(pl.multiple_of(device * k_cols + chunk * k_part, 128), k_part)
            grad_q[:, q_at] = pack[:, at : at + q_part]
            at += q_part
            grad_k[:, k_at] = pack[:, at : at + k_part]
            at += k_part
            grad_v[:, k_at] = pack[:, at : at + k_part]
            at += k_part


def finish_kernel(*refs):
    shares, total = refs[:-1], refs[-1]
    cols = shares[0].shape[2]
    for chunk in range(CHUNKS):
        kept, came = shares[2 * chunk : 2 * chunk + 2]
        whole_sum = kept[...] + came[...].astype(jnp.float32)
        total[0, :, :, chunk * cols : (chunk + 1) * cols] = whole_sum.astype(jnp.bfloat16)


def place(index, tp, tp_count, rows):
    block = index // rows
    return lax.rem(tp - block + tp_count, tp_count) * rows + lax.rem(index, rows)


def attend_kernel(chunk, tp_count, meta, *refs):
    packs, refs = refs[:tp_count], refs[tp_count:]
    earlier, refs = refs[: tp_count if chunk else 0], refs[tp_count if chunk else 0 :]
    (own, other), refs = refs[:2], refs[2:]
    backs, refs = refs[:tp_count], refs[tp_count:]
    own_grad, other_grad = refs[:2]
    q_all, do_all, keys, values, keys_t, bias, scores, grad_prob, weights, grad_scores, dk, dv = refs[
        2:
    ]
    rows = packs[0].shape[0]
    resp = rows * tp_count
    half, k_cols = other.shape[1:]
    kv_heads = k_cols // HEAD_DIM
    prompt_len = 2 * half
    total = prompt_len + resp
    per_half = half // PTILE
    q_cols = kv_heads * PER_KV * HEAD_DIM
    tp, section, length = meta[TP], meta[SECTION], meta[LENGTH]
    taken = chunk * 2 * (q_cols + k_cols)
    given = chunk * (q_cols + 2 * k_cols)
    for back, block in zip(backs, earlier):
        back[:, :given] = block[...]

    key_at = place(lax.broadcasted_iota(jnp.int32, (resp, resp), 0), tp, tp_count, rows)
    row_at = place(lax.broadcasted_iota(jnp.int32, (resp, resp), 1), tp, tp_count, rows)
    bias[...] = jnp.where(key_at <= row_at, 0.0, MASKED)
    live = (
        place(lax.broadcasted_iota(jnp.int32, (1, resp), 1), tp, tp_count, rows) < length
    ).astype(jnp.float32)
    tile_bias = []
    for tile in range(2 * per_half):
        side = section if tile < per_half else 1 - section
        visible = meta[VISIBLE + side * per_half + tile % per_half]
        tile_bias.append(jnp.where(visible == 1, 0.0, MASKED))

    nt = (((1,), (1,)), ((), ()))
    for kv in range(kv_heads):
        at = slice(kv * HEAD_DIM, (kv + 1) * HEAD_DIM)
        keys[:half] = own[0, :, at]
        values[:half] = own[1, :, at]
        keys[half:prompt_len] = other[0, :, at]
        values[half:prompt_len] = other[1, :, at]
        for i in range(tp_count):
            here = slice(i * rows, (i + 1) * rows)
            there = slice(prompt_len + i * rows, prompt_len + (i + 1) * rows)
            k_from = taken + 2 * q_cols + kv * HEAD_DIM
            keys[there] = packs[i][:, k_from : k_from + HEAD_DIM]
            values[there] = packs[i][:, k_from + k_cols : k_from + k_cols + HEAD_DIM]
            for head in range(PER_KV):
                q_from = taken + (kv * PER_KV + head) * HEAD_DIM
                q_all[head, here] = packs[i][:, q_from : q_from + HEAD_DIM]
                do_all[head, here] = packs[i][:, q_cols + q_from : q_cols + q_from + HEAD_DIM]
        keys_t[...] = keys[...].T

        def products(head, tile):
            span = slice(tile * PTILE, (tile + 1) * PTILE)
            part = lax.dot_general(
                keys[span], q_all[head], nt, preferred_element_type=jnp.float32
            )
            if tile >= 2 * per_half:
                low = tile * PTILE - prompt_len
                part = part + bias[low : low + PTILE]
            scores[head % 2, span] = part
            grad_prob[head % 2, span] = lax.dot_general(
                values[span], do_all[head], nt, preferred_element_type=jnp.float32
            )
            top = jnp.max(part.reshape(PTILE // 8, 8, resp), axis=0)
            return top + tile_bias[tile] if tile < 2 * per_half else top

        tiles = total // PTILE
        tops = [products(0, tile) for tile in range(tiles)]
        for head in range(PER_KV):
            buf = head % 2
            largest = jnp.max(functools.reduce(jnp.maximum, tops), axis=0, keepdims=True)
            sums, dots, tops = [], [], []
            for tile in range(tiles):
                span = slice(tile * PTILE, (tile + 1) * PTILE)
                shift = largest - tile_bias[tile] if tile < 2 * per_half else largest
                exponent = jnp.exp2((scores[buf, span] - shift) * (SCALING * LOG2E))
                scores[buf, span] = exponent
                sums.append(jnp.sum(exponent.reshape(PTILE // 8, 8, resp), axis=0))
                weighed = exponent * grad_prob[buf, span]
                dots.append(jnp.sum(weighed.reshape(PTILE // 8, 8, resp), axis=0))
                if head + 1 < PER_KV:
                    tops.append(products(head + 1, tile))
            inverse = 1.0 / jnp.sum(functools.reduce(jnp.add, sums), axis=0, keepdims=True)
            row_delta = (
                jnp.sum(functools.reduce(jnp.add, dots), axis=0, keepdims=True) * inverse
            )
            inverse = inverse * live
            for tile in range(tiles):
                span = slice(tile * PTILE, (tile + 1) * PTILE)
                probabilities = scores[buf, span] * inverse
                weights[buf, span] = probabilities.astype(jnp.bfloat16)
                grad_scores[buf, span] = (
                    probabilities * (grad_prob[buf, span] - row_delta)
                ).astype(jnp.bfloat16)
            for target, left, right in (
                (dv, weights, do_all),
                (dk, grad_scores, q_all),
            ):
                product = jnp.dot(left[buf], right[head], preferred_element_type=jnp.float32)
                target[...] = product if head == 0 else target[...] + product
            grad_query_t = jnp.dot(
                keys_t[...], grad_scores[buf], preferred_element_type=jnp.float32
            )
            grad_query = (grad_query_t.T * SCALING).astype(jnp.bfloat16)
            q_from = given + (kv * PER_KV + head) * HEAD_DIM
            for i in range(tp_count):
                backs[i][:, q_from : q_from + HEAD_DIM] = grad_query[i * rows : (i + 1) * rows]

        own_grad[0, :, at] = (dk[:half] * SCALING).astype(jnp.bfloat16)
        other_grad[0, :, at] = (dk[half:prompt_len] * SCALING).astype(jnp.bfloat16)
        own_grad[1, :, at] = dv[:half].astype(jnp.bfloat16)
        other_grad[1, :, at] = dv[half:prompt_len].astype(jnp.bfloat16)
        for i in range(tp_count):
            k_from = given + q_cols + kv * HEAD_DIM
            v_from = k_from + k_cols
            span = slice(prompt_len + i * rows, prompt_len + (i + 1) * rows)
            backs[i][:, k_from : k_from + HEAD_DIM] = (dk[span] * SCALING).astype(jnp.bfloat16)
            backs[i][:, v_from : v_from + HEAD_DIM] = dv[span].astype(jnp.bfloat16)


def attend(chunk, meta, packs, earlier, own, other):
    tp_count, rows = len(packs), packs[0].shape[0]
    resp = rows * tp_count
    half, k_cols = other.shape[1:]
    kv_heads = k_cols // HEAD_DIM
    q_cols = kv_heads * PER_KV * HEAD_DIM
    total = 2 * half + resp
    f32, bf16 = jnp.float32, jnp.bfloat16
    flops = 10 * resp * total * kv_heads * PER_KV * HEAD_DIM
    results = pl.pallas_call(
        functools.partial(attend_kernel, chunk, tp_count),
        out_shape=[
            jax.ShapeDtypeStruct((rows, (chunk + 1) * (q_cols + 2 * k_cols)), bf16)
        ]
        * tp_count
        + [jax.ShapeDtypeStruct(other.shape, bf16)] * 2,
        in_specs=[scalars()] + [whole()] * (tp_count + len(earlier) + 2),
        out_specs=[whole()] * (tp_count + 2),
        scratch_shapes=[
            pltpu.VMEM((PER_KV, resp, HEAD_DIM), bf16),
            pltpu.VMEM((PER_KV, resp, HEAD_DIM), bf16),
            pltpu.VMEM((total, HEAD_DIM), bf16),
            pltpu.VMEM((total, HEAD_DIM), bf16),
            pltpu.VMEM((HEAD_DIM, total), bf16),
            pltpu.VMEM((resp, resp), f32),
            pltpu.VMEM((2, total, resp), f32),
            pltpu.VMEM((2, total, resp), f32),
            pltpu.VMEM((2, total, resp), bf16),
            pltpu.VMEM((2, total, resp), bf16),
            pltpu.VMEM((total, HEAD_DIM), f32),
            pltpu.VMEM((total, HEAD_DIM), f32),
        ],
        compiler_params=pltpu.CompilerParams(vmem_limit_bytes=ATTEND_VMEM),
        cost_estimate=pl.CostEstimate(
            flops=8 * flops, bytes_accessed=6 * 1024 * 1024, transcendentals=flops // 1280
        ),
        name="attend",
    )(meta, *packs, *earlier, own, other)
    return results[:tp_count], results[tp_count], results[tp_count + 1]


def shards(
    resp_queries, resp_keys, resp_values, resp_dout, prompt_kv, lengths, owners, visible_tiles
):
    tp_count = lax.axis_size("tp")
    tp = lax.axis_index("tp").astype(jnp.int32)[None]
    section = lax.axis_index("section").astype(jnp.int32)[None]
    at_row = lax.rem(lax.axis_index("group").astype(jnp.int32), ROW)
    rows = resp_queries.shape[0]
    half = prompt_kv.shape[2] // 2
    k_part = prompt_kv.shape[3] // CHUNKS
    pack_cols = 2 * (resp_queries.shape[1] + resp_keys.shape[1]) // tp_count
    bf16, f32 = jnp.bfloat16, jnp.float32
    part = jax.ShapeDtypeStruct((2, half, k_part), bf16)

    halves = small_call(
        halves_kernel,
        "halves",
        [part] * CHUNKS,
        [scalars(), whole()],
    )(section, prompt_kv)
    sibling_owner = shifted(after(owners, halves), "section", 1)
    meta = jnp.concatenate([tp, section, lengths, visible_tiles[0]])
    meta = after(meta, sibling_owner)
    packs = small_call(
        pack_kernel,
        "pack",
        [jax.ShapeDtypeStruct((rows, pack_cols), bf16)] * tp_count,
        [scalars()] + [whole()] * 4,
    )(meta, resp_queries, resp_dout, resp_keys, resp_values)
    arrived = {d: shifted(packs[d], "tp", d) for d in range(1, tp_count, 2)}
    for d in range(2, tp_count, 2):
        arrived[d] = shifted(after(packs[d], arrived), "tp", d)
    arrived = [packs[0]] + [arrived[d] for d in range(1, tp_count)]

    before = [to_row(block, 1) for block in halves]
    sends = [
        [jnp.where(at_row + offset >= ROW, before[c], halves[c]) for offset in range(1, WIN)]
        for c in range(CHUNKS)
    ]
    sends[0] = list(lax.optimization_barrier(after(sends[0], packs)))
    offers = []
    for c in range(CHUNKS):
        offer = {0: halves[c]}
        for offset in (1, 3, 2):
            send = sends[c][offset - 1]
            if c:
                send = after(send, offers[c - 1][offset])
            offer[offset] = along_row(send, offset)
        offers.append([offer[offset] for offset in range(WIN)])

    backs, shares, passing, ringed, terms = [], [], [], {}, []
    for c in range(CHUNKS):
        wanted, own = small_call(
            pick_kernel, "pick", [part] * 2, [scalars()] * 2 + [whole()] * WIN
        )(sibling_owner, owners, *offers[c])
        other = after(shifted(wanted, "section", 1), terms)
        backs, own_grad, other_grad = attend(c, meta, arrived, backs, own, other)
        if c == CHUNKS - 1:
            returned = {1: shifted(backs[1], "tp", -1)}
            for d in range(2, tp_count):
                first = after(backs[d], returned[1] if d > 2 else shares[1])
                returned[d] = shifted(first, "tp", -d)
        sibling_grad = after(shifted(other_grad, "section", 1), passing)
        terms = []
        for offset in range(WIN):
            term = jnp.where(owners[0] == offset, own_grad.astype(f32), 0.0) + jnp.where(
                sibling_owner[0] == offset, sibling_grad.astype(f32), 0.0
            )
            terms.append(term if offset == 0 else term.astype(bf16))
        terms = lax.optimization_barrier(terms)
        for offset in (1, 3, 2):
            term = after(terms[offset], ringed[offset]) if c else terms[offset]
            ringed[offset] = along_row(term, -offset)
        kept, passed = terms[0], jnp.zeros(part.shape, f32)
        for offset in range(1, WIN):
            term = ringed[offset].astype(f32)
            crossing = at_row + offset >= ROW
            kept = kept + jnp.where(crossing, 0.0, term)
            passed = passed + jnp.where(crossing, term, 0.0)
        passed = passed.astype(bf16)
        if c == CHUNKS - 1:
            passed = after(passed, (returned[1], returned[2]))
        passing.append(passed)
        shares += [kept, to_row(passed, -1)]

    prompt_grads = small_call(
        finish_kernel,
        "finish",
        jax.ShapeDtypeStruct((1, 2, half, prompt_kv.shape[3]), bf16),
        [whole()] * len(shares),
    )(*shares)
    grads = small_call(
        unpack_kernel,
        "unpack",
        [
            jax.ShapeDtypeStruct(resp_queries.shape, bf16),
            jax.ShapeDtypeStruct(resp_keys.shape, bf16),
            jax.ShapeDtypeStruct(resp_values.shape, bf16),
        ],
        [scalars()] + [whole()] * tp_count,
    )(tp, backs[0], *[returned[d] for d in range(1, tp_count)])
    return (grads[0], grads[1], grads[2], prompt_grads)


def solution(mesh):
    placed = (
        P(("section", "group", "tp"), None),
        P(("section", "group", "tp"), None),
        P(("section", "group", "tp"), None),
        P(("section", "group", "tp"), None),
        P("group", None, None, "tp"),
        P(("section", "group")),
        P(("section", "group")),
        P(("section", "group"), None),
    )
    return jax.shard_map(
        shards,
        mesh=mesh,
        in_specs=placed,
        out_specs=(
            P(("section", "group", "tp"), None),
            P(("section", "group", "tp"), None),
            P(("section", "group", "tp"), None),
            P("group", None, "section", "tp"),
        ),
        check_vma=False,
    )
```

```python
import functools

import jax
import jax.numpy as jnp
from jax import lax
from jax.experimental import pallas as pl
from jax.experimental.pallas import tpu as pltpu
from jax.sharding import PartitionSpec as P

HEADS = 40
KV_HEADS = 8
HEAD_DIM = 128
PTILE = 128
WIN = 4
PER_KV = HEADS // KV_HEADS
CHUNKS = 2
ROW = 4

MASKED = -1e30
SCALING = HEAD_DIM ** (-0.5)
LOG2E = 1.4426950408889634
ATTEND_VMEM = 24 * 1024 * 1024
SMALL_VMEM = 8 * 1024 * 1024

TP, SECTION, LENGTH, VISIBLE = 0, 1, 2, 3


def shifted(block, axis, distance):
    devices = range(lax.axis_size(axis))
    route = [((i - distance) % len(devices), i) for i in devices]
    return lax.ppermute(block, axis, route)


def after(block, earlier):
    return lax.optimization_barrier((block, earlier))[0]


def along_row(block, distance):
    count = lax.axis_size("group")
    route = [(i - i % ROW + (i - distance) % ROW, i) for i in range(count)]
    return lax.ppermute(block, "group", route)


def to_row(block, distance):
    return shifted(block, "group", distance * ROW)


def whole():
    return pl.BlockSpec(memory_space=pltpu.VMEM)


def scalars():
    return pl.BlockSpec(memory_space=pltpu.SMEM)


def small_call(kernel, name, out_shape, in_specs):
    return pl.pallas_call(
        kernel,
        out_shape=out_shape,
        in_specs=in_specs,
        out_specs=jax.tree.map(lambda _: whole(), out_shape),
        compiler_params=pltpu.CompilerParams(vmem_limit_bytes=SMALL_VMEM),
        name=name,
    )


def halves_kernel(section, prompt, *parts):
    half, cols = parts[0].shape[1:]
    rows = pl.ds(pl.multiple_of(section[0] * half, half), half)
    for chunk, part in enumerate(parts):
        part[...] = prompt[0, :, rows, chunk * cols : (chunk + 1) * cols]


def sends_kernel(place, own, before, *sends):
    for offset, send in enumerate(sends, 1):

        @pl.when(place[0] + offset >= ROW)
        def _(send=send):
            send[...] = before[...]

        @pl.when(place[0] + offset < ROW)
        def _(send=send):
            send[...] = own[...]


def pick_kernel(first, second, *refs):
    choices, chosen = refs[:WIN], refs[WIN:]
    for which, target in zip((first, second), chosen):
        for offset, choice in enumerate(choices):

            @pl.when(which[0] == offset)
            def _(choice=choice, target=target):
                target[...] = choice[...]


def pack_kernel(meta, queries, grad_out, keys, values, *packs):
    tp_count = len(packs)
    for d, pack in enumerate(packs):
        device, at = lax.rem(meta[TP] + d, tp_count), 0
        for chunk in range(CHUNKS):
            for source in (queries, grad_out, keys, values):
                cols = source.shape[1] // tp_count
                part = cols // CHUNKS
                start = pl.multiple_of(device * cols + chunk * part, 128)
                pack[:, at : at + part] = source[:, pl.ds(start, part)]
                at += part


def unpack_kernel(tp, *refs):
    packs, (grad_q, grad_k, grad_v) = refs[:-3], refs[-3:]
    tp_count = len(packs)
    q_cols = grad_q.shape[1] // tp_count
    k_cols = grad_k.shape[1] // tp_count
    q_part, k_part = q_cols // CHUNKS, k_cols // CHUNKS
    for d, pack in enumerate(packs):
        device, at = lax.rem(tp[0] + d, tp_count), 0
        for chunk in range(CHUNKS):
            q_at = pl.ds(pl.multiple_of(device * q_cols + chunk * q_part, 128), q_part)
            k_at = pl.ds(pl.multiple_of(device * k_cols + chunk * k_part, 128), k_part)
            grad_q[:, q_at] = pack[:, at : at + q_part]
            at += q_part
            grad_k[:, k_at] = pack[:, at : at + k_part]
            at += k_part
            grad_v[:, k_at] = pack[:, at : at + k_part]
            at += k_part


def finish_kernel(*refs):
    shares, total = refs[:-1], refs[-1]
    cols = shares[0].shape[2]
    for chunk in range(CHUNKS):
        kept, came = shares[2 * chunk : 2 * chunk + 2]
        whole_sum = kept[...] + came[...].astype(jnp.float32)
        total[0, :, :, chunk * cols : (chunk + 1) * cols] = whole_sum.astype(jnp.bfloat16)


def place(index, tp, tp_count, rows):
    block = index // rows
    return lax.rem(tp - block + tp_count, tp_count) * rows + lax.rem(index, rows)


def attend_kernel(chunk, tp_count, meta, *refs):
    packs, refs = refs[:tp_count], refs[tp_count:]
    earlier, refs = refs[: tp_count if chunk else 0], refs[tp_count if chunk else 0 :]
    (own, other), refs = refs[:2], refs[2:]
    backs, refs = refs[:tp_count], refs[tp_count:]
    own_grad, other_grad = refs[:2]
    q_all, do_all, keys, values, keys_t, bias, scores, grad_prob, weights, grad_scores, dk, dv = refs[
        2:
    ]
    rows = packs[0].shape[0]
    resp = rows * tp_count
    half, k_cols = other.shape[1:]
    kv_heads = k_cols // HEAD_DIM
    prompt_len = 2 * half
    total = prompt_len + resp
    per_half = half // PTILE
    q_cols = kv_heads * PER_KV * HEAD_DIM
    tp, section, length = meta[TP], meta[SECTION], meta[LENGTH]
    taken = chunk * 2 * (q_cols + k_cols)
    given = chunk * (q_cols + 2 * k_cols)
    for back, block in zip(backs, earlier):
        back[:, :given] = block[...]

    key_at = place(lax.broadcasted_iota(jnp.int32, (resp, resp), 0), tp, tp_count, rows)
    row_at = place(lax.broadcasted_iota(jnp.int32, (resp, resp), 1), tp, tp_count, rows)
    bias[...] = jnp.where(key_at <= row_at, 0.0, MASKED)
    live = (
        place(lax.broadcasted_iota(jnp.int32, (1, resp), 1), tp, tp_count, rows) < length
    ).astype(jnp.float32)
    tile_bias = []
    for tile in range(2 * per_half):
        side = section if tile < per_half else 1 - section
        visible = meta[VISIBLE + side * per_half + tile % per_half]
        tile_bias.append(jnp.where(visible == 1, 0.0, MASKED))

    nt = (((1,), (1,)), ((), ()))
    for kv in range(kv_heads):
        at = slice(kv * HEAD_DIM, (kv + 1) * HEAD_DIM)
        keys[:half] = own[0, :, at]
        values[:half] = own[1, :, at]
        keys[half:prompt_len] = other[0, :, at]
        values[half:prompt_len] = other[1, :, at]
        for i in range(tp_count):
            here = slice(i * rows, (i + 1) * rows)
            there = slice(prompt_len + i * rows, prompt_len + (i + 1) * rows)
            k_from = taken + 2 * q_cols + kv * HEAD_DIM
            keys[there] = packs[i][:, k_from : k_from + HEAD_DIM]
            values[there] = packs[i][:, k_from + k_cols : k_from + k_cols + HEAD_DIM]
            for head in range(PER_KV):
                q_from = taken + (kv * PER_KV + head) * HEAD_DIM
                q_all[head, here] = packs[i][:, q_from : q_from + HEAD_DIM]
                do_all[head, here] = packs[i][:, q_cols + q_from : q_cols + q_from + HEAD_DIM]
        keys_t[...] = keys[...].T

        def products(head, tile):
            span = slice(tile * PTILE, (tile + 1) * PTILE)
            part = lax.dot_general(
                keys[span], q_all[head], nt, preferred_element_type=jnp.float32
            )
            if tile >= 2 * per_half:
                low = tile * PTILE - prompt_len
                part = part + bias[low : low + PTILE]
            scores[head % 2, span] = part
            grad_prob[head % 2, span] = lax.dot_general(
                values[span], do_all[head], nt, preferred_element_type=jnp.float32
            )
            top = jnp.max(part.reshape(PTILE // 8, 8, resp), axis=0)
            return top + tile_bias[tile] if tile < 2 * per_half else top

        tiles = total // PTILE
        tops = [products(0, tile) for tile in range(tiles)]
        for head in range(PER_KV):
            buf = head % 2
            largest = jnp.max(functools.reduce(jnp.maximum, tops), axis=0, keepdims=True)
            sums, dots, tops = [], [], []
            for tile in range(tiles):
                span = slice(tile * PTILE, (tile + 1) * PTILE)
                shift = largest - tile_bias[tile] if tile < 2 * per_half else largest
                exponent = jnp.exp2((scores[buf, span] - shift) * (SCALING * LOG2E))
                scores[buf, span] = exponent
                sums.append(jnp.sum(exponent.reshape(PTILE // 8, 8, resp), axis=0))
                weighed = exponent * grad_prob[buf, span]
                dots.append(jnp.sum(weighed.reshape(PTILE // 8, 8, resp), axis=0))
                if head + 1 < PER_KV:
                    tops.append(products(head + 1, tile))
            inverse = 1.0 / jnp.sum(functools.reduce(jnp.add, sums), axis=0, keepdims=True)
            row_delta = (
                jnp.sum(functools.reduce(jnp.add, dots), axis=0, keepdims=True) * inverse
            )
            inverse = inverse * live
            for tile in range(tiles):
                span = slice(tile * PTILE, (tile + 1) * PTILE)
                probabilities = scores[buf, span] * inverse
                weights[buf, span] = probabilities.astype(jnp.bfloat16)
                grad_scores[buf, span] = (
                    probabilities * (grad_prob[buf, span] - row_delta)
                ).astype(jnp.bfloat16)
            for target, left, right in (
                (dv, weights, do_all),
                (dk, grad_scores, q_all),
            ):
                product = jnp.dot(left[buf], right[head], preferred_element_type=jnp.float32)
                target[...] = product if head == 0 else target[...] + product
            grad_query_t = jnp.dot(
                keys_t[...], grad_scores[buf], preferred_element_type=jnp.float32
            )
            grad_query = (grad_query_t.T * SCALING).astype(jnp.bfloat16)
            q_from = given + (kv * PER_KV + head) * HEAD_DIM
            for i in range(tp_count):
                backs[i][:, q_from : q_from + HEAD_DIM] = grad_query[i * rows : (i + 1) * rows]

        own_grad[0, :, at] = (dk[:half] * SCALING).astype(jnp.bfloat16)
        other_grad[0, :, at] = (dk[half:prompt_len] * SCALING).astype(jnp.bfloat16)
        own_grad[1, :, at] = dv[:half].astype(jnp.bfloat16)
        other_grad[1, :, at] = dv[half:prompt_len].astype(jnp.bfloat16)
        for i in range(tp_count):
            k_from = given + q_cols + kv * HEAD_DIM
            v_from = k_from + k_cols
            span = slice(prompt_len + i * rows, prompt_len + (i + 1) * rows)
            backs[i][:, k_from : k_from + HEAD_DIM] = (dk[span] * SCALING).astype(jnp.bfloat16)
            backs[i][:, v_from : v_from + HEAD_DIM] = dv[span].astype(jnp.bfloat16)


def attend(chunk, meta, packs, earlier, own, other):
    tp_count, rows = len(packs), packs[0].shape[0]
    resp = rows * tp_count
    half, k_cols = other.shape[1:]
    kv_heads = k_cols // HEAD_DIM
    q_cols = kv_heads * PER_KV * HEAD_DIM
    total = 2 * half + resp
    f32, bf16 = jnp.float32, jnp.bfloat16
    flops = 10 * resp * total * kv_heads * PER_KV * HEAD_DIM
    results = pl.pallas_call(
        functools.partial(attend_kernel, chunk, tp_count),
        out_shape=[
            jax.ShapeDtypeStruct((rows, (chunk + 1) * (q_cols + 2 * k_cols)), bf16)
        ]
        * tp_count
        + [jax.ShapeDtypeStruct(other.shape, bf16)] * 2,
        in_specs=[scalars()] + [whole()] * (tp_count + len(earlier) + 2),
        out_specs=[whole()] * (tp_count + 2),
        scratch_shapes=[
            pltpu.VMEM((PER_KV, resp, HEAD_DIM), bf16),
            pltpu.VMEM((PER_KV, resp, HEAD_DIM), bf16),
            pltpu.VMEM((total, HEAD_DIM), bf16),
            pltpu.VMEM((total, HEAD_DIM), bf16),
            pltpu.VMEM((HEAD_DIM, total), bf16),
            pltpu.VMEM((resp, resp), f32),
            pltpu.VMEM((2, total, resp), f32),
            pltpu.VMEM((2, total, resp), f32),
            pltpu.VMEM((2, total, resp), bf16),
            pltpu.VMEM((2, total, resp), bf16),
            pltpu.VMEM((total, HEAD_DIM), f32),
            pltpu.VMEM((total, HEAD_DIM), f32),
        ],
        compiler_params=pltpu.CompilerParams(vmem_limit_bytes=ATTEND_VMEM),
        cost_estimate=pl.CostEstimate(
            flops=8 * flops, bytes_accessed=6 * 1024 * 1024, transcendentals=flops // 1280
        ),
        name="attend",
    )(meta, *packs, *earlier, own, other)
    return results[:tp_count], results[tp_count], results[tp_count + 1]


def shards(
    resp_queries, resp_keys, resp_values, resp_dout, prompt_kv, lengths, owners, visible_tiles
):
    tp_count = lax.axis_size("tp")
    tp = lax.axis_index("tp").astype(jnp.int32)[None]
    section = lax.axis_index("section").astype(jnp.int32)[None]
    at_row = lax.rem(lax.axis_index("group").astype(jnp.int32), ROW)
    rows = resp_queries.shape[0]
    half = prompt_kv.shape[2] // 2
    k_part = prompt_kv.shape[3] // CHUNKS
    pack_cols = 2 * (resp_queries.shape[1] + resp_keys.shape[1]) // tp_count
    bf16, f32 = jnp.bfloat16, jnp.float32
    part = jax.ShapeDtypeStruct((2, half, k_part), bf16)

    halves = small_call(
        halves_kernel,
        "halves",
        [part] * CHUNKS,
        [scalars(), whole()],
    )(section, prompt_kv)
    sibling_owner = shifted(after(owners, halves), "section", 1)
    meta = jnp.concatenate([tp, section, lengths, visible_tiles[0]])
    meta = after(meta, sibling_owner)
    packs = small_call(
        pack_kernel,
        "pack",
        [jax.ShapeDtypeStruct((rows, pack_cols), bf16)] * tp_count,
        [scalars()] + [whole()] * 4,
    )(meta, resp_queries, resp_dout, resp_keys, resp_values)
    arrived = {d: shifted(packs[d], "tp", d) for d in range(1, tp_count, 2)}
    for d in range(2, tp_count, 2):
        arrived[d] = shifted(after(packs[d], arrived), "tp", d)
    arrived = [packs[0]] + [arrived[d] for d in range(1, tp_count)]

    before = [to_row(block, 1) for block in halves]
    sends = [
        [jnp.where(at_row + offset >= ROW, before[c], halves[c]) for offset in range(1, WIN)]
        for c in range(CHUNKS)
    ]
    sends[0] = list(lax.optimization_barrier(after(sends[0], packs)))
    offers = []
    for c in range(CHUNKS):
        offer = {0: halves[c]}
        for offset in (1, 3, 2):
            send = sends[c][offset - 1]
            if c:
                send = after(send, offers[c - 1][offset])
            offer[offset] = along_row(send, offset)
        offers.append([offer[offset] for offset in range(WIN)])

    backs, shares, passing, ringed, terms = [], [], [], {}, []
    for c in range(CHUNKS):
        wanted, own = small_call(
            pick_kernel, "pick", [part] * 2, [scalars()] * 2 + [whole()] * WIN
        )(sibling_owner, owners, *offers[c])
        other = after(shifted(wanted, "section", 1), terms)
        backs, own_grad, other_grad = attend(c, meta, arrived, backs, own, other)
        if c == CHUNKS - 1:
            returned = {1: shifted(backs[1], "tp", -1)}
            for d in range(2, tp_count):
                first = after(backs[d], returned[1] if d > 2 else shares[1])
                returned[d] = shifted(first, "tp", -d)
        sibling_grad = after(shifted(other_grad, "section", 1), passing)
        terms = []
        for offset in range(WIN):
            term = jnp.where(owners[0] == offset, own_grad.astype(f32), 0.0) + jnp.where(
                sibling_owner[0] == offset, sibling_grad.astype(f32), 0.0
            )
            terms.append(term if offset == 0 else term.astype(bf16))
        terms = lax.optimization_barrier(terms)
        for offset in (1, 3, 2):
            term = after(terms[offset], ringed[offset]) if c else terms[offset]
            ringed[offset] = along_row(term, -offset)
        kept, passed = terms[0], jnp.zeros(part.shape, f32)
        for offset in range(1, WIN):
            term = ringed[offset].astype(f32)
            crossing = at_row + offset >= ROW
            kept = kept + jnp.where(crossing, 0.0, term)
            passed = passed + jnp.where(crossing, term, 0.0)
        passed = passed.astype(bf16)
        if c == CHUNKS - 1:
            passed = after(passed, (returned[1], returned[2]))
        passing.append(passed)
        shares += [kept, to_row(passed, -1)]

    prompt_grads = small_call(
        finish_kernel,
        "finish",
        jax.ShapeDtypeStruct((1, 2, half, prompt_kv.shape[3]), bf16),
        [whole()] * len(shares),
    )(*shares)
    grads = small_call(
        unpack_kernel,
        "unpack",
        [
            jax.ShapeDtypeStruct(resp_queries.shape, bf16),
            jax.ShapeDtypeStruct(resp_keys.shape, bf16),
            jax.ShapeDtypeStruct(resp_values.shape, bf16),
        ],
        [scalars()] + [whole()] * tp_count,
    )(after(tp, prompt_grads), backs[0], *[returned[d] for d in range(1, tp_count)])
    return (grads[0], grads[1], grads[2], prompt_grads)


def solution(mesh):
    placed = (
        P(("section", "group", "tp"), None),
        P(("section", "group", "tp"), None),
        P(("section", "group", "tp"), None),
        P(("section", "group", "tp"), None),
        P("group", None, None, "tp"),
        P(("section", "group")),
        P(("section", "group")),
        P(("section", "group"), None),
    )
    return jax.shard_map(
        shards,
        mesh=mesh,
        in_specs=placed,
        out_specs=(
            P(("section", "group", "tp"), None),
            P(("section", "group", "tp"), None),
            P(("section", "group", "tp"), None),
            P("group", None, "section", "tp"),
        ),
        check_vma=False,
    )
```

```python
import functools

import jax
import jax.numpy as jnp
from jax import lax
from jax.experimental import pallas as pl
from jax.experimental.pallas import tpu as pltpu
from jax.sharding import PartitionSpec as P

HEADS = 40
KV_HEADS = 8
HEAD_DIM = 128
PTILE = 128
WIN = 4
PER_KV = HEADS // KV_HEADS
CHUNKS = 2
ROW = 4

MASKED = -1e30
SCALING = HEAD_DIM ** (-0.5)
LOG2E = 1.4426950408889634
ATTEND_VMEM = 24 * 1024 * 1024
SMALL_VMEM = 8 * 1024 * 1024

TP, SECTION, LENGTH, VISIBLE = 0, 1, 2, 3


def shifted(block, axis, distance):
    devices = range(lax.axis_size(axis))
    route = [((i - distance) % len(devices), i) for i in devices]
    return lax.ppermute(block, axis, route)


def after(block, earlier):
    return lax.optimization_barrier((block, earlier))[0]


def along_row(block, distance):
    count = lax.axis_size("group")
    route = [(i - i % ROW + (i - distance) % ROW, i) for i in range(count)]
    return lax.ppermute(block, "group", route)


def to_row(block, distance):
    return shifted(block, "group", distance * ROW)


def whole():
    return pl.BlockSpec(memory_space=pltpu.VMEM)


def scalars():
    return pl.BlockSpec(memory_space=pltpu.SMEM)


def small_call(kernel, name, out_shape, in_specs):
    return pl.pallas_call(
        kernel,
        out_shape=out_shape,
        in_specs=in_specs,
        out_specs=jax.tree.map(lambda _: whole(), out_shape),
        compiler_params=pltpu.CompilerParams(vmem_limit_bytes=SMALL_VMEM),
        name=name,
    )


def halves_kernel(section, prompt, *parts):
    half, cols = parts[0].shape[1:]
    rows = pl.ds(pl.multiple_of(section[0] * half, half), half)
    for chunk, part in enumerate(parts):
        part[...] = prompt[0, :, rows, chunk * cols : (chunk + 1) * cols]


def sends_kernel(place, own, before, *sends):
    for offset, send in enumerate(sends, 1):

        @pl.when(place[0] + offset >= ROW)
        def _(send=send):
            send[...] = before[...]

        @pl.when(place[0] + offset < ROW)
        def _(send=send):
            send[...] = own[...]


def pick_kernel(first, second, *refs):
    choices, chosen = refs[:WIN], refs[WIN:]
    for which, target in zip((first, second), chosen):
        for offset, choice in enumerate(choices):

            @pl.when(which[0] == offset)
            def _(choice=choice, target=target):
                target[...] = choice[...]


def pack_kernel(meta, queries, grad_out, keys, values, *packs):
    tp_count = len(packs)
    for d, pack in enumerate(packs):
        device, at = lax.rem(meta[TP] + d, tp_count), 0
        for chunk in range(CHUNKS):
            for source in (queries, grad_out, keys, values):
                cols = source.shape[1] // tp_count
                part = cols // CHUNKS
                start = pl.multiple_of(device * cols + chunk * part, 128)
                pack[:, at : at + part] = source[:, pl.ds(start, part)]
                at += part


def unpack_kernel(tp, *refs):
    packs, (grad_q, grad_k, grad_v) = refs[:-3], refs[-3:]
    tp_count = len(packs)
    q_cols = grad_q.shape[1] // tp_count
    k_cols = grad_k.shape[1] // tp_count
    q_part, k_part = q_cols // CHUNKS, k_cols // CHUNKS
    for d, pack in enumerate(packs):
        device, at = lax.rem(tp[0] + d, tp_count), 0
        for chunk in range(CHUNKS):
            q_at = pl.ds(pl.multiple_of(device * q_cols + chunk * q_part, 128), q_part)
            k_at = pl.ds(pl.multiple_of(device * k_cols + chunk * k_part, 128), k_part)
            grad_q[:, q_at] = pack[:, at : at + q_part]
            at += q_part
            grad_k[:, k_at] = pack[:, at : at + k_part]
            at += k_part
            grad_v[:, k_at] = pack[:, at : at + k_part]
            at += k_part


def finish_kernel(*refs):
    shares, total = refs[:-1], refs[-1]
    cols = shares[0].shape[2]
    for chunk in range(CHUNKS):
        kept, came = shares[2 * chunk : 2 * chunk + 2]
        whole_sum = kept[...] + came[...].astype(jnp.float32)
        total[0, :, :, chunk * cols : (chunk + 1) * cols] = whole_sum.astype(jnp.bfloat16)


def place(index, tp, tp_count, rows):
    block = index // rows
    return lax.rem(tp - block + tp_count, tp_count) * rows + lax.rem(index, rows)


def attend_kernel(chunk, tp_count, meta, *refs):
    packs, refs = refs[:tp_count], refs[tp_count:]
    earlier, refs = refs[: tp_count if chunk else 0], refs[tp_count if chunk else 0 :]
    (own, other), refs = refs[:2], refs[2:]
    backs, refs = refs[:tp_count], refs[tp_count:]
    own_grad, other_grad = refs[:2]
    q_all, do_all, keys, values, keys_t, bias, scores, grad_prob, weights, grad_scores, dk, dv = refs[
        2:
    ]
    rows = packs[0].shape[0]
    resp = rows * tp_count
    half, k_cols = other.shape[1:]
    kv_heads = k_cols // HEAD_DIM
    prompt_len = 2 * half
    total = prompt_len + resp
    per_half = half // PTILE
    q_cols = kv_heads * PER_KV * HEAD_DIM
    tp, section, length = meta[TP], meta[SECTION], meta[LENGTH]
    taken = chunk * 2 * (q_cols + k_cols)
    given = chunk * (q_cols + 2 * k_cols)
    for back, block in zip(backs, earlier):
        back[:, :given] = block[...]

    key_at = place(lax.broadcasted_iota(jnp.int32, (resp, resp), 0), tp, tp_count, rows)
    row_at = place(lax.broadcasted_iota(jnp.int32, (resp, resp), 1), tp, tp_count, rows)
    bias[...] = jnp.where(key_at <= row_at, 0.0, MASKED)
    live = (
        place(lax.broadcasted_iota(jnp.int32, (1, resp), 1), tp, tp_count, rows) < length
    ).astype(jnp.float32)
    tile_bias = []
    for tile in range(2 * per_half):
        side = section if tile < per_half else 1 - section
        visible = meta[VISIBLE + side * per_half + tile % per_half]
        tile_bias.append(jnp.where(visible == 1, 0.0, MASKED))

    nt = (((1,), (1,)), ((), ()))
    for kv in range(kv_heads):
        at = slice(kv * HEAD_DIM, (kv + 1) * HEAD_DIM)
        keys[:half] = own[0, :, at]
        values[:half] = own[1, :, at]
        keys[half:prompt_len] = other[0, :, at]
        values[half:prompt_len] = other[1, :, at]
        for i in range(tp_count):
            here = slice(i * rows, (i + 1) * rows)
            there = slice(prompt_len + i * rows, prompt_len + (i + 1) * rows)
            k_from = taken + 2 * q_cols + kv * HEAD_DIM
            keys[there] = packs[i][:, k_from : k_from + HEAD_DIM]
            values[there] = packs[i][:, k_from + k_cols : k_from + k_cols + HEAD_DIM]
            for head in range(PER_KV):
                q_from = taken + (kv * PER_KV + head) * HEAD_DIM
                q_all[head, here] = packs[i][:, q_from : q_from + HEAD_DIM]
                do_all[head, here] = packs[i][:, q_cols + q_from : q_cols + q_from + HEAD_DIM]
        keys_t[...] = keys[...].T

        def products(head, tile):
            span = slice(tile * PTILE, (tile + 1) * PTILE)
            part = lax.dot_general(
                keys[span], q_all[head], nt, preferred_element_type=jnp.float32
            )
            if tile >= 2 * per_half:
                low = tile * PTILE - prompt_len
                part = part + bias[low : low + PTILE]
            scores[head % 2, span] = part
            grad_prob[head % 2, span] = lax.dot_general(
                values[span], do_all[head], nt, preferred_element_type=jnp.float32
            )
            top = jnp.max(part.reshape(PTILE // 8, 8, resp), axis=0)
            return top + tile_bias[tile] if tile < 2 * per_half else top

        tiles = total // PTILE
        tops = [products(0, tile) for tile in range(tiles)]
        for head in range(PER_KV):
            buf = head % 2
            largest = jnp.max(functools.reduce(jnp.maximum, tops), axis=0, keepdims=True)
            sums, dots, tops = [], [], []
            for tile in range(tiles):
                span = slice(tile * PTILE, (tile + 1) * PTILE)
                shift = largest - tile_bias[tile] if tile < 2 * per_half else largest
                exponent = jnp.exp2((scores[buf, span] - shift) * (SCALING * LOG2E))
                scores[buf, span] = exponent
                sums.append(jnp.sum(exponent.reshape(PTILE // 8, 8, resp), axis=0))
                weighed = exponent * grad_prob[buf, span]
                dots.append(jnp.sum(weighed.reshape(PTILE // 8, 8, resp), axis=0))
                if head + 1 < PER_KV:
                    tops.append(products(head + 1, tile))
            inverse = 1.0 / jnp.sum(functools.reduce(jnp.add, sums), axis=0, keepdims=True)
            row_delta = (
                jnp.sum(functools.reduce(jnp.add, dots), axis=0, keepdims=True) * inverse
            )
            inverse = inverse * live
            for tile in range(tiles):
                span = slice(tile * PTILE, (tile + 1) * PTILE)
                probabilities = scores[buf, span] * inverse
                weights[buf, span] = probabilities.astype(jnp.bfloat16)
                grad_scores[buf, span] = (
                    probabilities * (grad_prob[buf, span] - row_delta)
                ).astype(jnp.bfloat16)
            for target, left, right in (
                (dv, weights, do_all),
                (dk, grad_scores, q_all),
            ):
                product = jnp.dot(left[buf], right[head], preferred_element_type=jnp.float32)
                target[...] = product if head == 0 else target[...] + product
            grad_query_t = jnp.dot(
                keys_t[...], grad_scores[buf], preferred_element_type=jnp.float32
            )
            grad_query = (grad_query_t.T * SCALING).astype(jnp.bfloat16)
            q_from = given + (kv * PER_KV + head) * HEAD_DIM
            for i in range(tp_count):
                backs[i][:, q_from : q_from + HEAD_DIM] = grad_query[i * rows : (i + 1) * rows]

        own_grad[0, :, at] = (dk[:half] * SCALING).astype(jnp.bfloat16)
        other_grad[0, :, at] = (dk[half:prompt_len] * SCALING).astype(jnp.bfloat16)
        own_grad[1, :, at] = dv[:half].astype(jnp.bfloat16)
        other_grad[1, :, at] = dv[half:prompt_len].astype(jnp.bfloat16)
        for i in range(tp_count):
            k_from = given + q_cols + kv * HEAD_DIM
            v_from = k_from + k_cols
            span = slice(prompt_len + i * rows, prompt_len + (i + 1) * rows)
            backs[i][:, k_from : k_from + HEAD_DIM] = (dk[span] * SCALING).astype(jnp.bfloat16)
            backs[i][:, v_from : v_from + HEAD_DIM] = dv[span].astype(jnp.bfloat16)


def attend(chunk, meta, packs, earlier, own, other):
    tp_count, rows = len(packs), packs[0].shape[0]
    resp = rows * tp_count
    half, k_cols = other.shape[1:]
    kv_heads = k_cols // HEAD_DIM
    q_cols = kv_heads * PER_KV * HEAD_DIM
    total = 2 * half + resp
    f32, bf16 = jnp.float32, jnp.bfloat16
    flops = 10 * resp * total * kv_heads * PER_KV * HEAD_DIM
    results = pl.pallas_call(
        functools.partial(attend_kernel, chunk, tp_count),
        out_shape=[
            jax.ShapeDtypeStruct((rows, (chunk + 1) * (q_cols + 2 * k_cols)), bf16)
        ]
        * tp_count
        + [jax.ShapeDtypeStruct(other.shape, bf16)] * 2,
        in_specs=[scalars()] + [whole()] * (tp_count + len(earlier) + 2),
        out_specs=[whole()] * (tp_count + 2),
        scratch_shapes=[
            pltpu.VMEM((PER_KV, resp, HEAD_DIM), bf16),
            pltpu.VMEM((PER_KV, resp, HEAD_DIM), bf16),
            pltpu.VMEM((total, HEAD_DIM), bf16),
            pltpu.VMEM((total, HEAD_DIM), bf16),
            pltpu.VMEM((HEAD_DIM, total), bf16),
            pltpu.VMEM((resp, resp), f32),
            pltpu.VMEM((2, total, resp), f32),
            pltpu.VMEM((2, total, resp), f32),
            pltpu.VMEM((2, total, resp), bf16),
            pltpu.VMEM((2, total, resp), bf16),
            pltpu.VMEM((total, HEAD_DIM), f32),
            pltpu.VMEM((total, HEAD_DIM), f32),
        ],
        compiler_params=pltpu.CompilerParams(vmem_limit_bytes=ATTEND_VMEM),
        cost_estimate=pl.CostEstimate(
            flops=8 * flops, bytes_accessed=6 * 1024 * 1024, transcendentals=flops // 1280
        ),
        name="attend",
    )(meta, *packs, *earlier, own, other)
    return results[:tp_count], results[tp_count], results[tp_count + 1]


def shards(
    resp_queries, resp_keys, resp_values, resp_dout, prompt_kv, lengths, owners, visible_tiles
):
    tp_count = lax.axis_size("tp")
    tp = lax.axis_index("tp").astype(jnp.int32)[None]
    section = lax.axis_index("section").astype(jnp.int32)[None]
    at_row = lax.rem(lax.axis_index("group").astype(jnp.int32), ROW)
    rows = resp_queries.shape[0]
    half = prompt_kv.shape[2] // 2
    k_part = prompt_kv.shape[3] // CHUNKS
    pack_cols = 2 * (resp_queries.shape[1] + resp_keys.shape[1]) // tp_count
    bf16, f32 = jnp.bfloat16, jnp.float32
    part = jax.ShapeDtypeStruct((2, half, k_part), bf16)

    halves = small_call(
        halves_kernel,
        "halves",
        [part] * CHUNKS,
        [scalars(), whole()],
    )(section, prompt_kv)
    sibling_owner = shifted(after(owners, halves), "section", 1)
    meta = jnp.concatenate([tp, section, lengths, visible_tiles[0]])
    meta = after(meta, sibling_owner)
    packs = small_call(
        pack_kernel,
        "pack",
        [jax.ShapeDtypeStruct((rows, pack_cols), bf16)] * tp_count,
        [scalars()] + [whole()] * 4,
    )(meta, resp_queries, resp_dout, resp_keys, resp_values)
    arrived = {d: shifted(packs[d], "tp", d) for d in range(1, tp_count, 2)}
    for d in range(2, tp_count, 2):
        arrived[d] = shifted(after(packs[d], arrived), "tp", d)
    arrived = [packs[0]] + [arrived[d] for d in range(1, tp_count)]

    before = [to_row(block, 1) for block in halves]
    sends = [
        [jnp.where(at_row + offset >= ROW, before[c], halves[c]) for offset in range(1, WIN)]
        for c in range(CHUNKS)
    ]
    sends[0] = list(lax.optimization_barrier(after(sends[0], packs)))
    offers = []
    for c in range(CHUNKS):
        offer = {0: halves[c]}
        for offset in (1, 3, 2):
            send = sends[c][offset - 1]
            if c:
                send = after(send, offers[c - 1][offset])
            offer[offset] = along_row(send, offset)
        offers.append([offer[offset] for offset in range(WIN)])

    backs, shares, passing, ringed, terms = [], [], [], {}, []
    for c in range(CHUNKS):
        wanted, own = small_call(
            pick_kernel, "pick", [part] * 2, [scalars()] * 2 + [whole()] * WIN
        )(sibling_owner, owners, *offers[c])
        other = after(shifted(wanted, "section", 1), terms)
        backs, own_grad, other_grad = attend(c, meta, arrived, backs, own, other)
        if c == CHUNKS - 1:
            returned = {d: shifted(backs[d], "tp", -d) for d in (1, 2)}
            shares[1] = to_row(after(shares[1], returned[1]), -1)
            for d in range(3, tp_count):
                returned[d] = shifted(after(backs[d], returned), "tp", -d)
        sibling_grad = after(shifted(other_grad, "section", 1), passing)
        terms = []
        for offset in range(WIN):
            term = jnp.where(owners[0] == offset, own_grad.astype(f32), 0.0) + jnp.where(
                sibling_owner[0] == offset, sibling_grad.astype(f32), 0.0
            )
            terms.append(term if offset == 0 else term.astype(bf16))
        terms = lax.optimization_barrier(terms)
        for offset in (1, 3, 2):
            term = after(terms[offset], ringed[offset]) if c else terms[offset]
            ringed[offset] = along_row(term, -offset)
        kept, passed = terms[0], jnp.zeros(part.shape, f32)
        for offset in range(1, WIN):
            term = ringed[offset].astype(f32)
            crossing = at_row + offset >= ROW
            kept = kept + jnp.where(crossing, 0.0, term)
            passed = passed + jnp.where(crossing, term, 0.0)
        passed = passed.astype(bf16)
        if c == CHUNKS - 1:
            passed = after(passed, (returned[1], returned[2]))
        passing.append(passed)
        shares += [kept, passed if c < CHUNKS - 1 else to_row(passed, -1)]

    prompt_grads = small_call(
        finish_kernel,
        "finish",
        jax.ShapeDtypeStruct((1, 2, half, prompt_kv.shape[3]), bf16),
        [whole()] * len(shares),
    )(*shares)
    grads = small_call(
        unpack_kernel,
        "unpack",
        [
            jax.ShapeDtypeStruct(resp_queries.shape, bf16),
            jax.ShapeDtypeStruct(resp_keys.shape, bf16),
            jax.ShapeDtypeStruct(resp_values.shape, bf16),
        ],
        [scalars()] + [whole()] * tp_count,
    )(after(tp, prompt_grads), backs[0], *[returned[d] for d in range(1, tp_count)])
    return (grads[0], grads[1], grads[2], prompt_grads)


def solution(mesh):
    placed = (
        P(("section", "group", "tp"), None),
        P(("section", "group", "tp"), None),
        P(("section", "group", "tp"), None),
        P(("section", "group", "tp"), None),
        P("group", None, None, "tp"),
        P(("section", "group")),
        P(("section", "group")),
        P(("section", "group"), None),
    )
    return jax.shard_map(
        shards,
        mesh=mesh,
        in_specs=placed,
        out_specs=(
            P(("section", "group", "tp"), None),
            P(("section", "group", "tp"), None),
            P(("section", "group", "tp"), None),
            P("group", None, "section", "tp"),
        ),
        check_vma=False,
    )
```

```python
import functools

import jax
import jax.numpy as jnp
from jax import lax
from jax.experimental import pallas as pl
from jax.experimental.pallas import tpu as pltpu
from jax.sharding import PartitionSpec as P

HEADS = 40
KV_HEADS = 8
HEAD_DIM = 128
PTILE = 128
WIN = 4
PER_KV = HEADS // KV_HEADS
CHUNKS = 2
ROW = 4

MASKED = -1e30
SCALING = HEAD_DIM ** (-0.5)
LOG2E = 1.4426950408889634
ATTEND_VMEM = 24 * 1024 * 1024
SMALL_VMEM = 8 * 1024 * 1024

TP, SECTION, LENGTH, VISIBLE = 0, 1, 2, 3


def shifted(block, axis, distance):
    devices = range(lax.axis_size(axis))
    route = [((i - distance) % len(devices), i) for i in devices]
    return lax.ppermute(block, axis, route)


def after(block, earlier):
    return lax.optimization_barrier((block, earlier))[0]


def along_row(block, distance):
    count = lax.axis_size("group")
    route = [(i - i % ROW + (i - distance) % ROW, i) for i in range(count)]
    return lax.ppermute(block, "group", route)


def to_row(block, distance):
    return shifted(block, "group", distance * ROW)


def whole():
    return pl.BlockSpec(memory_space=pltpu.VMEM)


def scalars():
    return pl.BlockSpec(memory_space=pltpu.SMEM)


def small_call(kernel, name, out_shape, in_specs):
    return pl.pallas_call(
        kernel,
        out_shape=out_shape,
        in_specs=in_specs,
        out_specs=jax.tree.map(lambda _: whole(), out_shape),
        compiler_params=pltpu.CompilerParams(vmem_limit_bytes=SMALL_VMEM),
        name=name,
    )


def halves_kernel(section, prompt, *parts):
    half, cols = parts[0].shape[1:]
    rows = pl.ds(pl.multiple_of(section[0] * half, half), half)
    for chunk, part in enumerate(parts):
        part[...] = prompt[0, :, rows, chunk * cols : (chunk + 1) * cols]


def sends_kernel(place, own, before, *sends):
    for offset, send in enumerate(sends, 1):

        @pl.when(place[0] + offset >= ROW)
        def _(send=send):
            send[...] = before[...]

        @pl.when(place[0] + offset < ROW)
        def _(send=send):
            send[...] = own[...]


def pick_kernel(first, second, *refs):
    choices, chosen = refs[:WIN], refs[WIN:]
    for which, target in zip((first, second), chosen):
        for offset, choice in enumerate(choices):

            @pl.when(which[0] == offset)
            def _(choice=choice, target=target):
                target[...] = choice[...]


def pack_kernel(meta, queries, grad_out, keys, values, *packs):
    tp_count = len(packs)
    for d, pack in enumerate(packs):
        device, at = lax.rem(meta[TP] + d, tp_count), 0
        for chunk in range(CHUNKS):
            for source in (queries, grad_out, keys, values):
                cols = source.shape[1] // tp_count
                part = cols // CHUNKS
                start = pl.multiple_of(device * cols + chunk * part, 128)
                pack[:, at : at + part] = source[:, pl.ds(start, part)]
                at += part


def unpack_kernel(tp, *refs):
    packs, (grad_q, grad_k, grad_v) = refs[:-3], refs[-3:]
    tp_count = len(packs)
    q_cols = grad_q.shape[1] // tp_count
    k_cols = grad_k.shape[1] // tp_count
    q_part, k_part = q_cols // CHUNKS, k_cols // CHUNKS
    for d, pack in enumerate(packs):
        device, at = lax.rem(tp[0] + d, tp_count), 0
        for chunk in range(CHUNKS):
            q_at = pl.ds(pl.multiple_of(device * q_cols + chunk * q_part, 128), q_part)
            k_at = pl.ds(pl.multiple_of(device * k_cols + chunk * k_part, 128), k_part)
            grad_q[:, q_at] = pack[:, at : at + q_part]
            at += q_part
            grad_k[:, k_at] = pack[:, at : at + k_part]
            at += k_part
            grad_v[:, k_at] = pack[:, at : at + k_part]
            at += k_part


def finish_kernel(*refs):
    shares, total = refs[:-1], refs[-1]
    cols = shares[0].shape[2]
    for chunk in range(CHUNKS):
        kept, came = shares[2 * chunk : 2 * chunk + 2]
        whole_sum = kept[...] + came[...].astype(jnp.float32)
        total[0, :, :, chunk * cols : (chunk + 1) * cols] = whole_sum.astype(jnp.bfloat16)


def place(index, tp, tp_count, rows):
    block = index // rows
    return lax.rem(tp - block + tp_count, tp_count) * rows + lax.rem(index, rows)


def attend_kernel(chunk, tp_count, meta, *refs):
    packs, refs = refs[:tp_count], refs[tp_count:]
    earlier, refs = refs[: tp_count if chunk else 0], refs[tp_count if chunk else 0 :]
    (own, other), refs = refs[:2], refs[2:]
    backs, refs = refs[:tp_count], refs[tp_count:]
    own_grad, other_grad = refs[:2]
    q_all, do_all, keys, values, keys_t, bias, scores, grad_prob, weights, grad_scores, dk, dv = refs[
        2:
    ]
    rows = packs[0].shape[0]
    resp = rows * tp_count
    half, k_cols = other.shape[1:]
    kv_heads = k_cols // HEAD_DIM
    prompt_len = 2 * half
    total = prompt_len + resp
    per_half = half // PTILE
    q_cols = kv_heads * PER_KV * HEAD_DIM
    tp, section, length = meta[TP], meta[SECTION], meta[LENGTH]
    taken = chunk * 2 * (q_cols + k_cols)
    given = chunk * (q_cols + 2 * k_cols)
    for back, block in zip(backs, earlier):
        back[:, :given] = block[...]

    key_at = place(lax.broadcasted_iota(jnp.int32, (resp, resp), 0), tp, tp_count, rows)
    row_at = place(lax.broadcasted_iota(jnp.int32, (resp, resp), 1), tp, tp_count, rows)
    bias[...] = jnp.where(key_at <= row_at, 0.0, MASKED)
    live = (
        place(lax.broadcasted_iota(jnp.int32, (1, resp), 1), tp, tp_count, rows) < length
    ).astype(jnp.float32)
    tile_bias = []
    for tile in range(2 * per_half):
        side = section if tile < per_half else 1 - section
        visible = meta[VISIBLE + side * per_half + tile % per_half]
        tile_bias.append(jnp.where(visible == 1, 0.0, MASKED))

    nt = (((1,), (1,)), ((), ()))
    for kv in range(kv_heads):
        at = slice(kv * HEAD_DIM, (kv + 1) * HEAD_DIM)
        keys[:half] = own[0, :, at]
        values[:half] = own[1, :, at]
        keys[half:prompt_len] = other[0, :, at]
        values[half:prompt_len] = other[1, :, at]
        for i in range(tp_count):
            here = slice(i * rows, (i + 1) * rows)
            there = slice(prompt_len + i * rows, prompt_len + (i + 1) * rows)
            k_from = taken + 2 * q_cols + kv * HEAD_DIM
            keys[there] = packs[i][:, k_from : k_from + HEAD_DIM]
            values[there] = packs[i][:, k_from + k_cols : k_from + k_cols + HEAD_DIM]
            for head in range(PER_KV):
                q_from = taken + (kv * PER_KV + head) * HEAD_DIM
                q_all[head, here] = packs[i][:, q_from : q_from + HEAD_DIM]
                do_all[head, here] = packs[i][:, q_cols + q_from : q_cols + q_from + HEAD_DIM]
        keys_t[...] = keys[...].T

        def products(head, tile):
            span = slice(tile * PTILE, (tile + 1) * PTILE)
            part = lax.dot_general(
                keys[span], q_all[head], nt, preferred_element_type=jnp.float32
            )
            if tile >= 2 * per_half:
                low = tile * PTILE - prompt_len
                part = part + bias[low : low + PTILE]
            scores[head % 2, span] = part
            grad_prob[head % 2, span] = lax.dot_general(
                values[span], do_all[head], nt, preferred_element_type=jnp.float32
            )
            top = jnp.max(part.reshape(PTILE // 8, 8, resp), axis=0)
            return top + tile_bias[tile] if tile < 2 * per_half else top

        tiles = total // PTILE
        tops = [products(0, tile) for tile in range(tiles)]
        for head in range(PER_KV):
            buf = head % 2
            largest = jnp.max(functools.reduce(jnp.maximum, tops), axis=0, keepdims=True)
            sums, dots, tops = [], [], []
            for tile in range(tiles):
                span = slice(tile * PTILE, (tile + 1) * PTILE)
                shift = largest - tile_bias[tile] if tile < 2 * per_half else largest
                exponent = jnp.exp2((scores[buf, span] - shift) * (SCALING * LOG2E))
                scores[buf, span] = exponent
                sums.append(jnp.sum(exponent.reshape(PTILE // 8, 8, resp), axis=0))
                weighed = exponent * grad_prob[buf, span]
                dots.append(jnp.sum(weighed.reshape(PTILE // 8, 8, resp), axis=0))
                if head + 1 < PER_KV:
                    tops.append(products(head + 1, tile))
            inverse = 1.0 / jnp.sum(functools.reduce(jnp.add, sums), axis=0, keepdims=True)
            row_delta = (
                jnp.sum(functools.reduce(jnp.add, dots), axis=0, keepdims=True) * inverse
            )
            inverse = inverse * live
            for tile in range(tiles):
                span = slice(tile * PTILE, (tile + 1) * PTILE)
                probabilities = scores[buf, span] * inverse
                weights[buf, span] = probabilities.astype(jnp.bfloat16)
                grad_scores[buf, span] = (
                    probabilities * (grad_prob[buf, span] - row_delta)
                ).astype(jnp.bfloat16)
            for target, left, right in (
                (dv, weights, do_all),
                (dk, grad_scores, q_all),
            ):
                product = jnp.dot(left[buf], right[head], preferred_element_type=jnp.float32)
                target[...] = product if head == 0 else target[...] + product
            grad_query_t = jnp.dot(
                keys_t[...], grad_scores[buf], preferred_element_type=jnp.float32
            )
            grad_query = (grad_query_t.T * SCALING).astype(jnp.bfloat16)
            q_from = given + (kv * PER_KV + head) * HEAD_DIM
            for i in range(tp_count):
                backs[i][:, q_from : q_from + HEAD_DIM] = grad_query[i * rows : (i + 1) * rows]

        own_grad[0, :, at] = (dk[:half] * SCALING).astype(jnp.bfloat16)
        other_grad[0, :, at] = (dk[half:prompt_len] * SCALING).astype(jnp.bfloat16)
        own_grad[1, :, at] = dv[:half].astype(jnp.bfloat16)
        other_grad[1, :, at] = dv[half:prompt_len].astype(jnp.bfloat16)
        for i in range(tp_count):
            k_from = given + q_cols + kv * HEAD_DIM
            v_from = k_from + k_cols
            span = slice(prompt_len + i * rows, prompt_len + (i + 1) * rows)
            backs[i][:, k_from : k_from + HEAD_DIM] = (dk[span] * SCALING).astype(jnp.bfloat16)
            backs[i][:, v_from : v_from + HEAD_DIM] = dv[span].astype(jnp.bfloat16)


def attend(chunk, meta, packs, earlier, own, other):
    tp_count, rows = len(packs), packs[0].shape[0]
    resp = rows * tp_count
    half, k_cols = other.shape[1:]
    kv_heads = k_cols // HEAD_DIM
    q_cols = kv_heads * PER_KV * HEAD_DIM
    total = 2 * half + resp
    f32, bf16 = jnp.float32, jnp.bfloat16
    flops = 10 * resp * total * kv_heads * PER_KV * HEAD_DIM
    results = pl.pallas_call(
        functools.partial(attend_kernel, chunk, tp_count),
        out_shape=[
            jax.ShapeDtypeStruct((rows, (chunk + 1) * (q_cols + 2 * k_cols)), bf16)
        ]
        * tp_count
        + [jax.ShapeDtypeStruct(other.shape, bf16)] * 2,
        in_specs=[scalars()] + [whole()] * (tp_count + len(earlier) + 2),
        out_specs=[whole()] * (tp_count + 2),
        scratch_shapes=[
            pltpu.VMEM((PER_KV, resp, HEAD_DIM), bf16),
            pltpu.VMEM((PER_KV, resp, HEAD_DIM), bf16),
            pltpu.VMEM((total, HEAD_DIM), bf16),
            pltpu.VMEM((total, HEAD_DIM), bf16),
            pltpu.VMEM((HEAD_DIM, total), bf16),
            pltpu.VMEM((resp, resp), f32),
            pltpu.VMEM((2, total, resp), f32),
            pltpu.VMEM((2, total, resp), f32),
            pltpu.VMEM((2, total, resp), bf16),
            pltpu.VMEM((2, total, resp), bf16),
            pltpu.VMEM((total, HEAD_DIM), f32),
            pltpu.VMEM((total, HEAD_DIM), f32),
        ],
        compiler_params=pltpu.CompilerParams(vmem_limit_bytes=ATTEND_VMEM),
        cost_estimate=pl.CostEstimate(
            flops=8 * flops, bytes_accessed=6 * 1024 * 1024, transcendentals=flops // 1280
        ),
        name="attend",
    )(meta, *packs, *earlier, own, other)
    return results[:tp_count], results[tp_count], results[tp_count + 1]


def shards(
    resp_queries, resp_keys, resp_values, resp_dout, prompt_kv, lengths, owners, visible_tiles
):
    tp_count = lax.axis_size("tp")
    tp = lax.axis_index("tp").astype(jnp.int32)[None]
    section = lax.axis_index("section").astype(jnp.int32)[None]
    at_row = lax.rem(lax.axis_index("group").astype(jnp.int32), ROW)
    rows = resp_queries.shape[0]
    half = prompt_kv.shape[2] // 2
    k_part = prompt_kv.shape[3] // CHUNKS
    pack_cols = 2 * (resp_queries.shape[1] + resp_keys.shape[1]) // tp_count
    bf16, f32 = jnp.bfloat16, jnp.float32
    part = jax.ShapeDtypeStruct((2, half, k_part), bf16)

    halves = small_call(
        halves_kernel,
        "halves",
        [part] * CHUNKS,
        [scalars(), whole()],
    )(section, prompt_kv)
    sibling_owner = shifted(after(owners, halves), "section", 1)
    meta = jnp.concatenate([tp, section, lengths, visible_tiles[0]])
    meta = after(meta, sibling_owner)
    packs = small_call(
        pack_kernel,
        "pack",
        [jax.ShapeDtypeStruct((rows, pack_cols), bf16)] * tp_count,
        [scalars()] + [whole()] * 4,
    )(meta, resp_queries, resp_dout, resp_keys, resp_values)
    arrived = {d: shifted(packs[d], "tp", d) for d in range(1, tp_count, 2)}
    for d in range(2, tp_count, 2):
        arrived[d] = shifted(after(packs[d], arrived), "tp", d)
    arrived = [packs[0]] + [arrived[d] for d in range(1, tp_count)]

    before = [to_row(block, 1) for block in halves]
    sends = [
        [jnp.where(at_row + offset >= ROW, before[c], halves[c]) for offset in range(1, WIN)]
        for c in range(CHUNKS)
    ]
    sends[0] = list(lax.optimization_barrier(after(sends[0], packs)))
    offers = []
    for c in range(CHUNKS):
        offer = {0: halves[c]}
        for offset in (2, 1, 3):
            send = sends[c][offset - 1]
            if c:
                send = after(send, offers[c - 1][offset])
            offer[offset] = along_row(send, offset)
        offers.append([offer[offset] for offset in range(WIN)])

    backs, shares, passing, ringed, terms = [], [], [], {}, []
    for c in range(CHUNKS):
        wanted, own = small_call(
            pick_kernel, "pick", [part] * 2, [scalars()] * 2 + [whole()] * WIN
        )(sibling_owner, owners, *offers[c])
        other = after(shifted(wanted, "section", 1), terms)
        backs, own_grad, other_grad = attend(c, meta, arrived, backs, own, other)
        if c == CHUNKS - 1:
            returned = {1: shifted(backs[1], "tp", -1)}
            for d in range(2, tp_count):
                first = after(backs[d], returned[1] if d > 2 else shares[1])
                returned[d] = shifted(first, "tp", -d)
        sibling_grad = after(shifted(other_grad, "section", 1), passing)
        terms = []
        for offset in range(WIN):
            term = jnp.where(owners[0] == offset, own_grad.astype(f32), 0.0) + jnp.where(
                sibling_owner[0] == offset, sibling_grad.astype(f32), 0.0
            )
            terms.append(term if offset == 0 else term.astype(bf16))
        terms = lax.optimization_barrier(terms)
        for offset in (2, 1, 3):
            term = after(terms[offset], ringed[offset]) if c else terms[offset]
            ringed[offset] = along_row(term, -offset)
        kept, passed = terms[0], jnp.zeros(part.shape, f32)
        for offset in range(1, WIN):
            term = ringed[offset].astype(f32)
            crossing = at_row + offset >= ROW
            kept = kept + jnp.where(crossing, 0.0, term)
            passed = passed + jnp.where(crossing, term, 0.0)
        passed = passed.astype(bf16)
        if c == CHUNKS - 1:
            passed = after(passed, (returned[1], returned[2]))
        passing.append(passed)
        shares += [kept, to_row(passed, -1)]

    prompt_grads = small_call(
        finish_kernel,
        "finish",
        jax.ShapeDtypeStruct((1, 2, half, prompt_kv.shape[3]), bf16),
        [whole()] * len(shares),
    )(*shares)
    grads = small_call(
        unpack_kernel,
        "unpack",
        [
            jax.ShapeDtypeStruct(resp_queries.shape, bf16),
            jax.ShapeDtypeStruct(resp_keys.shape, bf16),
            jax.ShapeDtypeStruct(resp_values.shape, bf16),
        ],
        [scalars()] + [whole()] * tp_count,
    )(after(tp, prompt_grads), backs[0], *[returned[d] for d in range(1, tp_count)])
    return (grads[0], grads[1], grads[2], prompt_grads)


def solution(mesh):
    placed = (
        P(("section", "group", "tp"), None),
        P(("section", "group", "tp"), None),
        P(("section", "group", "tp"), None),
        P(("section", "group", "tp"), None),
        P("group", None, None, "tp"),
        P(("section", "group")),
        P(("section", "group")),
        P(("section", "group"), None),
    )
    return jax.shard_map(
        shards,
        mesh=mesh,
        in_specs=placed,
        out_specs=(
            P(("section", "group", "tp"), None),
            P(("section", "group", "tp"), None),
            P(("section", "group", "tp"), None),
            P("group", None, "section", "tp"),
        ),
        check_vma=False,
    )
```
